32 devices in a mesh: dp: 8 (over z, x), tensor: 4 (over y, core).
Axes of the slice: x: 2, y: 2, z: 4, core: 2. Of those that a mesh axis runs over, the one named last changes fastest.
Arguments:
- hidden_input: bfloat16 [8192, 2048], P(('dp', 'tensor')), may hold values from -6 to 6
- output_gradient: bfloat16 [8192, 2048], P(('dp', 'tensor')), may hold values from -6 to 6
- lengths: int32 [8], replicated, may hold values from 193 to 2048, as said below
- attention_norm_gain: bfloat16 [2048], replicated, may hold values from 0.5 to 1.5
- query_weight: bfloat16 [2048, 2048], P(('dp', 'tensor')), may hold values from -0.125 to 0.125
- key_weight: bfloat16 [2048, 512], P(('dp', 'tensor')), may hold values from -0.125 to 0.125
- value_weight: bfloat16 [2048, 512], P(('dp', 'tensor')), may hold values from -0.125 to 0.125
- output_weight: bfloat16 [2048, 2048], P(('dp', 'tensor')), may hold values from -0.5 to 0.5
- query_adapter_first: bfloat16 [2048, 8], replicated, may hold values from -0.125 to 0.125
- query_adapter_second: bfloat16 [8, 2048], replicated, may hold values from -1 to 1
- key_adapter_first: bfloat16 [2048, 8], replicated, may hold values from -0.125 to 0.125
- key_adapter_second: bfloat16 [8, 512], replicated, may hold values from -1 to 1
- value_adapter_first: bfloat16 [2048, 8], replicated, may hold values from -0.125 to 0.125
- value_adapter_second: bfloat16 [8, 512], replicated, may hold values from -1 to 1
- output_adapter_first: bfloat16 [2048, 8], replicated, may hold values from -0.5 to 0.5
- output_adapter_second: bfloat16 [8, 2048], replicated, may hold values from -1 to 1
- query_feature_weight: bfloat16 [32, 64, 64], replicated, may hold values from -0.75 to 0.75
- key_feature_weight: bfloat16 [8, 64, 64], replicated, may hold values from -0.75 to 0.75
- feedforward_norm_gain: bfloat16 [2048], replicated, may hold values from 0.5 to 1.5
- gate_weight: bfloat16 [2048, 8192], P('dp', 'tensor'), may hold values from -0.125 to 0.125
- up_weight: bfloat16 [2048, 8192], P('dp', 'tensor'), may hold values from -0.125 to 0.125
- down_weight: bfloat16 [8192, 2048], P('tensor', 'dp'), may hold values from -0.0625 to 0.0625
Outputs:
- block_out: bfloat16 [8192, 2048], P(('dp', 'tensor'))
- in_grad: float32 [8192, 2048], P(('dp', 'tensor'))
- grad_norm_attn: float32 [2048], replicated
- grad_w_query: float32 [2048, 2048], P(('dp', 'tensor'))
- grad_w_key: float32 [2048, 512], P(('dp', 'tensor'))
- grad_w_value: float32 [2048, 512], P(('dp', 'tensor'))
- grad_w_out: float32 [2048, 2048], P(('dp', 'tensor'))
- grad_lora_qa: float32 [2048, 8], replicated
- grad_lora_qb: float32 [8, 2048], replicated
- grad_lora_ka: float32 [2048, 8], replicated
- grad_lora_kb: float32 [8, 512], replicated
- grad_lora_va: float32 [2048, 8], replicated
- grad_lora_vb: float32 [8, 512], replicated
- grad_lora_oa: float32 [2048, 8], replicated
- grad_lora_ob: float32 [8, 2048], replicated
- grad_map_query: float32 [32, 64, 64], replicated
- grad_map_key: float32 [8, 64, 64], replicated
- grad_norm_mlp: float32 [2048], replicated
- grad_w_gate: float32 [2048, 8192], P('dp', 'tensor')
- grad_w_up: float32 [2048, 8192], P('dp', 'tensor')
- grad_w_down: float32 [8192, 2048], P('tensor', 'dp')
The draws below stay inside these ranges and needn't reach their ends.
Inputs may be any that keep to these rules, and one draw needn't show every extreme that they name: `lengths`: each sequence fills ceil(length / 64) blocks of 64 rows, laid end to end in order, and all sequences together fill the 8192 rows; the longest is exactly 2048.
All inputs are finite; a program needn't handle non-finite values.
Results may differ from the reference program's by a relative error of at most 0.019.
Values may be sent and summed in bfloat16 or wider, within the bound.
A program may use at most 320 MiB of HBM per device.

```python
import math
import jax
import jax.numpy as jnp
from jax import lax

MODEL_WIDTH = 2048
QUERY_HEADS = 32
KEY_VALUE_HEADS = 8
HEAD_SIZE = 64
FF = 8192
ADAPTER_RANK = 8
WINDOW_ROWS = 64
TOK_DEV = 256
TOKENS = 8192
NSEQ = 8
MOST_LEN = 2048
QUERY_FEATURES = 2048
KEY_FEATURES = 512


def fill_side(key, count, total, most_spans, has_long):
    place_key, weight_key, order_key = jax.random.split(key, 3)
    indices = jnp.arange(count, dtype=jnp.int32)
    position = jax.random.randint(place_key, (), 0, count)
    long_here = jnp.logical_and(has_long, indices == position)
    base = jnp.where(long_here, most_spans, 4).astype(jnp.int32)
    spare = total - jnp.sum(base)
    ceiling = jnp.where(long_here, 0, most_spans - 4).astype(jnp.int32)
    raw_weight = jax.random.randint(weight_key, (count,), 0, 8)
    weights = jnp.where(long_here, 0, 1 + raw_weight * raw_weight).astype(jnp.int32)
    extra = jnp.minimum(ceiling, spare * weights // jnp.maximum(jnp.sum(weights), 1)).astype(jnp.int32)
    ranking = jax.random.permutation(order_key, count).astype(jnp.int32)

    def add_span(counter, current):
        open_slot = current < ceiling
        chosen = jnp.argmin(jnp.where(open_slot, ranking, count + 1))
        return current.at[chosen].add(1)
    extra = lax.fori_loop(0, spare - jnp.sum(extra), add_span, extra)
    return (base + extra, long_here)


def draw_lengths(key, part):
    key = jax.random.fold_in(key, 7)
    side_key, left_key, right_key, pad_key = jax.random.split(key, 4)
    device_blocks = TOK_DEV // WINDOW_ROWS
    all_spans = TOKENS // WINDOW_ROWS
    device_count = TOKENS // TOK_DEV
    most_spans = MOST_LEN // WINDOW_ROWS
    left_total = device_count // 2 * device_blocks - 1
    bridge = device_blocks + 2
    right_total = all_spans - left_total - bridge
    left_count = (NSEQ - 1) // 2
    right_count = NSEQ - 1 - left_count
    long_left = jax.random.randint(side_key, (), 0, 2) == 0
    left_spans, left_long = fill_side(left_key, left_count, left_total, most_spans, long_left)
    right_spans, right_long = fill_side(right_key, right_count, right_total, most_spans, jnp.logical_not(long_left))
    spans = jnp.concatenate([left_spans, jnp.full((1,), bridge, jnp.int32), right_spans])
    unpadded = jnp.concatenate([left_long, jnp.ones((1,), bool), right_long])
    padding = jnp.where(unpadded, 0, jax.random.randint(pad_key, (NSEQ,), 0, WINDOW_ROWS))
    return (spans * WINDOW_ROWS - padding).astype(jnp.int32)


def level_of(key, dims, shards, low, high):
    def one(dim, shards_of):
        draws = jax.random.uniform(jax.random.fold_in(jax.random.fold_in(key, 6), dim), (shards_of,), jnp.float32, low / len(shards), high / len(shards))
        return jnp.repeat(jnp.exp(draws), dims[dim] // shards_of).reshape((-1,) + (1,) * (len(dims) - dim - 1))

    loudness = one(*shards[0])
    for cut in shards[1:]:
        loudness = loudness * one(*cut)
    return loudness


def bell_draw(rng, shape, spread, reach, pieces=(), held_as=jnp.bfloat16):
    entries = jax.random.normal(rng, shape, jnp.float32) * spread
    if len(pieces) > 0:
        entries = level_of(rng, shape, pieces, -0.22, 0.18) * entries
    return jnp.clip(entries, min=-reach, max=reach).astype(held_as)


def setup_inputs(seed: int = 0) -> dict:
    keys = jax.random.split(jax.random.key(seed), 23)
    hidden_input = bell_draw(keys[0], (TOKENS, MODEL_WIDTH), 1.0, 6.0, ((0, 32),))
    output_gradient = bell_draw(keys[1], (TOKENS, MODEL_WIDTH), 1.0, 6.0, ((0, 32),))
    lengths = draw_lengths(jax.random.fold_in(keys[22], 71), 0)
    attention_norm_gain = jnp.clip(1.0 + 0.1 * jax.random.normal(keys[3], (MODEL_WIDTH,), jnp.float32), 0.5, 1.5).astype(jnp.bfloat16)
    query_weight = bell_draw(keys[4], (MODEL_WIDTH, QUERY_FEATURES), MODEL_WIDTH ** -0.5, 0.125, ((0, 32),))
    key_weight = bell_draw(keys[5], (MODEL_WIDTH, KEY_FEATURES), MODEL_WIDTH ** -0.5, 0.125, ((0, 32),))
    value_weight = bell_draw(keys[6], (MODEL_WIDTH, KEY_FEATURES), MODEL_WIDTH ** -0.5, 0.125, ((0, 32),))
    output_weight = bell_draw(keys[7], (QUERY_FEATURES, MODEL_WIDTH), (QUERY_FEATURES // 16) ** -0.5, 0.5, ((0, 32),))
    query_adapter_first = bell_draw(keys[8], (MODEL_WIDTH, ADAPTER_RANK), MODEL_WIDTH ** -0.5, 0.125)
    query_adapter_second = bell_draw(keys[9], (ADAPTER_RANK, QUERY_FEATURES), (4 * ADAPTER_RANK) ** -0.5, 1.0)
    key_adapter_first = bell_draw(keys[10], (MODEL_WIDTH, ADAPTER_RANK), MODEL_WIDTH ** -0.5, 0.125)
    key_adapter_second = bell_draw(keys[11], (ADAPTER_RANK, KEY_FEATURES), (4 * ADAPTER_RANK) ** -0.5, 1.0)
    value_adapter_first = bell_draw(keys[12], (MODEL_WIDTH, ADAPTER_RANK), MODEL_WIDTH ** -0.5, 0.125)
    value_adapter_second = bell_draw(keys[13], (ADAPTER_RANK, KEY_FEATURES), (4 * ADAPTER_RANK) ** -0.5, 1.0)
    output_adapter_first = bell_draw(keys[14], (QUERY_FEATURES, ADAPTER_RANK), (QUERY_FEATURES // 16) ** -0.5, 0.5)
    output_adapter_second = bell_draw(keys[15], (ADAPTER_RANK, MODEL_WIDTH), (4 * ADAPTER_RANK) ** -0.5, 1.0)
    query_feature_weight = bell_draw(keys[16], (QUERY_HEADS, HEAD_SIZE, HEAD_SIZE), HEAD_SIZE ** -0.5, 0.75)
    key_feature_weight = bell_draw(keys[17], (KEY_VALUE_HEADS, HEAD_SIZE, HEAD_SIZE), HEAD_SIZE ** -0.5, 0.75)
    feedforward_norm_gain = jnp.clip(1.0 + 0.1 * jax.random.normal(keys[18], (MODEL_WIDTH,), jnp.float32), 0.5, 1.5).astype(jnp.bfloat16)
    gate_weight = bell_draw(keys[19], (MODEL_WIDTH, FF), MODEL_WIDTH ** -0.5, 0.125, ((0, 8), (1, 4)))
    up_weight = bell_draw(keys[20], (MODEL_WIDTH, FF), MODEL_WIDTH ** -0.5, 0.125, ((0, 8), (1, 4)))
    down_weight = bell_draw(keys[21], (FF, MODEL_WIDTH), FF ** -0.5, 0.0625, ((0, 4), (1, 8)))
    return {"hidden_input": hidden_input, "output_gradient": output_gradient, "lengths": lengths, "attention_norm_gain": attention_norm_gain, "query_weight": query_weight, "key_weight": key_weight, "value_weight": value_weight, "output_weight": output_weight, "query_adapter_first": query_adapter_first, "query_adapter_second": query_adapter_second, "key_adapter_first": key_adapter_first, "key_adapter_second": key_adapter_second, "value_adapter_first": value_adapter_first, "value_adapter_second": value_adapter_second, "output_adapter_first": output_adapter_first, "output_adapter_second": output_adapter_second, "query_feature_weight": query_feature_weight, "key_feature_weight": key_feature_weight, "feedforward_norm_gain": feedforward_norm_gain, "gate_weight": gate_weight, "up_weight": up_weight, "down_weight": down_weight}


EPSILON = 1e-05
FLOOR_SCORE = -1e+30
HIGHEST = lax.Precision.HIGHEST

@jax.custom_vjp
def low(v):
    return lax.optimization_barrier(v.astype(jnp.bfloat16)).astype(jnp.float32)

@jax.custom_vjp
def low_back(v):
    return v

def low_keep(v):
    return (low(v), None)

def low_pass(kept, grad):
    return (grad,)

def back_keep(v):
    return (v, None)

def back_low(kept, grad):
    return (low(grad),)
low.defvjp(low_keep, low_pass)
low_back.defvjp(back_keep, back_low)

def rounded_pair(value_vectors):
    return low_back(low(value_vectors))

def matrix_product(left, right):
    return jnp.dot(left, right, precision=HIGHEST)

def rms_norm(value_vectors, gain):
    return value_vectors * lax.rsqrt(lax.optimization_barrier(jnp.mean(value_vectors * value_vectors, -1, keepdims=True)) + EPSILON) * gain

def feature_map(logits):
    return jnp.concatenate([jax.nn.softmax(logits, -1), jax.nn.softmax(-logits, -1)], -1)

def layout(lengths):
    seq_spans = ((lengths + WINDOW_ROWS - 1) // WINDOW_ROWS).astype(jnp.int32)
    seq_ends = jnp.cumsum(seq_spans).astype(jnp.int32)
    seq_begins = seq_ends - seq_spans
    token_ids = jnp.arange(TOKENS, dtype=jnp.int32)
    token_seq = lax.optimization_barrier(jnp.sum((token_ids[:, None] >= (seq_ends * WINDOW_ROWS)[None, :]).astype(jnp.int32), 1)).astype(jnp.int32)
    onehot = (token_seq[:, None] == jnp.arange(NSEQ, dtype=jnp.int32)[None, :]).astype(jnp.int32)
    offset = lax.optimization_barrier(jnp.sum(onehot * (seq_begins * WINDOW_ROWS)[None, :], 1)).astype(jnp.int32)
    limit = lax.optimization_barrier(jnp.sum(onehot * lengths[None, :], 1)).astype(jnp.int32)
    valid_mask = (token_ids - offset < limit).astype(jnp.float32)[:, None]
    span_ids = jnp.arange(TOKENS // WINDOW_ROWS, dtype=jnp.int32)
    sequence_begins = jnp.any(span_ids[:, None] == seq_begins[None, :], 1).astype(jnp.float32)
    return (valid_mask, sequence_begins)

def span_step(query_feature_four, key_feature_weight, carry, inputs):
    state, norm_state = carry
    query_rows, key_rows, value_rows, begin = inputs
    keep = 1.0 - begin
    state = state * keep
    norm_state = norm_state * keep
    q_logits = low_back(jnp.einsum('tkgd,kgde->tkge', query_rows, query_feature_four, precision=HIGHEST))
    q_feat = low(feature_map(q_logits))
    k_logits = low_back(jnp.einsum('tkd,kde->tke', key_rows, key_feature_weight, precision=HIGHEST))
    k_feat = low(feature_map(k_logits))
    scores = low_back(jnp.einsum('tkgd,skd->kgts', query_rows, key_rows, precision=HIGHEST) * (1.0 / math.sqrt(HEAD_SIZE)))
    causal = jnp.arange(WINDOW_ROWS)[:, None] >= jnp.arange(WINDOW_ROWS)[None, :]
    masked = jnp.where(causal, scores, FLOOR_SCORE)
    top = lax.optimization_barrier(jnp.max(masked, -1, keepdims=True))
    expo = jnp.where(causal, jnp.exp(masked - top), 0.0)
    probs = low(expo)
    win_num = jnp.einsum('kgts,skd->tkgd', probs, value_rows, precision=HIGHEST)
    win_den = jnp.transpose(lax.optimization_barrier(jnp.sum(expo, -1)), (2, 0, 1))
    shrink = jnp.transpose(jnp.exp(-top[..., 0]), (2, 0, 1))
    lin_num = jnp.einsum('tkgf,kfd->tkgd', q_feat, state, precision=HIGHEST)
    lin_den = jnp.einsum('tkgf,kf->tkg', q_feat, norm_state, precision=HIGHEST)
    numer = low_back(win_num + shrink[..., None] * lin_num)
    denom = win_den + shrink * lin_den
    attended_rows = low(numer / denom[..., None])
    state = state + jnp.einsum('skf,skd->kfd', k_feat, value_rows, precision=HIGHEST)
    norm_state = norm_state + lax.optimization_barrier(jnp.sum(k_feat, 0))
    return ((state, norm_state), attended_rows)

def mlp_block(feedforward_norm_gain, gate_weight, up_weight, down_weight, rows):
    normed = low(rms_norm(rows, feedforward_norm_gain))
    gate = low_back(matrix_product(normed, gate_weight))
    upper = low_back(matrix_product(normed, up_weight))
    hidden = low(jax.nn.silu(gate) * upper)
    return low_back(matrix_product(hidden, down_weight))

def forward_pass(valid_mask, sequence_begins, hidden_input, attention_norm_gain, query_weight, key_weight, value_weight, output_weight, query_adapter_first, query_adapter_second, key_adapter_first, key_adapter_second, value_adapter_first, value_adapter_second, output_adapter_first, output_adapter_second, query_feature_weight, key_feature_weight, feedforward_norm_gain, gate_weight, up_weight, down_weight):
    query_group_width = QUERY_HEADS // KEY_VALUE_HEADS
    window_count = TOKENS // WINDOW_ROWS
    normed = low(rms_norm(hidden_input, attention_norm_gain))

    def project_rows(weight, first, second):
        low_rank = rounded_pair(matrix_product(normed, first))
        return rounded_pair(matrix_product(normed, weight) + matrix_product(low_rank, second))
    query_vectors = project_rows(query_weight, query_adapter_first, query_adapter_second).reshape(window_count, WINDOW_ROWS, KEY_VALUE_HEADS, query_group_width, HEAD_SIZE)
    key_vectors = project_rows(key_weight, key_adapter_first, key_adapter_second).reshape(window_count, WINDOW_ROWS, KEY_VALUE_HEADS, HEAD_SIZE)
    value_vectors = project_rows(value_weight, value_adapter_first, value_adapter_second).reshape(window_count, WINDOW_ROWS, KEY_VALUE_HEADS, HEAD_SIZE)
    query_feature_four = query_feature_weight.reshape(KEY_VALUE_HEADS, query_group_width, HEAD_SIZE, HEAD_SIZE)
    stepper = jax.checkpoint(span_step)
    start_index = (jnp.zeros((KEY_VALUE_HEADS, 2 * HEAD_SIZE, HEAD_SIZE), jnp.float32), jnp.zeros((KEY_VALUE_HEADS, 2 * HEAD_SIZE), jnp.float32))
    ignored, attended_rows = lax.scan(lambda carry, inputs: stepper(query_feature_four, key_feature_weight, carry, inputs), start_index, (query_vectors, key_vectors, value_vectors, sequence_begins))
    attended_rows = attended_rows.reshape(TOKENS, QUERY_HEADS * HEAD_SIZE)
    adapter_output = rounded_pair(matrix_product(attended_rows, output_adapter_first))
    branch_output = low_back(matrix_product(attended_rows, output_weight) + matrix_product(adapter_output, output_adapter_second))
    resid = hidden_input + branch_output
    block_rows = 2048
    mlp_fn = jax.checkpoint(mlp_block)
    mlp_out = lax.map(lambda rows: mlp_fn(feedforward_norm_gain, gate_weight, up_weight, down_weight, rows), resid.reshape(TOKENS // block_rows, block_rows, MODEL_WIDTH)).reshape(TOKENS, MODEL_WIDTH)
    return valid_mask * (resid + mlp_out)

def reference(hidden_input, output_gradient, lengths, attention_norm_gain, query_weight, key_weight, value_weight, output_weight, query_adapter_first, query_adapter_second, key_adapter_first, key_adapter_second, value_adapter_first, value_adapter_second, output_adapter_first, output_adapter_second, query_feature_weight, key_feature_weight, feedforward_norm_gain, gate_weight, up_weight, down_weight):
    valid_mask, sequence_begins = layout(lengths)
    parameter_set = tuple((item_value.astype(jnp.float32) for item_value in (hidden_input, attention_norm_gain, query_weight, key_weight, value_weight, output_weight, query_adapter_first, query_adapter_second, key_adapter_first, key_adapter_second, value_adapter_first, value_adapter_second, output_adapter_first, output_adapter_second, query_feature_weight, key_feature_weight, feedforward_norm_gain, gate_weight, up_weight, down_weight)))
    output, pullback = jax.vjp(lambda *items: forward_pass(valid_mask, sequence_begins, *items), *parameter_set)
    grads = pullback(output_gradient.astype(jnp.float32))
    return (output.astype(jnp.bfloat16), grads[0], grads[1], grads[2], grads[3], grads[4], grads[5], grads[6], grads[7], grads[8], grads[9], grads[10], grads[11], grads[12], grads[13], grads[14], grads[15], grads[16], grads[17], grads[18], grads[19])
```

```python
import math

import jax
import jax.numpy as jnp
from jax import lax
from jax.experimental import pallas as pl
from jax.experimental.pallas import tpu as pltpu
from jax.sharding import PartitionSpec as P

HEAD = 64
WINDOW = 64
EPSILON = 1e-05
FLOOR_SCORE = -1e30
HIGHEST = lax.Precision.HIGHEST
F32 = jnp.float32
BF16 = jnp.bfloat16
CHUNKS = 2


def dot(a, b, out=F32):
    return jnp.dot(a, b, preferred_element_type=F32).astype(out)


def dot_nt(a, b, out=F32):
    return lax.dot_general(a, b, (((1,), (1,)), ((), ())), preferred_element_type=F32).astype(out)


def dot_tn(a, b, out=F32):
    return lax.dot_general(a, b, (((0,), (0,)), ((), ())), preferred_element_type=F32).astype(out)


def rms_forward(v, gain):
    inv_root = lax.rsqrt(jnp.mean(v * v, -1, keepdims=True) + EPSILON)
    normed = v * inv_root
    return normed, inv_root, (normed * gain).astype(BF16)


def rms_backward(grad_out, normed, inv_root, gain):
    scaled = grad_out * gain
    return inv_root * (scaled - normed * jnp.mean(scaled * normed, -1, keepdims=True))


def feature_map(logits):
    return jnp.concatenate([jax.nn.softmax(logits, -1), jax.nn.softmax(-logits, -1)], -1)


def feature_back(grad_feat, logits):
    half = logits.shape[-1]
    plus = jax.nn.softmax(logits, -1)
    minus = jax.nn.softmax(-logits, -1)
    grad_plus = grad_feat[..., :half]
    grad_minus = grad_feat[..., half:]
    result = plus * (grad_plus - jnp.sum(plus * grad_plus, -1, keepdims=True))
    result = result - minus * (grad_minus - jnp.sum(minus * grad_minus, -1, keepdims=True))
    return result.astype(BF16)


MESH = pl.DeviceIdType.MESH


class Post:
    def __init__(self, sends, recvs):
        self.sends, self.recvs, self.copies = sends, recvs, []
        self.received = set()

    def send(self, src, dst, device):
        i = len(self.copies)
        copy = pltpu.make_async_remote_copy(
            src_ref=src,
            dst_ref=dst,
            send_sem=self.sends.at[i],
            recv_sem=self.recvs.at[i],
            device_id=device,
            device_id_type=MESH,
        )
        copy.start()
        self.copies.append(copy)
        return i

    def arrived(self, i):
        if i not in self.received:
            self.received.add(i)
            self.copies[i].wait_recv()

    def finish(self):
        for i in range(len(self.copies)):
            self.arrived(i)
        for copy in self.copies:
            copy.wait_send()


class Links:
    def __init__(self, mesh):
        self.dp = mesh.shape["dp"]
        self.tensor = mesh.shape["tensor"]
        self.outer = self.dp // 2
        self.layer = 2 * self.tensor
        self.calls = 0

    def coords(self):
        dp = lax.axis_index("dp")
        tensor = lax.axis_index("tensor")
        self.place = dp // 2
        self.side = dp % 2
        self.rank = self.side * self.tensor + tensor


    def flip(self, offset):
        dp = lax.axis_index("dp")
        tensor = lax.axis_index("tensor")
        if offset & 4:
            dp = dp + 1 - 2 * (dp % 2)
        if offset & 2:
            tensor = tensor + 2 - 4 * ((tensor // 2) % 2)
        if offset & 1:
            tensor = tensor + 1 - 2 * (tensor % 2)
        return {"dp": dp, "tensor": tensor}, (dp % 2) * self.tensor + tensor

    def meet(self, devices):
        barrier = pltpu.get_barrier_semaphore()
        for device in devices:
            pl.semaphore_signal(barrier, inc=1, device_id=device, device_id_type=MESH)
        pl.semaphore_wait(barrier, len(devices))

    def call(self, kernel, outs, args, copies, scratch=(), local=0, vmem=48):
        self.calls += 1
        sems = [pltpu.SemaphoreType.DMA((copies,)), pltpu.SemaphoreType.DMA((copies,))]
        sems += [pltpu.SemaphoreType.DMA((max(local, 1),))]
        return pl.pallas_call(
            kernel,
            out_shape=[jax.ShapeDtypeStruct(s, t) for s, t, _ in outs],
            in_specs=[pl.BlockSpec(memory_space=pl.ANY)] * len(args),
            out_specs=[pl.BlockSpec(memory_space=space) for _, _, space in outs],
            scratch_shapes=sems + list(scratch),
            compiler_params=pltpu.CompilerParams(
                collective_id=self.calls, has_side_effects=True, vmem_limit_bytes=vmem * 2**20
            ),
        )(*args)

    def gather_steps(self, post, v, out, local):
        half = v.shape[0] // 2
        a, b = pl.ds(0, half), pl.ds(half, half)
        rank = self.flip(0)[1]
        (dev_c, rank_c), (dev_y, rank_y), (dev_x, rank_x) = (self.flip(i) for i in (1, 2, 4))
        rank_xy = self.flip(6)[1]
        own = pltpu.make_async_copy(v, out.at[rank], local)
        own.start()
        x1 = post.send(v.at[a], out.at[rank, a], dev_x)
        y1 = post.send(v.at[b], out.at[rank, b], dev_y)
        x2 = post.send(v.at[b], out.at[rank, b], dev_x)
        y2 = post.send(v.at[a], out.at[rank, a], dev_y)
        post.send(v, out.at[rank], dev_c)
        post.arrived(x1)
        y3 = post.send(out.at[rank_x, a], out.at[rank_x, a], dev_y)
        post.send(out.at[rank_x, a], out.at[rank_x, a], dev_c)
        post.arrived(y1)
        x3 = post.send(out.at[rank_y, b], out.at[rank_y, b], dev_x)
        post.send(out.at[rank_y, b], out.at[rank_y, b], dev_c)
        yield
        post.arrived(x2)
        post.send(out.at[rank_x, b], out.at[rank_x, b], dev_c)
        post.arrived(y2)
        post.send(out.at[rank_y, a], out.at[rank_y, a], dev_c)
        yield
        post.arrived(y3)
        post.send(out.at[rank_xy, a], out.at[rank_xy, a], dev_c)
        post.arrived(x3)
        post.send(out.at[rank_xy, b], out.at[rank_xy, b], dev_c)
        own.wait()

    def gather_rows(self, *arrays):
        many = len(arrays)

        def kernel(*refs):
            ins, outs = refs[:many], refs[many : 2 * many]
            sends, recvs, local = refs[2 * many :]
            post = Post(sends, recvs)
            self.meet([self.flip(i)[0] for i in (1, 2, 4)])
            steps = [
                self.gather_steps(post, v, out, local.at[i])
                for i, (v, out) in enumerate(zip(ins, outs))
            ]
            for step in steps:
                for _ in step:
                    pass
            post.finish()

        outs = [((self.layer,) + v.shape, v.dtype, pl.ANY) for v in arrays]
        return self.call(kernel, outs, arrays, 13 * many, local=many)

    def start_rows(self, v, halves):
        chunks = halves.shape[1]

        def kernel(v, halves, out, block, sends, recvs, local):
            post = Post(sends, recvs)
            self.meet([self.flip(i)[0] for i in (1, 2, 4)])
            side = lax.axis_index("dp") % 2
            dev_x = self.flip(4)[0]
            own = []
            for c in range(chunks):
                own.append(
                    pltpu.make_async_copy(halves.at[side, c], block.at[c, side], local.at[1 + c])
                )
                own[-1].start()
            post.send(halves.at[1 - side, 0], block.at[0, side], dev_x)
            steps = self.gather_steps(post, v, out, local.at[0])
            for _ in steps:
                pass
            for c in range(1, chunks):
                post.send(halves.at[1 - side, c], block.at[c, side], dev_x)
            post.finish()
            for copy in own:
                copy.wait()

        outs = [
            ((self.layer,) + v.shape, v.dtype, pl.ANY),
            ((chunks, 2) + halves.shape[2:], halves.dtype, pl.ANY),
        ]
        return self.call(kernel, outs, (v, halves), 13 + chunks, local=1 + chunks)

    def scatter_rows(self, parts):
        _, rows, width = parts.shape
        half = rows // 2
        step = 16

        def kernel(parts, out, sends, recvs, local, mine, got, xs, ys):
            post = Post(sends, recvs)
            devs = [self.flip(i) for i in range(8)]
            dev_c, dev_y, dev_x = devs[1][0], devs[2][0], devs[4][0]
            self.meet([dev_c, dev_y, dev_x])
            order = [(3, 0), (3, 1), (2, 0), (1, 1), (1, 0), (2, 1), (0, 0), (0, 1)]
            arrive = {}
            for n, (i, h) in enumerate(order):
                cut = pl.ds(h * half, half)
                own = pltpu.make_async_copy(
                    parts.at[devs[2 * i][1], cut], mine.at[i, h], local.at[n]
                )
                own.start()
                far = post.send(parts.at[devs[2 * i + 1][1], cut], got.at[i, h], dev_c)
                arrive[i, h] = (own, far)

            def add(dst, one, two):
                @pl.loop(0, half // step)
                def _(j):
                    at = pl.ds(pl.multiple_of(j * step, step), step)
                    total = one[at, :].astype(F32) + two[at, :].astype(F32)
                    dst[at, :] = total.astype(dst.dtype)

            def pair(i, h):
                own, far = arrive[i, h]
                own.wait()
                post.arrived(far)
                add(mine.at[i, h], mine.at[i, h], got.at[i, h])

            pair(3, 0)
            x1 = post.send(mine.at[3, 0], xs.at[0], dev_x)
            pair(3, 1)
            y1 = post.send(mine.at[3, 1], ys.at[0], dev_y)
            pair(2, 0)
            x2 = post.send(mine.at[2, 0], xs.at[1], dev_x)
            pair(1, 1)
            y2 = post.send(mine.at[1, 1], ys.at[1], dev_y)
            pair(1, 0)
            pair(2, 1)
            pair(0, 0)
            pair(0, 1)
            post.arrived(x1)
            add(mine.at[1, 0], mine.at[1, 0], xs.at[0])
            y3 = post.send(mine.at[1, 0], ys.at[2], dev_y)
            post.arrived(y1)
            add(mine.at[2, 1], mine.at[2, 1], ys.at[0])
            x3 = post.send(mine.at[2, 1], xs.at[2], dev_x)
            low, high = out.at[pl.ds(0, half)], out.at[pl.ds(half, half)]
            post.arrived(x2)
            add(low, mine.at[0, 0], xs.at[1])
            post.arrived(y2)
            add(high, mine.at[0, 1], ys.at[1])
            post.arrived(y3)
            add(low, low, ys.at[2])
            post.arrived(x3)
            add(high, high, xs.at[2])
            post.finish()

        outs = [((rows, width), F32, pltpu.VMEM)]
        scratch = [
            pltpu.VMEM((4, 2, half, width), BF16),
            pltpu.VMEM((4, 2, half, width), BF16),
            pltpu.VMEM((3, half, width), BF16),
            pltpu.VMEM((3, half, width), BF16),
        ]
        return self.call(kernel, outs, (parts,), 14, scratch, local=8)[0]

    def exchange(self, *arrays):
        many, layer = len(arrays), self.layer

        def kernel(*refs):
            ins, outs = refs[:many], refs[many : 2 * many]
            sends, recvs, local = refs[2 * many :]
            post = Post(sends, recvs)
            self.meet([self.flip(r)[0] for r in range(1, layer)])
            rank = self.flip(0)[1]
            own = []
            for i, (v, out) in enumerate(zip(ins, outs)):
                for r in (6, 7, 4, 5, 2, 3, 1):
                    device, target = self.flip(r)
                    post.send(v.at[target], out.at[rank], device)
                own.append(pltpu.make_async_copy(v.at[rank], out.at[rank], local.at[i]))
                own[-1].start()
            post.finish()
            for copy in own:
                copy.wait()

        outs = [(v.shape, v.dtype, pl.ANY) for v in arrays]
        return self.call(kernel, outs, arrays, 7 * many, local=many)

    def between(self, v):
        n = self.outer

        def kernel(v, out, sends, recvs, local):
            del local
            post = Post(sends, recvs)
            dp = lax.axis_index("dp")
            devices = [{"dp": (dp + 2 * d) % self.dp} for d in range(1, n)]
            self.meet(devices)
            for d, device in enumerate(devices):
                post.send(v, out.at[d], device)
            post.finish()

        return self.call(kernel, [((n - 1,) + v.shape, v.dtype, pl.ANY)], (v,), n - 1)[0]

    def sum_small(self, whole, part):
        stages = 0
        while 1 << stages < self.outer:
            stages += 1

        def kernel(whole, part, out_w, out_p, sends, recvs, local, got_w, got_p):
            dp = lax.axis_index("dp")
            post = Post(sends, recvs)
            layers = []
            for s in range(stages):
                step = 2 << s
                layers.append({"dp": dp + step - 2 * step * ((dp // step) % 2)})
            near = [self.flip(i)[0] for i in (1, 2, 4)]
            self.meet(near + layers)
            copies = [
                pltpu.make_async_copy(whole, out_w, local.at[0]),
                pltpu.make_async_copy(part, out_p, local.at[1]),
            ]
            for copy in copies:
                copy.start()
            for copy in copies:
                copy.wait()
            for n, device in enumerate(near + layers):
                moves = [(out_w, got_w)]
                if n >= len(near):
                    moves.append((out_p, got_p))
                ids = [post.send(v, got.at[n], device) for v, got in moves]
                for i, (v, got) in zip(ids, moves):
                    post.arrived(i)
                    post.copies[i].wait_send()
                    v[...] = v[...] + got[n]
            post.copies = []

        n = 3 + stages
        return self.call(
            kernel,
            [(whole.shape, F32, pltpu.VMEM), (part.shape, F32, pltpu.VMEM)],
            (whole, part),
            3 + 2 * stages,
            [pltpu.VMEM((n,) + whole.shape, F32), pltpu.VMEM((n,) + part.shape, F32)],
            local=2,
        )


    def groups(self):
        return [[2 * o + b for o in range(self.outer)] for b in range(2)]

    def gather_outer(self, v):
        return lax.all_gather(v, "dp", axis_index_groups=self.groups(), tiled=True)

    def scatter_outer(self, v):
        return lax.psum_scatter(v, "dp", axis_index_groups=self.groups(), tiled=True)

    def other_side(self, v):
        return lax.ppermute(v, "dp", [(i, i ^ 1) for i in range(self.dp)])


def attention_forward(q, k, v, map_q, map_k, same, before, last_mask, carry):
    windows = k.shape[0]
    scale = 1.0 / math.sqrt(HEAD)
    q_logits = jnp.einsum("ntgd,gde->ntge", q, map_q, preferred_element_type=F32)
    q_feat = feature_map(q_logits).astype(BF16)
    k_logits = jnp.einsum("nsd,de->nse", k, map_k, preferred_element_type=F32)
    k_feat = feature_map(k_logits).astype(BF16)
    scores = jnp.einsum("ntgd,nsd->ngts", q, k, preferred_element_type=F32) * scale
    causal = jnp.arange(WINDOW)[:, None] >= jnp.arange(WINDOW)[None, :]
    masked = jnp.where(causal, scores, FLOOR_SCORE)
    top = jnp.max(masked, -1, keepdims=True)
    expo = jnp.where(causal, jnp.exp(masked - top), 0.0)
    probs = expo.astype(BF16)
    win_num = jnp.einsum("ngts,nsd->ntgd", probs, v, preferred_element_type=F32)
    win_den = jnp.transpose(jnp.sum(expo, -1), (0, 2, 1))
    shrink = jnp.transpose(jnp.exp(-top[..., 0]), (0, 2, 1))
    v_one = jnp.concatenate([v, jnp.ones((windows, WINDOW, 1), BF16)], -1)
    updates = jnp.einsum("nsf,nsd->nfd", k_feat, v_one, preferred_element_type=F32)
    summary = jnp.einsum("c,cfd->fd", last_mask, updates, precision=HIGHEST)
    states = jnp.einsum("ab,bfd->afd", before, updates, precision=HIGHEST)
    states = states + same[:, None, None] * carry(summary)[None]
    linear = jnp.einsum("ntgf,nfd->ntgd", q_feat.astype(F32), states, precision=HIGHEST)
    numer = win_num + shrink[..., None] * linear[..., :HEAD]
    denom = win_den + shrink * linear[..., HEAD]
    ratio = numer / denom[..., None]
    return ratio, (q_logits, q_feat, k_logits, k_feat, expo, probs, shrink, states, denom, ratio)


def attention_backward(kept, grad, q, k, v, map_q, map_k, first_mask, after, before, carry):
    q_logits, q_feat, k_logits, k_feat, expo, probs, shrink, states, denom, ratio = kept
    windows = k.shape[0]
    scale = 1.0 / math.sqrt(HEAD)
    causal = jnp.arange(WINDOW)[:, None] >= jnp.arange(WINDOW)[None, :]
    q_feat_full = q_feat.astype(F32)
    k_feat_full = k_feat.astype(F32)
    grad_num = (grad / denom[..., None]).astype(BF16)
    grad_den = -jnp.sum(grad * ratio, -1) / denom
    grad_probs = jnp.einsum("ntgd,nsd->ngts", grad_num, v, preferred_element_type=F32)
    grad_expo = grad_probs + jnp.transpose(grad_den, (0, 2, 1))[..., None]
    grad_scores = jnp.where(causal, expo * grad_expo, 0.0).astype(BF16)
    dq = jnp.einsum("ngts,nsd->ntgd", grad_scores, k, preferred_element_type=F32) * scale
    dk = jnp.einsum("ngts,ntgd->nsd", grad_scores, q, preferred_element_type=F32) * scale
    dv = jnp.einsum("ngts,ntgd->nsd", probs, grad_num, preferred_element_type=F32)
    both = jnp.concatenate([grad_num.astype(F32), grad_den[..., None]], -1)
    grad_states = jnp.einsum(
        "ntgf,ntgd->nfd", q_feat_full, both * shrink[..., None], precision=HIGHEST
    )
    grad_q_feat = shrink[..., None] * jnp.einsum(
        "ntgd,nfd->ntgf", both, states, precision=HIGHEST
    )
    summary = jnp.einsum("c,cfd->fd", first_mask, grad_states, precision=HIGHEST)
    grad_updates = jnp.einsum("ab,afd->bfd", before, grad_states, precision=HIGHEST)
    grad_updates = grad_updates + after[:, None, None] * carry(summary)[None]
    v_one = jnp.concatenate([v.astype(F32), jnp.ones((windows, WINDOW, 1), F32)], -1)
    grad_k_feat = jnp.einsum("nfd,nsd->nsf", grad_updates, v_one, precision=HIGHEST)
    dv = dv + jnp.einsum("nsf,nfd->nsd", k_feat_full, grad_updates[..., :HEAD], precision=HIGHEST)
    grad_q_logits = feature_back(grad_q_feat, q_logits)
    grad_k_logits = feature_back(grad_k_feat, k_logits)
    dq = dq + jnp.einsum("ntge,gde->ntgd", grad_q_logits, map_q, preferred_element_type=F32)
    dk = dk + jnp.einsum("nse,de->nsd", grad_k_logits, map_k, preferred_element_type=F32)
    grad_map_q = jnp.einsum("ntgd,ntge->gde", q, grad_q_logits, preferred_element_type=F32)
    grad_map_k = jnp.einsum("nsd,nse->de", k, grad_k_logits, preferred_element_type=F32)
    return dq, dk, dv, grad_map_q, grad_map_k


def shards(
    links,
    hidden_input,
    output_gradient,
    lengths,
    attention_norm_gain,
    query_weight,
    key_weight,
    value_weight,
    output_weight,
    query_adapter_first,
    query_adapter_second,
    key_adapter_first,
    key_adapter_second,
    value_adapter_first,
    value_adapter_second,
    output_adapter_first,
    output_adapter_second,
    query_feature_weight,
    key_feature_weight,
    feedforward_norm_gain,
    gate_weight,
    up_weight,
    down_weight,
):
    links.coords()
    place, side, rank = links.place, links.side, links.rank
    outer, layer = links.outer, links.layer
    rows, width = hidden_input.shape
    layer_rows = rows * layer
    windows = layer_rows // WINDOW
    kv_heads = key_feature_weight.shape[0]
    group = query_feature_weight.shape[0] // kv_heads
    q_wide = group * HEAD

    spans = (lengths + WINDOW - 1) // WINDOW
    seq_ends = jnp.cumsum(spans)
    seq_begins = seq_ends - spans

    def sequence_of(span):
        return jnp.sum((span[..., None] >= seq_ends).astype(jnp.int32), -1)

    local = jnp.arange(windows, dtype=jnp.int32)
    span_seq = sequence_of(place * windows + local)
    seq_first, seq_last = span_seq[0], span_seq[-1]
    before = (
        (local[None, :] < local[:, None]) & (span_seq[None, :] == span_seq[:, None])
    ).astype(F32)
    token_ids = (place * layer + rank) * rows + jnp.arange(rows, dtype=jnp.int32)
    token_seq = sequence_of(token_ids // WINDOW)
    onehot = (token_seq[:, None] == jnp.arange(lengths.shape[0], dtype=jnp.int32)).astype(jnp.int32)
    offset = jnp.sum(onehot * seq_begins * WINDOW, 1)
    limit = jnp.sum(onehot * lengths, 1)
    valid = (token_ids - offset < limit).astype(F32)[:, None]

    def own(v, axis, size):
        return lax.dynamic_slice_in_dim(v, rank * size, size, axis)

    inputs_full = hidden_input.astype(F32)
    gain_one = attention_norm_gain.astype(F32)
    gain_two = feedforward_norm_gain.astype(F32)
    normed_one, inv_one, first_rows = rms_forward(inputs_full, gain_one)

    hidden_part = gate_weight.shape[1] // 2
    chunk = hidden_part // CHUNKS
    third = gate_weight.shape[0]
    down_turned = down_weight.T

    def in_halves(w):
        return w.reshape(third, 2, CHUNKS, chunk).transpose(1, 2, 0, 3)

    halves = jnp.concatenate([in_halves(w) for w in (gate_weight, up_weight, down_turned)], -1)

    row_part = query_weight.shape[0]
    rank_size = query_adapter_first.shape[1]
    kv_end = q_wide + 2 * HEAD
    per_head = outer
    gathered = links.gather_outer(
        jnp.concatenate([query_weight, key_weight, value_weight, output_weight], 1)[None]
    )
    first_blocks, weight_blocks = links.start_rows(first_rows, halves)
    first_all = first_blocks.reshape(layer_rows, width)
    blocks = [
        links.gather_outer(weight_blocks[c].reshape(2 * third, 3 * chunk)) for c in range(CHUNKS)
    ]
    many = max(1, per_head // layer)
    q_all, kv_all = query_weight.shape[1], key_weight.shape[1]
    parts = jnp.concatenate(
        [
            gathered[:, :, a:b].reshape(outer, row_part, layer, -1).transpose(2, 0, 1, 3)
            for a, b in ((0, q_all), (q_all, q_all + kv_all), (q_all + kv_all, q_all + 2 * kv_all))
        ],
        -1,
    )
    out_rows = gathered[:, :, q_all + 2 * kv_all :]
    held = jnp.arange(layer)[:, None] * per_head // layer + jnp.arange(many)[None, :]
    out_parts = out_rows[held]
    parts, out_parts = links.exchange(
        parts.reshape(layer, outer * row_part, kv_end), out_parts
    )
    qkv_weight = parts.reshape(layer, outer, row_part, kv_end).transpose(1, 0, 2, 3)
    adapters = jnp.concatenate([query_adapter_first, key_adapter_first, value_adapter_first], 1)
    qkv_weight = jnp.concatenate([qkv_weight.reshape(width, kv_end), adapters], 1)
    second_q = own(query_adapter_second, 1, q_wide)
    second_k = own(key_adapter_second, 1, HEAD)
    second_v = own(value_adapter_second, 1, HEAD)
    if per_head >= layer:
        out_own = out_parts.transpose(1, 0, 2, 3).reshape(-1, width)
    else:
        start = (rank % (layer // per_head)) * per_head
        out_own = lax.dynamic_slice_in_dim(out_parts, start, per_head, 0).reshape(-1, width)
    oa_own = own(output_adapter_first, 0, q_wide)

    projected = dot(first_all, qkv_weight)
    low_rank = projected[:, kv_end:].astype(BF16)
    low_q, low_k, low_v = (low_rank[:, i * rank_size : (i + 1) * rank_size] for i in range(3))
    second = jnp.concatenate(
        [
            projected[:, :q_wide] + dot(low_q, second_q),
            projected[:, q_wide : q_wide + HEAD] + dot(low_k, second_k),
            projected[:, q_wide + HEAD : kv_end] + dot(low_v, second_v),
        ],
        1,
    ).astype(BF16)

    qkv = second
    q = qkv[:, :q_wide].reshape(windows, WINDOW, group, HEAD)
    k = qkv[:, q_wide : q_wide + HEAD].reshape(windows, WINDOW, HEAD)
    v = qkv[:, q_wide + HEAD :].reshape(windows, WINDOW, HEAD)
    map_q = lax.dynamic_slice_in_dim(query_feature_weight, rank * group, group, 0)
    map_k = lax.dynamic_slice_in_dim(key_feature_weight, rank, 1, 0)[0]

    def carry_forward(summary):
        got = links.between(summary)
        total = jnp.zeros_like(summary)
        for d in range(1, outer):
            joined = sequence_of((place - d + 1) * windows - 1) == seq_first
            total = total + jnp.where(joined & (place >= d), got[d - 1], 0.0)
        return total

    def carry_backward(summary):
        got = links.between(summary)
        total = jnp.zeros_like(summary)
        for d in range(1, outer):
            joined = sequence_of((place + d) * windows) == seq_last
            total = total + jnp.where(joined & (place + d < outer), got[outer - d - 1], 0.0)
        return total

    first_mask = (span_seq == seq_first).astype(F32)
    last_mask = (span_seq == seq_last).astype(F32)
    ratio, kept = attention_forward(
        q, k, v, map_q, map_k, first_mask, before, last_mask, carry_forward
    )
    attended = ratio.astype(BF16).reshape(layer_rows, q_wide)
    low_out = dot(attended, oa_own, BF16)
    branch_part = dot(attended, out_own) + dot(low_out, output_adapter_second)
    branch_part = branch_part.astype(BF16).reshape(layer, rows, width)
    resid = inputs_full + links.scatter_rows(branch_part)

    normed_two, inv_two, rows_two = rms_forward(resid, gain_two)
    grad_y = output_gradient.astype(F32) * valid
    two_all, grad_all = (
        a.reshape(layer_rows, width)
        for a in links.gather_rows(rows_two, grad_y.astype(BF16))
    )
    mlp_part = jnp.zeros((layer_rows, width), F32)
    grad_two_part = jnp.zeros((layer_rows, width), F32)
    gate_outs, up_outs, down_outs = [], [], []
    for c in range(CHUNKS):
        gate_up, down_turned = blocks[c][:, : 2 * chunk], blocks[c][:, 2 * chunk :]
        both = dot(two_all, gate_up)
        gate, upper = both[:, :chunk], both[:, chunk:]
        sigmoid = jax.nn.sigmoid(gate)
        hidden = (gate * sigmoid * upper).astype(BF16)
        grad_hidden = dot(grad_all, down_turned)
        grad_gate = grad_hidden * upper * sigmoid * (1.0 + gate * (1.0 - sigmoid))
        grad_upper = grad_hidden * gate * sigmoid
        grad_both = jnp.concatenate([grad_gate.astype(BF16), grad_upper.astype(BF16)], 1)
        mlp_part = mlp_part + dot_nt(hidden, down_turned)
        grad_two_part = grad_two_part + dot_nt(grad_both, gate_up)
        grad_block = jnp.concatenate(
            [dot_tn(two_all, grad_both, BF16), dot_tn(grad_all, hidden, BF16)], 1
        )
        summed = links.scatter_outer(grad_block).reshape(2, third, 3 * chunk)
        mine = lax.dynamic_index_in_dim(summed, side, 0, False).astype(F32)
        got = links.other_side(lax.dynamic_index_in_dim(summed, 1 - side, 0, False)).astype(F32)
        gate_outs.append((mine[:, :chunk], got[:, :chunk]))
        up_outs.append((mine[:, chunk : 2 * chunk], got[:, chunk : 2 * chunk]))
        down_outs.append((mine[:, 2 * chunk :], got[:, 2 * chunk :]))

    def join(pairs, axis):
        mine = jnp.concatenate([p[0] for p in pairs], axis)
        got = jnp.concatenate([p[1] for p in pairs], axis)
        return jnp.concatenate(
            [jnp.where(side == 0, mine, got), jnp.where(side == 0, got, mine)], axis
        )

    grad_gate_sh, grad_up_sh = join(gate_outs, 1), join(up_outs, 1)
    grad_down_sh = join(down_outs, 1).T
    grad_two_part = grad_two_part.astype(BF16).reshape(layer, rows, width)
    grad_rows_two = links.scatter_rows(grad_two_part)
    mlp_part = mlp_part.astype(BF16).reshape(layer, rows, width)
    mlp_out = links.scatter_rows(mlp_part)
    block_out = (valid * (resid + mlp_out)).astype(BF16)

    grad_gain_two = jnp.sum(grad_rows_two * normed_two, 0)
    grad_resid = grad_y + rms_backward(grad_rows_two, normed_two, inv_two, gain_two)
    branch_all = links.gather_rows(grad_resid.astype(BF16))[0].reshape(layer_rows, width)
    back = dot_nt(branch_all, jnp.concatenate([out_own, output_adapter_second], 0))
    grad_low_out = back[:, q_wide:].astype(BF16)
    grad_attended = back[:, :q_wide] + dot_nt(grad_low_out, oa_own)
    grad_out_own = dot_tn(jnp.concatenate([attended, low_out], 1), branch_all)
    grad_ob = grad_out_own[q_wide:]
    grad_out_own = grad_out_own[:q_wide].astype(BF16)
    grad_oa_own = dot_tn(attended, grad_low_out)
    pieces = grad_out_own.reshape(per_head, row_part, width)

    dq, dk, dv, grad_map_q, grad_map_k = attention_backward(
        kept,
        grad_attended.reshape(windows, WINDOW, group, HEAD),
        q,
        k,
        v,
        map_q,
        map_k,
        first_mask,
        last_mask,
        before,
        carry_backward,
    )
    grads = jnp.concatenate(
        [
            dq.reshape(layer_rows, q_wide).astype(BF16),
            dk.reshape(layer_rows, HEAD).astype(BF16),
            dv.reshape(layer_rows, HEAD).astype(BF16),
        ],
        1,
    )
    grad_q, grad_k, grad_v = (
        grads[:, :q_wide],
        grads[:, q_wide : q_wide + HEAD],
        grads[:, q_wide + HEAD :],
    )
    grads_all = jnp.concatenate(
        [
            grads,
            dot_nt(grad_q, second_q, BF16),
            dot_nt(grad_k, second_k, BF16),
            dot_nt(grad_v, second_v, BF16),
        ],
        1,
    )
    grad_one_part = dot_nt(grads_all, qkv_weight)
    grad_gain_one = jnp.sum(grad_one_part * first_all.astype(F32), 0)
    grad_gain_one = grad_gain_one / gain_one
    grad_one_part = grad_one_part.astype(BF16).reshape(layer, rows, width)
    grad_rows_one = links.scatter_rows(grad_one_part)
    in_grad = grad_resid + rms_backward(grad_rows_one, normed_one, inv_one, gain_one)

    grad_qkv = dot_tn(first_all, grads_all)
    grad_first = grad_qkv[:, kv_end:]
    grad_qkv = grad_qkv[:, :kv_end].astype(BF16).reshape(outer, layer * row_part * kv_end)

    if per_head >= layer:
        pieces = pieces.reshape(many, layer, row_part, width).transpose(1, 0, 2, 3)
    else:
        pieces = pieces[jnp.arange(layer) % per_head][:, None]
    (got,) = links.exchange(pieces)
    if per_head >= layer:
        by_layer = got.reshape(outer, row_part * width)
    else:
        heads = jnp.arange(outer) * (layer // per_head) + rank // per_head
        by_layer = got[heads].reshape(outer, row_part * width)
    sums = jnp.concatenate([grad_qkv, by_layer], 1).reshape(-1, width)
    sums = links.scatter_outer(sums).reshape(-1)
    grad_out_sh = sums[grad_qkv.shape[1] :].reshape(row_part, width).astype(F32)
    (got,) = links.exchange(sums[: grad_qkv.shape[1]].reshape(layer, row_part, kv_end))
    got = got.astype(F32)
    grad_query_sh = got[:, :, :q_wide].transpose(1, 0, 2).reshape(row_part, -1)
    grad_key_sh = got[:, :, q_wide : q_wide + HEAD].transpose(1, 0, 2).reshape(row_part, -1)
    grad_value_sh = got[:, :, q_wide + HEAD :].transpose(1, 0, 2).reshape(row_part, -1)

    flat = [
        dot_tn(low_q, grad_q),
        dot_tn(low_k, grad_k),
        dot_tn(low_v, grad_v),
        grad_oa_own,
        grad_map_q,
        grad_map_k,
    ]
    whole = [grad_first, grad_ob, grad_gain_one, grad_gain_two]
    summed, part = links.sum_small(
        jnp.concatenate([a.reshape(-1) for a in whole]).reshape(-1, 512),
        jnp.concatenate([a.reshape(-1) for a in flat]).reshape(-1, 512),
    )
    summed = summed.reshape(-1)
    part = jnp.broadcast_to(part[None], (layer,) + part.shape)
    spread_all = links.exchange(part)[0].reshape(layer, -1)
    pieces_out, at = [], 0
    for a in flat:
        pieces_out.append(spread_all[:, at : at + a.size].reshape((layer,) + a.shape))
        at += a.size
    grad_qb, grad_kb, grad_vb = (
        p.transpose(1, 0, 2).reshape(rank_size, -1) for p in pieces_out[:3]
    )
    grad_oa = pieces_out[3].reshape(-1, rank_size)
    grad_map_q = pieces_out[4].reshape(-1, HEAD, HEAD)
    grad_map_k = pieces_out[5]

    outs, at = [], 0
    for a in whole:
        outs.append(summed[at : at + a.size].reshape(a.shape))
        at += a.size
    grad_first, grad_ob, grad_gain_one, grad_gain_two = outs
    grad_qa, grad_ka, grad_va = (
        grad_first[:, i * rank_size : (i + 1) * rank_size] for i in range(3)
    )
    return (
        block_out,
        in_grad,
        grad_gain_one,
        grad_query_sh,
        grad_key_sh,
        grad_value_sh,
        grad_out_sh,
        grad_qa,
        grad_qb,
        grad_ka,
        grad_kb,
        grad_va,
        grad_vb,
        grad_oa,
        grad_ob,
        grad_map_q,
        grad_map_k,
        grad_gain_two,
        grad_gate_sh,
        grad_up_sh,
        grad_down_sh,
    )


def solution(mesh):
    rows = P(("dp", "tensor"), None)
    gate = P("dp", "tensor")
    down = P("tensor", "dp")
    links = Links(mesh)
    return jax.shard_map(
        lambda *args: shards(links, *args),
        mesh=mesh,
        in_specs=(rows, rows, P(), P(), rows, rows, rows, rows)
        + (P(),) * 11
        + (gate, gate, down),
        out_specs=(rows, rows, P(), rows, rows, rows, rows)
        + (P(),) * 11
        + (gate, gate, down),
        check_vma=False,
    )
```

```python
import math

import jax
import jax.numpy as jnp
from jax import lax
from jax.experimental import pallas as pl
from jax.experimental.pallas import tpu as pltpu
from jax.sharding import PartitionSpec as P

HEAD = 64
WINDOW = 64
EPSILON = 1e-05
FLOOR_SCORE = -1e30
HIGHEST = lax.Precision.HIGHEST
F32 = jnp.float32
BF16 = jnp.bfloat16
CHUNKS = 2
TILE = 2 * WINDOW


def dot(a, b, out=F32):
    return jnp.dot(a, b, preferred_element_type=F32).astype(out)


def dot_nt(a, b, out=F32):
    return lax.dot_general(a, b, (((1,), (1,)), ((), ())), preferred_element_type=F32).astype(out)


def dot_tt(a, b, out=F32):
    return lax.dot_general(a, b, (((0,), (1,)), ((), ())), preferred_element_type=F32).astype(out)


def dot_tn(a, b, out=F32):
    return lax.dot_general(a, b, (((0,), (0,)), ((), ())), preferred_element_type=F32).astype(out)


def after(v, *others):
    return lax.optimization_barrier((v, *others))[0]


def rms_forward(v, gain):
    inv_root = lax.rsqrt(jnp.mean(v * v, -1, keepdims=True) + EPSILON)
    normed = v * inv_root
    return normed, inv_root, (normed * gain).astype(BF16)


def rms_backward(grad_out, normed, inv_root, gain):
    scaled = grad_out * gain
    return inv_root * (scaled - normed * jnp.mean(scaled * normed, -1, keepdims=True))


MESH = pl.DeviceIdType.MESH


def takes(microseconds):
    return pl.CostEstimate(
        flops=int(microseconds * 1e9),
        bytes_accessed=int(microseconds * 3.3e6),
        transcendentals=0,
    )


class Post:
    def __init__(self, sends, recvs):
        self.sends, self.recvs, self.copies = sends, recvs, []
        self.received, self.sent = set(), set()

    def send(self, src, dst, device):
        i = len(self.copies)
        copy = pltpu.make_async_remote_copy(
            src_ref=src,
            dst_ref=dst,
            send_sem=self.sends.at[i],
            recv_sem=self.recvs.at[i],
            device_id=device,
            device_id_type=MESH,
        )
        copy.start()
        self.copies.append(copy)
        return i

    def arrived(self, i):
        if i not in self.received:
            self.received.add(i)
            self.copies[i].wait_recv()

    def finish(self):
        for i in range(len(self.copies)):
            self.arrived(i)
        for i, copy in enumerate(self.copies):
            if i not in self.sent:
                copy.wait_send()


class Links:
    def __init__(self, mesh):
        self.dp = mesh.shape["dp"]
        self.tensor = mesh.shape["tensor"]
        self.outer = self.dp // 2
        self.layer = 2 * self.tensor
        self.calls = 0

    def coords(self):
        dp = lax.axis_index("dp")
        tensor = lax.axis_index("tensor")
        self.place = dp // 2
        self.side = dp % 2
        self.rank = self.side * self.tensor + tensor


    def flip(self, offset):
        dp = lax.axis_index("dp")
        tensor = lax.axis_index("tensor")
        if offset & 4:
            dp = dp + 1 - 2 * (dp % 2)
        if offset & 2:
            tensor = tensor + 2 - 4 * ((tensor // 2) % 2)
        if offset & 1:
            tensor = tensor + 1 - 2 * (tensor % 2)
        return {"dp": dp, "tensor": tensor}, (dp % 2) * self.tensor + tensor

    def meet(self, devices):
        barrier = pltpu.get_barrier_semaphore()
        for device in devices:
            pl.semaphore_signal(barrier, inc=1, device_id=device, device_id_type=MESH)
        pl.semaphore_wait(barrier, len(devices))

    def call(self, kernel, outs, args, copies, scratch=(), local=0, vmem=48, time=40):
        self.calls += 1
        sems = [pltpu.SemaphoreType.DMA((copies,)), pltpu.SemaphoreType.DMA((copies,))]
        sems += [pltpu.SemaphoreType.DMA((max(local, 1),))]
        return pl.pallas_call(
            kernel,
            out_shape=[jax.ShapeDtypeStruct(s, t) for s, t, _ in outs],
            in_specs=[pl.BlockSpec(memory_space=pl.ANY)] * len(args),
            out_specs=[pl.BlockSpec(memory_space=space) for _, _, space in outs],
            scratch_shapes=sems + list(scratch),
            cost_estimate=takes(time),
            compiler_params=pltpu.CompilerParams(
                collective_id=self.calls, has_side_effects=True, vmem_limit_bytes=vmem * 2**20
            ),
        )(*args)

    def gather_steps(self, post, v, out, local):
        half = v.shape[0] // 2
        a, b = pl.ds(0, half), pl.ds(half, half)
        rank = self.flip(0)[1]
        (dev_c, rank_c), (dev_y, rank_y), (dev_x, rank_x) = (self.flip(i) for i in (1, 2, 4))
        rank_xy = self.flip(6)[1]
        own = pltpu.make_async_copy(v, out.at[rank], local)
        own.start()
        x1 = post.send(v.at[a], out.at[rank, a], dev_x)
        y1 = post.send(v.at[b], out.at[rank, b], dev_y)
        x2 = post.send(v.at[b], out.at[rank, b], dev_x)
        y2 = post.send(v.at[a], out.at[rank, a], dev_y)
        post.send(v, out.at[rank], dev_c)
        post.arrived(x1)
        y3 = post.send(out.at[rank_x, a], out.at[rank_x, a], dev_y)
        post.send(out.at[rank_x, a], out.at[rank_x, a], dev_c)
        post.arrived(y1)
        x3 = post.send(out.at[rank_y, b], out.at[rank_y, b], dev_x)
        post.send(out.at[rank_y, b], out.at[rank_y, b], dev_c)
        yield
        post.arrived(x2)
        post.send(out.at[rank_x, b], out.at[rank_x, b], dev_c)
        post.arrived(y2)
        post.send(out.at[rank_y, a], out.at[rank_y, a], dev_c)
        yield
        post.arrived(y3)
        post.send(out.at[rank_xy, a], out.at[rank_xy, a], dev_c)
        post.arrived(x3)
        post.send(out.at[rank_xy, b], out.at[rank_xy, b], dev_c)
        own.wait()

    def gather_rows(self, *arrays):
        many = len(arrays)

        def kernel(*refs):
            ins, outs = refs[:many], refs[many : 2 * many]
            sends, recvs, local = refs[2 * many :]
            post = Post(sends, recvs)
            self.meet([self.flip(i)[0] for i in (1, 2, 4)])
            steps = [
                self.gather_steps(post, v, out, local.at[i])
                for i, (v, out) in enumerate(zip(ins, outs))
            ]
            for step in steps:
                for _ in step:
                    pass
            post.finish()

        outs = [((self.layer,) + v.shape, v.dtype, pl.ANY) for v in arrays]
        return self.call(kernel, outs, arrays, 13 * many, local=many, time=38 * many)

    def swap_sides(self, arrays, chunk):
        many = len(arrays)
        rows, columns = arrays[0].shape
        half = columns // 2
        chunks = half // chunk

        def kernel(*refs):
            ins, blocks = refs[:many], refs[many : many + chunks]
            sends, recvs, local = refs[many + chunks :]
            post = Post(sends, recvs)
            device = self.flip(4)[0]
            self.meet([device])
            side = lax.axis_index("dp") % 2
            own = []
            for c in range(chunks):
                for k, v in enumerate(ins):

                    def part(of):
                        start = pl.multiple_of(of * half + c * chunk, 128)
                        return v.at[:, pl.ds(start, chunk)]

                    out = blocks[c].at[side, :, pl.ds(k * chunk, chunk)]
                    post.send(part(1 - side), out, device)
                    own.append(pltpu.make_async_copy(part(side), out, local.at[len(own)]))
                    own[-1].start()
            post.finish()
            for copy in own:
                copy.wait()

        outs = [((2, rows, many * chunk), arrays[0].dtype, pl.ANY)] * chunks
        total = many * chunks
        return self.call(kernel, outs, tuple(arrays), total, local=total, time=36)

    def scatter_product(self, lefts, rights, columns=None, sums=None):
        many = len(lefts)
        layer = self.layer
        turned = columns is None
        rows = lefts[0].shape[1 if turned else 0] // layer
        width = rights[0].shape[1 if turned else 0]
        half, wide, step = rows // 2, min(width, 512), 16
        blocks = [
            (v.shape[0], rows) if turned else (rows, v.shape[1]) for v in lefts
        ]
        distinct = []
        for v in rights:
            if not any(v is w for w in distinct):
                distinct.append(v)
        which = [[v is w for w in distinct].index(True) for v in rights]
        extra = () if sums is None else tuple(sums)

        def kernel(*refs):
            refs = list(refs)

            def take(n):
                got = refs[:n]
                del refs[:n]
                return got

            lefts, rights, given = take(many), take(len(distinct)), take(len(extra))
            (out,), given_out = take(1), take(1 if extra else 0)
            sends, recvs, local = take(3)
            mine, far, got, xs, ys = take(5)
            weights, left_blocks = take(len(distinct)), take(many)
            post = Post(sends, recvs)
            devs = [self.flip(i) for i in range(8)]
            dev_c, dev_y, dev_x = devs[1][0], devs[2][0], devs[4][0]
            used = 0
            weight_loads = []
            for v, w in zip(rights, weights):
                weight_loads.append(pltpu.make_async_copy(v, w, local.at[used]))
                weight_loads[-1].start()
                used += 1
            order = (7, 6, 5, 4, 3, 2, 1, 0)
            loads = {}
            for n, i in enumerate(order):
                start = pl.multiple_of(devs[i][1] * rows, rows)
                for k, v in enumerate(lefts):
                    part = v.at[:, pl.ds(start, rows)] if turned else v.at[pl.ds(start, rows)]
                    copy = pltpu.make_async_copy(
                        part, left_blocks[k].at[i], local.at[used + n * many + k]
                    )
                    copy.start()
                    loads[i, k] = copy
            used += layer * many
            near = [dev_c, dev_y, dev_x]
            if extra:
                self.meet([devs[r][0] for r in range(1, layer)] + self.outer_partners())
                steps = self.sum_steps(post, given, given_out, refs, local, used)
            else:
                self.meet(near)
                steps = iter(())
            next(steps, None)
            for load in weight_loads:
                load.wait()

            def product(i, dst):
                for k in range(many):
                    loads[i, k].wait()

                @pl.loop(0, width // wide)
                def _(j):
                    at = pl.ds(pl.multiple_of(j * wide, wide), wide)
                    total = None
                    for k in range(many):
                        block = left_blocks[k][i]
                        weight = weights[which[k]]
                        if turned:
                            term = dot_tn(block, weight[:, at])
                        else:
                            term = dot_nt(block, weight[at, columns[k] : columns[k] + block.shape[1]])
                        total = term if total is None else total + term
                    dst[:, at] = total.astype(BF16)

            def add(dst, one, two):
                @pl.loop(0, dst.shape[0] // step)
                def _(j):
                    at = pl.ds(pl.multiple_of(j * step, step), step)
                    total = one[at, :].astype(F32) + two[at, :].astype(F32)
                    dst[at, :] = total.astype(dst.dtype)

            a, b = pl.ds(0, half), pl.ds(half, half)

            def pair(i):
                product(2 * i + 1, far.at[i])
                arrive = post.send(far.at[i], got.at[i], dev_c)
                product(2 * i, mine.at[i])
                post.arrived(arrive)
                add(mine.at[i], mine.at[i], got.at[i])

            pair(3)
            x1 = post.send(mine.at[3, a], xs.at[0], dev_x)
            y1 = post.send(mine.at[3, b], ys.at[0], dev_y)
            pair(2)
            x2 = post.send(mine.at[2, a], xs.at[1], dev_x)
            pair(1)
            y2 = post.send(mine.at[1, b], ys.at[1], dev_y)
            next(steps, None)
            post.arrived(x1)
            add(mine.at[1, a], mine.at[1, a], xs.at[0])
            y3 = post.send(mine.at[1, a], ys.at[2], dev_y)
            post.arrived(y1)
            add(mine.at[2, b], mine.at[2, b], ys.at[0])
            x3 = post.send(mine.at[2, b], xs.at[2], dev_x)
            next(steps, None)
            pair(0)
            low, high = out.at[a], out.at[b]
            post.arrived(x2)
            add(low, mine.at[0, a], xs.at[1])
            next(steps, None)
            post.arrived(y2)
            add(high, mine.at[0, b], ys.at[1])
            next(steps, None)
            post.arrived(y3)
            add(low, low, ys.at[2])
            post.arrived(x3)
            add(high, high, xs.at[2])
            for _ in steps:
                pass
            post.finish()

        outs = [((rows, width), F32, pltpu.VMEM)]
        scratch = [pltpu.VMEM((4, rows, width), BF16)] * 3
        scratch += [pltpu.VMEM((3, half, width), BF16)] * 2
        scratch += [pltpu.VMEM(v.shape, BF16) for v in distinct]
        scratch += [pltpu.VMEM((layer,) + block, BF16) for block in blocks]
        copies, local = 10, len(distinct) + layer * many
        if extra:
            all_sum, part = extra
            stages = len(self.outer_steps())
            size = all_sum.shape[0] // layer + part.shape[0]
            lanes = part.shape[1]
            outs += [((layer, size, lanes), F32, pltpu.VMEM)]
            scratch += [
                pltpu.VMEM((layer, all_sum.shape[0] // layer, lanes), F32),
                pltpu.VMEM((stages, size, lanes), F32),
            ]
            copies += stages + 2 * (layer - 1)
            local += 2
        got = self.call(
            kernel, outs, (*lefts, *distinct, *extra), copies, scratch, local=local, vmem=56
        )
        return got if extra else got[0]

    def outer_steps(self):
        steps = []
        while 1 << len(steps) < self.outer:
            steps.append(2 << len(steps))
        return steps

    def outer_partners(self):
        dp = lax.axis_index("dp")
        return [{"dp": dp + step - 2 * step * ((dp // step) % 2)} for step in self.outer_steps()]

    def sum_steps(self, post, given, outs, scratch, local, used):
        all_sum, part = given
        (out,) = outs
        pieces, got = scratch
        rank = self.flip(0)[1]
        share = pieces.shape[1]
        mine = out.at[rank]
        copies = [
            pltpu.make_async_copy(all_sum.at[pl.ds(pl.multiple_of(rank * share, 8), share)],
                                  pieces.at[rank], local.at[used]),
            pltpu.make_async_copy(part, mine.at[pl.ds(share, part.shape[0])], local.at[used + 1]),
        ]
        for copy in copies:
            copy.start()
        ids = []
        for r in range(1, self.layer):
            device, target = self.flip(r)
            piece = all_sum.at[pl.ds(pl.multiple_of(target * share, 8), share)]
            ids.append(post.send(piece, pieces.at[rank], device))
        yield
        for copy in copies:
            copy.wait()
        for i in ids:
            post.arrived(i)
        total = pieces[0]
        for r in range(1, self.layer):
            total = total + pieces[r]
        mine[:share] = total
        for n, device in enumerate(self.outer_partners()):
            i = post.send(mine, got.at[n], device)
            yield
            post.arrived(i)
            post.copies[i].wait_send()
            post.sent.add(i)
            mine[...] = mine[...] + got[n]
        for r in range(1, self.layer):
            post.send(mine, out.at[rank], self.flip(r)[0])
        yield

    def exchange_copies(self, v, out, sends, recvs, local, held):
        rank = self.flip(0)[1]

        def run(test, action):
            if held is None:
                action()
            else:
                pl.when(test)(action)

        own = pltpu.make_async_copy(v.at[rank], out.at[rank], local.at[0])
        copies = []
        for i, r in enumerate((6, 7, 4, 5, 2, 3, 1)):
            device, target = self.flip(r)
            copy = pltpu.make_async_remote_copy(
                src_ref=v.at[target],
                dst_ref=out.at[rank],
                send_sem=sends.at[i],
                recv_sem=recvs.at[i],
                device_id=device,
                device_id_type=MESH,
            )
            copies.append((target, copy))

        def start():
            own.start()
            for target, copy in copies:
                run(held and held(rank, target), copy.start)

        def wait():
            for target, copy in copies:
                run(held and held(target, rank), copy.wait_recv)
                run(held and held(rank, target), copy.wait_send)
            own.wait()

        return start, wait

    def exchange(self, v):
        def kernel(v, out, sends, recvs, local):
            self.meet([self.flip(r)[0] for r in range(1, self.layer)])
            start, wait = self.exchange_copies(v, out, sends, recvs, local, None)
            start()
            wait()

        return self.call(kernel, [(v.shape, v.dtype, pl.ANY)], (v,), 7, time=9)[0]

    def between(self, v, pieces, held):
        n = self.outer

        def kernel(v, pieces, out, got, sends, recvs, local):
            dp = lax.axis_index("dp")
            devices = [{"dp": (dp + 2 * d) % self.dp} for d in range(1, n)]
            self.meet(devices + [self.flip(r)[0] for r in range(1, self.layer)])
            post = Post(sends, recvs)
            for d, device in enumerate(devices):
                post.send(v, out.at[d], device)
            after_those = pl.ds(n - 1, 7)
            start, wait = self.exchange_copies(
                pieces, got, sends.at[after_those], recvs.at[after_those], local, held
            )
            start()
            post.finish()
            wait()

        outs = [((n - 1,) + v.shape, v.dtype, pl.ANY), (pieces.shape, pieces.dtype, pl.ANY)]
        return self.call(kernel, outs, (v, pieces), n - 1 + 7, time=20)


    def groups(self):
        return [[2 * o + b for o in range(self.outer)] for b in range(2)]

    def gather_outer(self, v):
        return lax.all_gather(v, "dp", axis_index_groups=self.groups(), tiled=True)

    def scatter_outer(self, v):
        return lax.psum_scatter(v, "dp", axis_index_groups=self.groups(), tiled=True)

    def other_side(self, v):
        return lax.ppermute(v, "dp", [(i, i ^ 1) for i in range(self.dp)])


def stable_maps(logits):
    plus = jnp.exp(logits - jnp.max(logits, 0, keepdims=True))
    minus = jnp.exp(jnp.min(logits, 0, keepdims=True) - logits)
    plus = plus * (1.0 / jnp.sum(plus, 0, keepdims=True))
    minus = minus * (1.0 / jnp.sum(minus, 0, keepdims=True))
    return plus, minus


def maps_back(grad, plus, minus):
    up, down = grad[:HEAD], grad[HEAD:]
    out = plus * (up - jnp.sum(plus * up, 0, keepdims=True))
    return (out - minus * (down - jnp.sum(minus * down, 0, keepdims=True))).astype(BF16)


def heads_wide(v, group):
    return jnp.concatenate([v[h * HEAD : (h + 1) * HEAD] for h in range(group)], 1)


def first_window(lanes):
    return lax.broadcasted_iota(jnp.int32, (1, lanes), 1) % TILE < WINDOW


def window_scores(keys, queries):
    lanes = queries.shape[1]
    scores = dot_tn(keys, queries) * (1.0 / math.sqrt(HEAD))
    j = lax.broadcasted_iota(jnp.int32, (TILE, lanes), 0)
    t = lax.broadcasted_iota(jnp.int32, (TILE, lanes), 1) % TILE
    seen = (j <= t) & (j // WINDOW == t // WINDOW)
    masked = jnp.where(seen, scores, FLOOR_SCORE)
    top = jnp.max(masked, 0, keepdims=True)
    return jnp.where(seen, jnp.exp(masked - top), 0.0), top


def key_kernel(keys, values, map_t, mask, feats, summary):
    summary[...] = jnp.zeros_like(summary)
    step = 2 * TILE

    @pl.loop(0, keys.shape[1] // step)
    def _(i):
        at = pl.ds(pl.multiple_of(i * step, step), step)
        plus, minus = stable_maps(dot(map_t[...], keys[:, at]))
        feat = jnp.concatenate([plus, minus], 0).astype(BF16)
        feats[:, at] = feat
        kept = (feat.astype(F32) * mask[:, at]).astype(BF16)
        summary[...] += dot_nt(kept, values[:, at])


def forward_kernel(
    keep, queries, keys, values, feats, map_t, carry, attended, ratios, denoms, states, state
):
    i = pl.program_id(0)
    group = map_t.shape[0]

    @pl.when(i == 0)
    def _():
        state[...] = carry[...]

    feat_k, vals = feats[...], values[...]
    one = state[...] * keep[2 * i]
    two = (one + dot_nt(feat_k[:, :WINDOW], vals[:, :WINDOW])) * keep[2 * i + 1]
    state[...] = two + dot_nt(feat_k[:, WINDOW:], vals[:, WINDOW:])
    one, two = one.astype(BF16), two.astype(BF16)
    states[0], states[1] = one, two
    rows = queries[...]
    wide = heads_wide(rows, group)
    logits = jnp.concatenate(
        [dot(map_t[h], rows[h * HEAD : (h + 1) * HEAD]) for h in range(group)], 1
    )
    feat_q = jnp.concatenate(stable_maps(logits), 0).astype(BF16)
    expo, top = window_scores(keys[...], wide)
    shrink = jnp.exp(-top)
    window = dot(vals[:HEAD], expo.astype(BF16))
    linear = jnp.where(first_window(wide.shape[1]), dot_tn(one, feat_q), dot_tn(two, feat_q))
    numer = window + shrink * linear[:HEAD]
    denom = jnp.sum(expo, 0, keepdims=True) + shrink * linear[HEAD : HEAD + 1]
    ratio = numer * (1.0 / denom)
    denoms[0] = denom
    for h in range(group):
        part = ratio[:, h * TILE : (h + 1) * TILE]
        ratios[h * HEAD : (h + 1) * HEAD] = part
        attended[h * HEAD : (h + 1) * HEAD] = part.astype(BF16)


def query_kernel(
    first, queries, keys, values, map_t, maps, states, grads, ratios, denoms,
    grad_q, grad_kv, grad_states, grad_maps, summary,
):
    i = pl.program_id(0)
    group = map_t.shape[0]

    @pl.when(i == 0)
    def _():
        grad_maps[...] = jnp.zeros_like(grad_maps)
        summary[...] = jnp.zeros_like(summary)

    rows, key_rows, vals = queries[...], keys[...], values[...]
    wide = heads_wide(rows, group)
    lanes = wide.shape[1]
    grad, ratio = heads_wide(grads[...], group), heads_wide(ratios[...], group)
    inverse = 1.0 / denoms[0]
    grad_num = (grad * inverse).astype(BF16)
    grad_den = -jnp.sum(grad * ratio, 0, keepdims=True) * inverse
    expo, top = window_scores(key_rows, wide)
    shrink = jnp.exp(-top)
    grad_scores = (expo * (dot_tn(vals[:HEAD], grad_num) + grad_den)).astype(BF16)
    scale = 1.0 / math.sqrt(HEAD)
    grad_kv[:HEAD] = dot_nt(wide, grad_scores) * scale
    grad_kv[HEAD:] = dot_nt(grad_num, expo.astype(BF16))
    logits = jnp.concatenate(
        [dot(map_t[h], rows[h * HEAD : (h + 1) * HEAD]) for h in range(group)], 1
    )
    plus, minus = stable_maps(logits)
    feat_q = jnp.concatenate([plus, minus], 0).astype(BF16)
    both = jnp.concatenate(
        [
            grad_num.astype(F32) * shrink,
            grad_den * shrink,
            jnp.zeros((2 * HEAD - HEAD - 1, lanes), F32),
        ],
        0,
    )
    early = first_window(lanes)
    state_one = dot_nt(feat_q, jnp.where(early, both, 0.0).astype(BF16))
    state_two = dot_nt(feat_q, jnp.where(early, 0.0, both).astype(BF16))
    grad_states[0], grad_states[1] = state_one, state_two
    summary[...] += state_one * first[2 * i] + state_two * first[2 * i + 1]
    both = both.astype(BF16)
    grad_feat = jnp.where(early, dot(states[0], both), dot(states[1], both))
    grad_logits = maps_back(grad_feat, plus, minus)
    window = dot(key_rows, grad_scores) * scale
    for h in range(group):
        at, cut = slice(h * HEAD, (h + 1) * HEAD), slice(h * TILE, (h + 1) * TILE)
        grad_q[at] = (window[:, cut] + dot(maps[h], grad_logits[:, cut])).astype(BF16)
        grad_maps[h] += dot_nt(rows[at], grad_logits[:, cut])


def pair_kernel(
    keep, keys, values, feats, map_t, map_k, grad_states, later, window, grad_kv, grad_map, state
):
    i = pl.program_id(0)
    tile = pl.num_programs(0) - 1 - i

    @pl.when(i == 0)
    def _():
        state[...] = later[...]
        grad_map[...] = jnp.zeros_like(grad_map)

    two = state[...]
    one = (two + grad_states[1]) * keep[2 * tile + 1]
    state[...] = (one + grad_states[0]) * keep[2 * tile]
    one, two = one.astype(BF16), two.astype(BF16)
    key_rows, vals, feat = keys[...], values[...], feats[...]
    early = first_window(TILE)
    grad_feat = jnp.where(early, dot(one, vals), dot(two, vals))
    linear = jnp.where(early, dot_tn(one, feat), dot_tn(two, feat))[:HEAD]
    plus, minus = stable_maps(dot(map_t[...], key_rows))
    grad_logits = maps_back(grad_feat, plus, minus)
    grad_kv[:HEAD] = (window[:HEAD] + dot(map_k[...], grad_logits)).astype(BF16)
    grad_kv[HEAD:] = (window[HEAD:] + linear).astype(BF16)
    grad_map[...] += dot_nt(key_rows, grad_logits)


def local_call(kernel, outs, args, time=10, vmem=32, **kwargs):
    return pl.pallas_call(
        kernel,
        out_shape=[jax.ShapeDtypeStruct(s, t) for s, t in outs],
        cost_estimate=takes(time),
        compiler_params=pltpu.CompilerParams(vmem_limit_bytes=vmem * 2**20),
        **kwargs,
    )(*args)


def feedforward_kernel(
    rows, grads, gate_w, up_w, down_w, hidden, grad_gate, grad_up, grad_w, both_t, hidden_t
):
    step = 512
    tile = gate_w.shape[1]

    @pl.loop(0, rows.shape[0] // step)
    def _(i):
        at = pl.ds(pl.multiple_of(i * step, step), step)
        gate = dot(rows[at, :], gate_w[...])
        upper = dot(rows[at, :], up_w[...])
        grad_hidden = dot(grads[at, :], down_w[...])
        sigmoid = 1.0 / (1.0 + jnp.exp(-gate))
        silu = gate * sigmoid
        inner = (silu * upper).astype(BF16)
        one = (grad_hidden * upper * sigmoid * (1.0 + gate * (1.0 - sigmoid))).astype(BF16)
        two = (grad_hidden * silu).astype(BF16)
        hidden[at, :], grad_gate[at, :], grad_up[at, :] = inner, one, two
        hidden_t[:, at] = inner.T
        both_t[:tile, at] = one.T
        both_t[tile:, at] = two.T

    wide = grad_w.shape[-1]

    @pl.loop(0, grad_w.shape[0])
    def _(z):
        at = pl.ds(pl.multiple_of(z * wide, wide), wide)
        both = dot(both_t[...], rows[:, at], BF16)
        grad_w[z, 0], grad_w[z, 1] = both[:tile], both[tile:]
        grad_w[z, 2] = dot(hidden_t[...], grads[:, at], BF16)


def feedforward(rows, grads, weights, chunk, outer):
    many, width = rows.shape
    tile = 256
    tiles, wide = chunk // tile, width // outer
    held = pl.BlockSpec((many, width), lambda j: (0, 0), pipeline_mode=pl.Buffered(1))

    def part(k):
        return pl.BlockSpec((width, tile), lambda j: (0, k * tiles + j))

    column = pl.BlockSpec((many, tile), lambda j: (0, j))
    return local_call(
        feedforward_kernel,
        [((many, chunk), BF16)] * 3 + [((outer, 3, chunk, wide), BF16)],
        (rows, grads, weights, weights, weights),
        time=35,
        vmem=60,
        grid=(tiles,),
        in_specs=[held, held, part(0), part(1), part(2)],
        out_specs=[column] * 3
        + [pl.BlockSpec((outer, 3, tile, wide), lambda j: (0, 0, j, 0))],
        scratch_shapes=[pltpu.VMEM((2 * tile, many), BF16), pltpu.VMEM((tile, many), BF16)],
    )


def whole(shape):
    return pl.BlockSpec(shape, lambda i: (0,) * len(shape))


SCALARS = pl.BlockSpec(memory_space=pltpu.SMEM)


def key_features(keys, values, map_t, mask):
    rows = keys.shape[1]
    return local_call(
        key_kernel,
        [((2 * HEAD, rows), BF16), ((2 * HEAD, 2 * HEAD), F32)],
        (keys, values, map_t, mask),
    )


def attention_forward(keep, queries, keys, values, feats, map_t, carry):
    group, rows = map_t.shape[0], keys.shape[1]
    tiles = rows // TILE
    cols = lambda n: pl.BlockSpec((n, TILE), lambda i: (0, i))
    return local_call(
        forward_kernel,
        [
            ((group * HEAD, rows), BF16),
            ((group * HEAD, rows), F32),
            ((tiles, 1, group * TILE), F32),
            ((2 * tiles, 2 * HEAD, 2 * HEAD), BF16),
        ],
        (keep, queries, keys, values, feats, map_t, carry),
        grid=(tiles,),
        in_specs=[
            SCALARS, cols(group * HEAD), cols(HEAD), cols(2 * HEAD), cols(2 * HEAD),
            whole(map_t.shape), whole(carry.shape),
        ],
        out_specs=[
            cols(group * HEAD),
            cols(group * HEAD),
            pl.BlockSpec((1, 1, group * TILE), lambda i: (i, 0, 0)),
            pl.BlockSpec((2, 2 * HEAD, 2 * HEAD), lambda i: (i, 0, 0)),
        ],
        scratch_shapes=[pltpu.VMEM((2 * HEAD, 2 * HEAD), F32)],
    )


def query_gradients(first, queries, keys, values, map_t, maps, states, grads, ratios, denoms):
    group, rows = map_t.shape[0], keys.shape[1]
    tiles = rows // TILE
    cols = lambda n: pl.BlockSpec((n, TILE), lambda i: (0, i))
    pairs = pl.BlockSpec((2, 2 * HEAD, 2 * HEAD), lambda i: (i, 0, 0))
    return local_call(
        query_kernel,
        [
            ((group * HEAD, rows), BF16),
            ((2 * HEAD, rows), F32),
            ((2 * tiles, 2 * HEAD, 2 * HEAD), F32),
            ((group, HEAD, HEAD), F32),
            ((2 * HEAD, 2 * HEAD), F32),
        ],
        (first, queries, keys, values, map_t, maps, states, grads, ratios, denoms),
        vmem=60,
        grid=(tiles,),
        in_specs=[
            SCALARS, cols(group * HEAD), cols(HEAD), cols(2 * HEAD), whole(map_t.shape),
            whole(maps.shape), pairs, cols(group * HEAD), cols(group * HEAD),
            pl.BlockSpec((1, 1, group * TILE), lambda i: (i, 0, 0)),
        ],
        out_specs=[
            cols(group * HEAD), cols(2 * HEAD), pairs, whole((group, HEAD, HEAD)),
            whole((2 * HEAD, 2 * HEAD)),
        ],
    )


def key_gradients(keep, keys, values, feats, map_t, map_k, grad_states, later, window):
    rows = keys.shape[1]
    tiles = rows // TILE
    cols = lambda n: pl.BlockSpec((n, TILE), lambda i: (0, tiles - 1 - i))
    return local_call(
        pair_kernel,
        [((2 * HEAD, rows), BF16), ((HEAD, HEAD), F32)],
        (keep, keys, values, feats, map_t, map_k, grad_states, later, window),
        grid=(tiles,),
        in_specs=[
            SCALARS, cols(HEAD), cols(2 * HEAD), cols(2 * HEAD), whole(map_t.shape),
            whole(map_k.shape),
            pl.BlockSpec((2, 2 * HEAD, 2 * HEAD), lambda i: (tiles - 1 - i, 0, 0)),
            whole(later.shape), cols(2 * HEAD),
        ],
        out_specs=[cols(2 * HEAD), whole((HEAD, HEAD))],
        scratch_shapes=[pltpu.VMEM((2 * HEAD, 2 * HEAD), F32)],
    )


def shards(
    links,
    hidden_input,
    output_gradient,
    lengths,
    attention_norm_gain,
    query_weight,
    key_weight,
    value_weight,
    output_weight,
    query_adapter_first,
    query_adapter_second,
    key_adapter_first,
    key_adapter_second,
    value_adapter_first,
    value_adapter_second,
    output_adapter_first,
    output_adapter_second,
    query_feature_weight,
    key_feature_weight,
    feedforward_norm_gain,
    gate_weight,
    up_weight,
    down_weight,
):
    links.coords()
    place, side, rank = links.place, links.side, links.rank
    outer, layer = links.outer, links.layer
    rows, width = hidden_input.shape
    layer_rows = rows * layer
    windows = layer_rows // WINDOW
    kv_heads = key_feature_weight.shape[0]
    group = query_feature_weight.shape[0] // kv_heads
    q_wide = group * HEAD

    spans = (lengths + WINDOW - 1) // WINDOW
    seq_ends = jnp.cumsum(spans)
    seq_begins = seq_ends - spans

    def sequence_of(span):
        return jnp.sum((span[..., None] >= seq_ends).astype(jnp.int32), -1)

    local = jnp.arange(windows, dtype=jnp.int32)
    span_seq = sequence_of(place * windows + local)
    seq_first, seq_last = span_seq[0], span_seq[-1]
    same_next = (span_seq[1:] == span_seq[:-1]).astype(F32)
    keep = jnp.concatenate([jnp.ones((1,), F32), same_next])
    first_mask = (span_seq == seq_first).astype(F32)
    last_mask = (span_seq == seq_last).astype(F32)
    token_ids = (place * layer + rank) * rows + jnp.arange(rows, dtype=jnp.int32)
    token_seq = sequence_of(token_ids // WINDOW)
    onehot = (token_seq[:, None] == jnp.arange(lengths.shape[0], dtype=jnp.int32)).astype(jnp.int32)
    offset = jnp.sum(onehot * seq_begins * WINDOW, 1)
    limit = jnp.sum(onehot * lengths, 1)
    valid = (token_ids - offset < limit).astype(F32)[:, None]

    def own(v, axis, size):
        return lax.dynamic_slice_in_dim(v, rank * size, size, axis)

    inputs_full = hidden_input.astype(F32)
    gain_one = attention_norm_gain.astype(F32)
    gain_two = feedforward_norm_gain.astype(F32)
    normed_one, inv_one, first_rows = rms_forward(inputs_full, gain_one)

    row_part = query_weight.shape[0]
    rank_size = query_adapter_first.shape[1]
    kv_end = q_wide + 2 * HEAD
    per_head = outer
    many = max(1, per_head // layer)
    parts = jnp.concatenate(
        [w.reshape(row_part, layer, -1) for w in (query_weight, key_weight, value_weight)], -1
    )
    parts = links.exchange(parts.transpose(1, 0, 2))
    heads_part = jnp.concatenate(
        [
            parts.reshape(layer * row_part, kv_end),
            output_weight.reshape(layer * row_part, width // layer),
        ],
        1,
    )
    gathered = links.gather_outer(heads_part)

    hidden_part = gate_weight.shape[1] // 2
    chunk = hidden_part // CHUNKS
    third = gate_weight.shape[0]

    halves = links.swap_sides(
        (gate_weight, up_weight, after(down_weight.T, parts)), chunk
    )
    blocks = [links.gather_outer(v.reshape(2 * third, 3 * chunk)) for v in halves]
    (first_blocks,) = links.gather_rows(after(first_rows, *halves))
    first_all = first_blocks.reshape(layer_rows, width)

    def held(source, head):
        return (source // per_head) == head % (layer // per_head)

    out_rows = gathered[:, kv_end:].reshape(outer, row_part, width)
    out_parts = out_rows[jnp.arange(layer)[:, None] * per_head // layer + jnp.arange(many)[None, :]]
    adapters = jnp.concatenate([query_adapter_first, key_adapter_first, value_adapter_first], 1)
    adapters = jnp.pad(adapters, ((0, 0), (0, -3 * rank_size % 16)))
    qkv_weight = jnp.concatenate([gathered[:, :kv_end], adapters], 1)
    second_q = own(query_adapter_second, 1, q_wide)
    second_k = own(key_adapter_second, 1, HEAD)
    second_v = own(value_adapter_second, 1, HEAD)
    oa_own = own(output_adapter_first, 0, q_wide)

    projected = dot_tt(qkv_weight, first_all)
    low_rank = projected[kv_end:].astype(BF16)
    low_q, low_k, low_v = (low_rank[i * rank_size : (i + 1) * rank_size] for i in range(3))
    queries = (projected[:q_wide] + dot_tn(second_q, low_q)).astype(BF16)
    keys = (projected[q_wide : q_wide + HEAD] + dot_tn(second_k, low_k)).astype(BF16)
    values = (projected[q_wide + HEAD : kv_end] + dot_tn(second_v, low_v)).astype(BF16)
    values = jnp.concatenate(
        [values, jnp.ones((1, layer_rows), BF16), jnp.zeros((HEAD - 1, layer_rows), BF16)], 0
    )
    maps_q = lax.dynamic_slice_in_dim(query_feature_weight, rank * group, group, 0)
    map_k = lax.dynamic_slice_in_dim(key_feature_weight, rank, 1, 0)[0]
    maps_q_turned, map_k_turned = maps_q.transpose(0, 2, 1), map_k.T

    def sent(source, head):
        return held(head, source)

    def carry_forward(summary):
        got, out_own = links.between(summary, out_parts, held if per_head < layer else None)
        total = jnp.zeros_like(summary)
        for d in range(1, outer):
            joined = sequence_of((place - d + 1) * windows - 1) == seq_first
            total = total + jnp.where(joined & (place >= d), got[d - 1], 0.0)
        return total, out_own

    def carry_backward(summary, pieces):
        got, pieces = links.between(summary, pieces, sent if per_head < layer else None)
        total = jnp.zeros_like(summary)
        for d in range(1, outer):
            joined = sequence_of((place + d) * windows) == seq_last
            total = total + jnp.where(joined & (place + d < outer), got[outer - d - 1], 0.0)
        return total, pieces

    last_tokens = jnp.repeat(last_mask, WINDOW)[None]
    feats, summary = key_features(keys, values, map_k_turned, last_tokens)
    carried, out_parts = carry_forward(summary)
    if per_head >= layer:
        out_own = out_parts.transpose(1, 0, 2, 3).reshape(-1, width)
    else:
        start = (rank % (layer // per_head)) * per_head
        out_own = lax.dynamic_slice_in_dim(out_parts, start, per_head, 0).reshape(-1, width)
    attended, ratios, denoms, states = attention_forward(
        keep, queries, keys, values, feats, maps_q_turned, carried
    )
    low_out = dot_tn(oa_own, attended, BF16)
    pad = 16 - rank_size
    out_both = jnp.concatenate([out_own, output_adapter_second, jnp.zeros((pad, width), BF16)], 0)
    attended_both = jnp.concatenate([attended, low_out, jnp.zeros((pad, layer_rows), BF16)], 0)
    resid = inputs_full + links.scatter_product([attended_both], [out_both])

    normed_two, inv_two, rows_two = rms_forward(resid, gain_two)
    rows_two = after(rows_two, blocks[0])
    grad_y = output_gradient.astype(F32) * valid
    two_all, grad_all = (
        a.reshape(layer_rows, width)
        for a in links.gather_rows(rows_two, grad_y.astype(BF16))
    )
    hiddens, grads_two, block_sums = [], [], []
    for c in range(CHUNKS):
        hidden, grad_gate, grad_up, grad_block = feedforward(
            two_all, grad_all, blocks[c], chunk, outer
        )
        hiddens.append(hidden)
        grads_two += [grad_gate, grad_up]
        block_sums.append(links.scatter_outer(grad_block.reshape(outer * 3 * chunk, -1)))
    grad_rows_two = links.scatter_product(
        grads_two, [blocks[i // 2] for i in range(2 * CHUNKS)], [0, chunk] * CHUNKS
    )

    grad_gain_two = jnp.sum(grad_rows_two * normed_two, 0)
    grad_resid = grad_y + rms_backward(grad_rows_two, normed_two, inv_two, gain_two)
    branch_all = links.gather_rows(grad_resid.astype(BF16))[0].reshape(layer_rows, width)
    back = dot_nt(out_both, branch_all)
    grad_low_out = back[q_wide : q_wide + rank_size].astype(BF16)
    grad_attended = back[:q_wide] + dot(oa_own, grad_low_out)
    grad_attended = after(grad_attended, block_sums[0])
    grad_out_own = dot(attended_both, branch_all)
    grad_ob = grad_out_own[q_wide : q_wide + rank_size]
    grad_out_own = grad_out_own[:q_wide].astype(BF16)
    grad_oa_own = dot_nt(attended, grad_low_out)
    pieces = grad_out_own.reshape(per_head, row_part, width)
    if per_head >= layer:
        pieces = pieces.reshape(many, layer, row_part, width).transpose(1, 0, 2, 3)
    else:
        pieces = pieces[jnp.arange(layer) % per_head][:, None]

    grad_q, window, grad_states, grad_map_q, summary = query_gradients(
        first_mask,
        queries,
        keys,
        values,
        maps_q_turned,
        maps_q,
        states,
        grad_attended,
        ratios,
        denoms,
    )
    later, pieces = carry_backward(summary, pieces)
    grad_kv, grad_map_k = key_gradients(
        keep,
        keys,
        values,
        feats,
        map_k_turned,
        map_k,
        grad_states,
        later,
        window,
    )
    grad_k, grad_v = grad_kv[:HEAD], grad_kv[HEAD:]
    grads_all = jnp.concatenate(
        [
            grad_q,
            grad_kv,
            dot(second_q, grad_q, BF16),
            dot(second_k, grad_k, BF16),
            dot(second_v, grad_v, BF16),
            jnp.zeros((-3 * rank_size % 16, layer_rows), BF16),
        ],
        0,
    )
    grad_qkv = dot_tt(first_all, grads_all)
    grad_gain_one = jnp.sum(grad_qkv * qkv_weight.astype(F32), 1) / gain_one
    grad_first = grad_qkv[:, kv_end : kv_end + 3 * rank_size]
    grad_qkv = grad_qkv[:, :kv_end].astype(BF16)

    if per_head >= layer:
        by_layer = pieces.reshape(outer, row_part, width)
    else:
        by_layer = pieces[jnp.arange(outer) * (layer // per_head) + rank // per_head]
    sums = jnp.concatenate([grad_qkv, by_layer.reshape(width, width // layer)], 1)
    grads_all = after(grads_all, sums, block_sums[-1])
    sums = links.scatter_outer(sums)

    part = [
        dot_nt(low_q, grad_q),
        dot_nt(low_k, grad_k),
        dot_nt(low_v, grad_v),
        grad_oa_own,
        grad_map_q,
        grad_map_k,
    ]
    all_sum = [grad_first, grad_ob, grad_gain_one, grad_gain_two]

    def flat(arrays, multiple):
        v = jnp.concatenate([a.reshape(-1) for a in arrays])
        return jnp.pad(v, (0, -v.size % (128 * multiple))).reshape(-1, 128)

    all_flat = flat(all_sum, 8 * layer)
    share = all_flat.shape[0] // layer
    grad_rows_one, small = links.scatter_product(
        [grads_all], [qkv_weight.T], sums=(all_flat, flat(part, 8))
    )
    summed, spread = small[:, :share], small[:, share:]
    in_grad = grad_resid + rms_backward(grad_rows_one, normed_one, inv_one, gain_one)
    spread = spread.reshape(layer, -1)
    parts, at = [], 0
    for a in part:
        parts.append(spread[:, at : at + a.size].reshape((layer,) + a.shape))
        at += a.size
    grad_qb, grad_kb, grad_vb = (p.transpose(1, 0, 2).reshape(rank_size, -1) for p in parts[:3])
    grad_oa = parts[3].reshape(-1, rank_size)
    grad_map_q = parts[4].reshape(-1, HEAD, HEAD)
    grad_map_k = parts[5]
    summed, at, outs = summed.reshape(-1), 0, []
    for a in all_sum:
        outs.append(summed[at : at + a.size].reshape(a.shape))
        at += a.size
    grad_first, grad_ob, grad_gain_one, grad_gain_two = outs
    grad_qa, grad_ka, grad_va = (
        grad_first[:, i * rank_size : (i + 1) * rank_size] for i in range(3)
    )

    grad_out_sh = sums[:, kv_end:].reshape(row_part, width).astype(F32)
    sums = after(sums[:, :kv_end], grad_rows_one)
    got = links.exchange(sums.reshape(layer, row_part, kv_end))
    mlp_out = links.scatter_product(
        [after(hiddens[0], got)] + hiddens[1:], blocks, [2 * chunk] * CHUNKS
    )
    block_out = (valid * (resid + mlp_out)).astype(BF16)
    got = got.astype(F32)
    grad_query_sh = got[:, :, :q_wide].transpose(1, 0, 2).reshape(row_part, -1)
    grad_key_sh = got[:, :, q_wide : q_wide + HEAD].transpose(1, 0, 2).reshape(row_part, -1)
    grad_value_sh = got[:, :, q_wide + HEAD :].transpose(1, 0, 2).reshape(row_part, -1)

    mine, theirs = [], []
    for summed in block_sums:
        mine.append(lax.dynamic_slice_in_dim(summed, side * third, third, 1))
        theirs.append(
            links.other_side(lax.dynamic_slice_in_dim(summed, (1 - side) * third, third, 1))
        )

    def units(k):
        own, other = (
            jnp.concatenate([v[k * chunk : (k + 1) * chunk] for v in many], 0)
            for many in (mine, theirs)
        )
        return jnp.concatenate(
            [jnp.where(side == 0, own, other), jnp.where(side == 0, other, own)], 0
        )

    grad_gate_sh, grad_up_sh = units(0).T.astype(F32), units(1).T.astype(F32)
    grad_down_sh = units(2).astype(F32)
    return (
        block_out,
        in_grad,
        grad_gain_one,
        grad_query_sh,
        grad_key_sh,
        grad_value_sh,
        grad_out_sh,
        grad_qa,
        grad_qb,
        grad_ka,
        grad_kb,
        grad_va,
        grad_vb,
        grad_oa,
        grad_ob,
        grad_map_q,
        grad_map_k,
        grad_gain_two,
        grad_gate_sh,
        grad_up_sh,
        grad_down_sh,
    )


def solution(mesh):
    rows = P(("dp", "tensor"), None)
    gate = P("dp", "tensor")
    down = P("tensor", "dp")
    links = Links(mesh)
    return jax.shard_map(
        lambda *args: shards(links, *args),
        mesh=mesh,
        in_specs=(rows, rows, P(), P(), rows, rows, rows, rows)
        + (P(),) * 11
        + (gate, gate, down),
        out_specs=(rows, rows, P(), rows, rows, rows, rows)
        + (P(),) * 11
        + (gate, gate, down),
        check_vma=False,
    )
```

```python
import math

import jax
import jax.numpy as jnp
from jax import lax
from jax.experimental import pallas as pl
from jax.experimental.pallas import tpu as pltpu
from jax.sharding import PartitionSpec as P

HEAD = 64
WINDOW = 64
EPSILON = 1e-05
FLOOR_SCORE = -1e30
HIGHEST = lax.Precision.HIGHEST
F32 = jnp.float32
BF16 = jnp.bfloat16
CHUNKS = 2
TILE = 2 * WINDOW


def dot(a, b, out=F32):
    return jnp.dot(a, b, preferred_element_type=F32).astype(out)


def dot_nt(a, b, out=F32):
    return lax.dot_general(a, b, (((1,), (1,)), ((), ())), preferred_element_type=F32).astype(out)


def dot_tt(a, b, out=F32):
    return lax.dot_general(a, b, (((0,), (1,)), ((), ())), preferred_element_type=F32).astype(out)


def dot_tn(a, b, out=F32):
    return lax.dot_general(a, b, (((0,), (0,)), ((), ())), preferred_element_type=F32).astype(out)


def after(v, *others):
    return lax.optimization_barrier((v, *others))[0]


def rms_forward(v, gain):
    inv_root = lax.rsqrt(jnp.mean(v * v, -1, keepdims=True) + EPSILON)
    normed = v * inv_root
    return normed, inv_root, (normed * gain).astype(BF16)


def rms_backward(grad_out, normed, inv_root, gain):
    scaled = grad_out * gain
    return inv_root * (scaled - normed * jnp.mean(scaled * normed, -1, keepdims=True))


MESH = pl.DeviceIdType.MESH


def takes(microseconds):
    return pl.CostEstimate(
        flops=int(microseconds * 1e9),
        bytes_accessed=int(microseconds * 3.3e6),
        transcendentals=0,
    )


class Post:
    def __init__(self, sends, recvs):
        self.sends, self.recvs, self.copies = sends, recvs, []
        self.received, self.sent = set(), set()

    def send(self, src, dst, device):
        i = len(self.copies)
        copy = pltpu.make_async_remote_copy(
            src_ref=src,
            dst_ref=dst,
            send_sem=self.sends.at[i],
            recv_sem=self.recvs.at[i],
            device_id=device,
            device_id_type=MESH,
        )
        copy.start()
        self.copies.append(copy)
        return i

    def arrived(self, i):
        if i not in self.received:
            self.received.add(i)
            self.copies[i].wait_recv()

    def finish(self):
        for i in range(len(self.copies)):
            self.arrived(i)
        for i, copy in enumerate(self.copies):
            if i not in self.sent:
                copy.wait_send()


class Gather:
    def __init__(self, links, post, v, out, local):
        self.post, self.v, self.out = post, v, out
        self.devices = [links.flip(i)[0] for i in range(8)]
        self.ranks = [links.flip(i)[1] for i in range(8)]
        self.rows = v.shape[0]
        self.half = self.rows // 2
        self.own = pltpu.make_async_copy(v, out.at[self.block(0)], local)
        self.ids = {}

    def block(self, offset):
        return pl.ds(pl.multiple_of(self.ranks[offset] * self.rows, self.rows), self.rows)

    def pair(self, offset):
        first = self.ranks[offset] // 2
        return pl.ds(pl.multiple_of(first * 2 * self.rows, 2 * self.rows), 2 * self.rows), first

    def have_pair(self, offset):
        self.have(offset)
        self.have(offset + 1)

    def send(self, offset, part, to):
        half = self.half
        start = pl.multiple_of(self.ranks[offset] * self.rows + part * half, half)
        there = self.out.at[pl.ds(start, half)]
        here = self.v.at[pl.ds(part * half, half)] if offset == 0 else there
        self.ids[offset ^ to, part] = self.post.send(here, there, self.devices[to])

    def start(self):
        self.own.start()
        self.send(0, 0, 4)
        self.send(0, 1, 2)
        self.send(0, 1, 4)
        self.send(0, 0, 2)
        self.send(0, 0, 1)
        self.send(0, 1, 1)

    def have(self, offset, *parts):
        if offset == 0:
            self.own.wait()
        for part in parts or ((0, 1) if offset else ()):
            self.post.arrived(self.ids[offset, part])

    def near(self):
        self.have(4, 0)
        self.send(4, 0, 2)
        self.send(4, 0, 1)
        self.have(2, 1)
        self.send(2, 1, 4)
        self.send(2, 1, 1)

    def middle(self):
        self.have(4, 1)
        self.send(4, 1, 1)
        self.have(2, 0)
        self.send(2, 0, 1)

    def last(self):
        self.have(6)
        self.send(6, 0, 1)
        self.send(6, 1, 1)

    COPIES = 14


class Links:
    def __init__(self, mesh):
        self.dp = mesh.shape["dp"]
        self.tensor = mesh.shape["tensor"]
        self.outer = self.dp // 2
        self.layer = 2 * self.tensor
        self.calls = 0

    def coords(self):
        dp = lax.axis_index("dp")
        tensor = lax.axis_index("tensor")
        self.place = dp // 2
        self.side = dp % 2
        self.rank = self.side * self.tensor + tensor


    def flip(self, offset):
        dp = lax.axis_index("dp")
        tensor = lax.axis_index("tensor")
        if offset & 4:
            dp = dp + 1 - 2 * (dp % 2)
        if offset & 2:
            tensor = tensor + 2 - 4 * ((tensor // 2) % 2)
        if offset & 1:
            tensor = tensor + 1 - 2 * (tensor % 2)
        return {"dp": dp, "tensor": tensor}, (dp % 2) * self.tensor + tensor

    def meet(self, devices):
        barrier = pltpu.get_barrier_semaphore()
        for device in devices:
            pl.semaphore_signal(barrier, inc=1, device_id=device, device_id_type=MESH)
        pl.semaphore_wait(barrier, len(devices))

    def call(self, kernel, outs, args, copies, scratch=(), local=0, vmem=48, time=40, specs=()):
        self.calls += 1
        sems = [pltpu.SemaphoreType.DMA((copies,)), pltpu.SemaphoreType.DMA((copies,))]
        sems += [pltpu.SemaphoreType.DMA((max(local, 1),))]
        return pl.pallas_call(
            kernel,
            out_shape=[jax.ShapeDtypeStruct(s, t) for s, t, _ in outs],
            in_specs=list(specs)
            + [pl.BlockSpec(memory_space=pl.ANY)] * (len(args) - len(specs)),
            out_specs=[pl.BlockSpec(memory_space=space) for _, _, space in outs],
            scratch_shapes=sems + list(scratch),
            cost_estimate=takes(time),
            compiler_params=pltpu.CompilerParams(
                collective_id=self.calls, has_side_effects=True, vmem_limit_bytes=vmem * 2**20
            ),
        )(*args)

    def gather_rows(self, v):
        def kernel(v, out, sends, recvs, local):
            post = Post(sends, recvs)
            self.meet([self.flip(i)[0] for i in (1, 2, 4)])
            gather = Gather(self, post, v, out, local.at[0])
            gather.start()
            gather.near()
            gather.middle()
            gather.last()
            gather.have(0)
            post.finish()

        outs = [((self.layer * v.shape[0], v.shape[1]), v.dtype, pl.ANY)]
        return self.call(kernel, outs, (v,), Gather.COPIES, time=38)[0]

    def gather_feedforward(self, v, grad, weights, chunk):
        layer, outer = self.layer, self.outer
        rows, width = v.shape
        many = layer * rows
        wide = width // outer

        def kernel(v, grad, w, all_rows, all_grads, hidden, grad_gate, grad_up, grad_w, *refs):
            sends, recvs, local, rows_in, grads_in, weight, both, both_t, hidden_t = refs
            post = Post(sends, recvs)
            load = pltpu.make_async_copy(w, weight, local.at[2])
            load.start()
            self.meet([self.flip(i)[0] for i in (1, 2, 4)])
            one = Gather(self, post, v, rows_in, local.at[0])
            two = Gather(self, post, grad, grads_in, local.at[1])
            one.start()
            load.wait()

            def forward(*offsets):
                for offset in offsets:
                    one.have_pair(offset)
                    at, _ = one.pair(offset)
                    both[at, :] = dot(rows_in[at, :], weight[:, : 2 * chunk])

            def backward(*offsets):
                for offset in offsets:
                    two.have_pair(offset)
                    at, _ = two.pair(offset)
                    grad_hidden = dot(grads_in[at, :], weight[:, 2 * chunk :])
                    inner, grad_g, grad_u = hidden_units(
                        both[at, :chunk], both[at, chunk:], grad_hidden
                    )
                    hidden[at, :], grad_gate[at, :], grad_up[at, :] = inner, grad_g, grad_u
                    hidden_t[:, at] = inner.T
                    both_t[:chunk, at] = grad_g.T
                    both_t[chunk:, at] = grad_u.T

            forward(0)
            one.near()
            one.middle()
            two.start()
            forward(4, 2)
            one.last()
            forward(6)
            out = [pltpu.make_async_copy(rows_in, all_rows, local.at[3])]
            out[0].start()
            backward(0)
            two.near()
            two.middle()
            backward(4, 2)
            two.last()
            backward(6)
            out.append(pltpu.make_async_copy(grads_in, all_grads, local.at[4]))
            out[1].start()

            @pl.loop(0, outer)
            def _(z):
                at = pl.ds(pl.multiple_of(z * wide, wide), wide)
                pair = dot(both_t[...], rows_in[:, at], BF16)
                grad_w[z, 0], grad_w[z, 1] = pair[:chunk], pair[chunk:]
                grad_w[z, 2] = dot(hidden_t[...], grads_in[:, at], BF16)

            post.finish()
            for copy in out:
                copy.wait()

        outs = [((many, width), BF16, pl.ANY)] * 2
        outs += [((many, chunk), BF16, pltpu.VMEM)] * 3
        outs += [((outer, 3, chunk, wide), BF16, pltpu.VMEM)]
        scratch = [
            pltpu.VMEM((many, width), BF16),
            pltpu.VMEM((many, width), BF16),
            pltpu.VMEM((width, 3 * chunk), BF16),
            pltpu.VMEM((many, 2 * chunk), F32),
            pltpu.VMEM((2 * chunk, many), BF16),
            pltpu.VMEM((chunk, many), BF16),
        ]
        return self.call(
            kernel, outs, (v, grad, weights), 2 * Gather.COPIES, scratch, local=5, vmem=62, time=90
        )

    def backward_rows(self, scalars, v, first_rows, arrays, held, row_part):
        layer, outer = self.layer, self.outer
        rows, width = v.shape
        many = layer * rows
        group = arrays["map_t"].shape[0]
        q_wide = group * HEAD
        kv_end = q_wide + 2 * HEAD
        names = list(arrays)
        inputs = len(names)
        wide = width // outer
        per_head = outer
        pieces = max(1, per_head // layer)
        tiles = many // TILE
        all_rows = arrays["weight_t"].shape[0]
        low_rows = all_rows - kv_end

        def kernel(first, keep, joined, v, first_rows, *refs):
            refs = list(refs)

            def take(n):
                got = refs[:n]
                del refs[:n]
                return got

            given = take(inputs)
            grads, sums, all_sum, part = take(4)
            sends, recvs, local = take(3)
            (rows_in, grad_t, window, grad_states, grad_low, grad_out, summary, got_s, state) = take(9)
            out_pieces, got_pieces = take(2)
            on = dict(zip(names, take(inputs)))
            post = Post(sends, recvs)
            loads = []
            for i, (name, a) in enumerate(zip(names, given)):
                loads.append(pltpu.make_async_copy(a, on[name], local.at[2 + i]))
                loads[-1].start()
            dp = lax.axis_index("dp")
            others = [{"dp": (dp + 2 * d) % self.dp} for d in range(1, outer)]
            self.meet([self.flip(r)[0] for r in range(1, layer)] + others)
            gather = Gather(self, post, v, rows_in, local.at[0])
            gather.start()
            part[...] = jnp.zeros_like(part)
            summary[...] = jnp.zeros_like(summary)
            grad_out[...] = jnp.zeros_like(grad_out)
            for load in loads:
                load.wait()

            def pair(offset):
                gather.have_pair(offset)
                at, number = gather.pair(offset)
                back = dot_nt(on["out_w"][...], rows_in[at, :])
                low = back[q_wide:].astype(BF16)
                grad_low[:, at] = low
                grad_t[:, at] = back[:q_wide] + dot(on["adapter"][...], low)

                @pl.loop(0, outer)
                def _(j):
                    cut = pl.ds(pl.multiple_of(j * wide, wide), wide)
                    grad_out[:, cut] += dot(on["attended"][:, at], rows_in[at, cut])

                each = 2 * rows // TILE

                @pl.loop(0, each)
                def _(k):
                    query_tile(
                        number * each + k, first, on, grad_t,
                        (grads, window, grad_states, part, summary),
                    )

            pair(0)
            gather.near()
            gather.middle()
            pair(4)
            pair(2)
            gather.last()
            pair(6)

            for d, device in enumerate(others):
                post.send(summary, got_s.at[d], device)
            marks = list(range(len(post.copies) - len(others), len(post.copies)))
            for n in range(marks[0]):
                post.copies[n].wait_send()
                post.sent.add(n)
            load = pltpu.make_async_copy(first_rows, rows_in, local.at[1])
            load.start()
            out_pieces[...] = grad_out[:q_wide, :].astype(BF16)
            rank = self.flip(0)[1]

            def rows_for(target, i):
                index = (i * layer + target) % per_head
                return pl.ds(pl.multiple_of(index * row_part, row_part), row_part)

            def run(test, action):
                if held is None:
                    action()
                else:
                    pl.when(test)(action)

            begun = len(post.copies)
            moves = []
            for r in range(1, layer):
                device, target = self.flip(r)
                for i in range(pieces):
                    n = begun + len(moves)
                    copy = pltpu.make_async_remote_copy(
                        src_ref=out_pieces.at[rows_for(target, i)],
                        dst_ref=got_pieces.at[rank, i],
                        send_sem=sends.at[n],
                        recv_sem=recvs.at[n],
                        device_id=device,
                        device_id_type=MESH,
                    )
                    run(held and held(target, rank), copy.start)
                    moves.append((target, copy))
            for i in range(pieces):
                got_pieces[rank, i] = out_pieces[rows_for(rank, i), :]
            for mark in marks:
                post.arrived(mark)
            later = jnp.zeros_like(summary)
            for e in range(outer - 1):
                later = later + got_s[e] * joined[e]
            state[...] = later

            @pl.loop(0, tiles)
            def _(i):
                key_tile(tiles - 1 - i, keep, on, window, grad_states, state, grads, part)

            grads[kv_end:, :] = dot(on["seconds"][...], grads[:kv_end, :], BF16)
            both = dot_nt(on["low_all"][...], grads[:kv_end, :])
            part[:8] = both[:8, :q_wide]
            part[8:16] = dot_nt(grad_low[...], on["attended"][:q_wide, :])[:8]
            part[80:88, 128 : 128 + HEAD] = both[8:16, q_wide : q_wide + HEAD]
            part[80:88, 128 + HEAD :] = both[16:24, q_wide + HEAD :]
            load.wait()

            @pl.loop(0, outer)
            def _(z):
                at = pl.ds(pl.multiple_of(z * wide, wide), wide)
                total = dot(grads[...], rows_in[:, at])
                sums[z, :kv_end] = total[:kv_end].astype(BF16)
                all_sum[:24, at] = total[kv_end : kv_end + 24]
                all_sum[24:32, at] = grad_out[q_wide : q_wide + 8, at]
                gain = jnp.sum(total * on["weight_t"][:, at].astype(F32), 0, keepdims=True)
                gains = on["gains"][:, at]
                line = lax.broadcasted_iota(jnp.int32, (8, wide), 0)
                gain = gain / gains[:1]
                all_sum[32:, at] = jnp.where(
                    line == 0, gain, jnp.where(line == 1, gains[1:2], 0.0)
                )

            for target, copy in moves:
                run(held and held(rank, target), copy.wait_recv)
                run(held and held(target, rank), copy.wait_send)
            for o in range(outer):
                if per_head >= layer:
                    head, i = o // pieces, o % pieces
                else:
                    head, i = o * (layer // per_head) + rank // per_head, 0
                for j in range(outer):
                    sums[o, kv_end + j * row_part : kv_end + (j + 1) * row_part] = got_pieces[
                        head, i, :, j * wide : (j + 1) * wide
                    ]
            post.finish()

        outs = [
            ((all_rows, many), BF16, pltpu.VMEM),
            ((outer, kv_end + outer * row_part, wide), BF16, pltpu.VMEM),
            ((40, width), F32, pltpu.VMEM),
            ((144, q_wide), F32, pltpu.VMEM),
        ]
        scratch = [
            pltpu.VMEM((many, width), BF16),
            pltpu.VMEM((q_wide, many), F32),
            pltpu.VMEM((2 * HEAD, many), F32),
            pltpu.VMEM((2 * tiles, 2 * HEAD, 2 * HEAD), F32),
            pltpu.VMEM((arrays["adapter"].shape[1], many), BF16),
            pltpu.VMEM(arrays["out_w"].shape, F32),
            pltpu.VMEM((2 * HEAD, 2 * HEAD), F32),
            pltpu.VMEM((outer - 1, 2 * HEAD, 2 * HEAD), F32),
            pltpu.VMEM((2 * HEAD, 2 * HEAD), F32),
            pltpu.VMEM((q_wide, width), BF16),
            pltpu.VMEM((layer, pieces, row_part, width), BF16),
        ]
        scratch += [pltpu.VMEM(a.shape, a.dtype) for a in arrays.values()]
        copies = Gather.COPIES + outer - 1 + pieces * (layer - 1)
        return self.call(
            kernel, outs, (*scalars, v, first_rows, *arrays.values()), copies, scratch,
            local=2 + inputs, vmem=60, time=8, specs=[SCALARS] * 3,
        )

    def swap_sides(self, arrays, chunk):
        many = len(arrays)
        rows, columns = arrays[0].shape
        half = columns // 2
        chunks = half // chunk

        def kernel(*refs):
            ins, blocks = refs[:many], refs[many : many + chunks]
            sends, recvs, local = refs[many + chunks :]
            post = Post(sends, recvs)
            device = self.flip(4)[0]
            self.meet([device])
            side = lax.axis_index("dp") % 2
            own = []
            for c in range(chunks):
                for k, v in enumerate(ins):

                    def part(of):
                        start = pl.multiple_of(of * half + c * chunk, 128)
                        return v.at[:, pl.ds(start, chunk)]

                    out = blocks[c].at[side, :, pl.ds(k * chunk, chunk)]
                    post.send(part(1 - side), out, device)
                    own.append(pltpu.make_async_copy(part(side), out, local.at[len(own)]))
                    own[-1].start()
            post.finish()
            for copy in own:
                copy.wait()

        outs = [((2, rows, many * chunk), arrays[0].dtype, pl.ANY)] * chunks
        total = many * chunks
        return self.call(kernel, outs, tuple(arrays), total, local=total, time=36)

    def scatter_job(self, post, refs, columns, turned, local, loads):
        lefts, rights, out, work = refs
        mine, far, got, xs, ys, weights, blocks = work
        layer, many, step = self.layer, len(lefts), 16
        rows, width = out.shape
        half, wide = rows // 2, min(width, 512)
        devs = [self.flip(i) for i in range(8)]
        dev_c, dev_y, dev_x = devs[1][0], devs[2][0], devs[4][0]
        used = 0

        def load(src, dst):
            nonlocal used
            copy = pltpu.make_async_copy(src, dst, local.at[loads + used])
            copy.start()
            used += 1
            return copy

        weight_loads = []
        for k, (v, w) in enumerate(zip(rights, weights)):
            part = v if turned else v.at[:, pl.ds(columns[k], w.shape[1])]
            weight_loads.append(load(part, w))
        block_loads = {}
        for i in range(layer - 1, -1, -1):
            start = pl.multiple_of(devs[i][1] * rows, rows)
            for k, v in enumerate(lefts):
                part = v.at[:, pl.ds(start, rows)] if turned else v.at[pl.ds(start, rows)]
                block_loads[i, k] = load(part, blocks[k].at[i])
        yield
        for copy in weight_loads:
            copy.wait()

        def product(i, dst):
            for k in range(many):
                block_loads[i, k].wait()

            @pl.loop(0, width // wide)
            def _(j):
                at = pl.ds(pl.multiple_of(j * wide, wide), wide)
                total = None
                for k in range(many):
                    if turned:
                        term = dot_tn(blocks[k][i], weights[k][:, at])
                    else:
                        term = dot_nt(blocks[k][i], weights[k][at, :])
                    total = term if total is None else total + term
                dst[:, at] = total.astype(BF16)

        def add(dst, one, two):
            @pl.loop(0, dst.shape[0] // step)
            def _(j):
                at = pl.ds(pl.multiple_of(j * step, step), step)
                total = one[at, :].astype(F32) + two[at, :].astype(F32)
                dst[at, :] = total.astype(dst.dtype)

        a, b = pl.ds(0, half), pl.ds(half, half)

        def pair(i):
            product(2 * i + 1, far.at[i])
            arrive = post.send(far.at[i], got.at[i], dev_c)
            product(2 * i, mine.at[i])
            post.arrived(arrive)
            add(mine.at[i], mine.at[i], got.at[i])

        pair(3)
        x1 = post.send(mine.at[3, a], xs.at[0], dev_x)
        y1 = post.send(mine.at[3, b], ys.at[0], dev_y)
        yield
        pair(2)
        x2 = post.send(mine.at[2, a], xs.at[1], dev_x)
        yield
        pair(1)
        y2 = post.send(mine.at[1, b], ys.at[1], dev_y)
        yield
        post.arrived(x1)
        add(mine.at[1, a], mine.at[1, a], xs.at[0])
        y3 = post.send(mine.at[1, a], ys.at[2], dev_y)
        post.arrived(y1)
        add(mine.at[2, b], mine.at[2, b], ys.at[0])
        x3 = post.send(mine.at[2, b], xs.at[2], dev_x)
        yield
        pair(0)
        yield
        low, high = out.at[a], out.at[b]
        post.arrived(x2)
        add(low, mine.at[0, a], xs.at[1])
        post.arrived(y2)
        add(high, mine.at[0, b], ys.at[1])
        yield
        post.arrived(y3)
        add(low, low, ys.at[2])
        post.arrived(x3)
        add(high, high, xs.at[2])
        yield

    def scatter_products(self, *jobs, sums=()):
        layer = self.layer
        outs, scratch, sizes, shapes, args = [], [], [], [], []
        local = 0
        for lefts, rights, columns in jobs:
            turned = columns is None
            many = len(lefts)
            rows = lefts[0].shape[1 if turned else 0] // layer
            width = rights[0].shape[1 if turned else 0]
            outs.append(((rows, width), F32, pltpu.VMEM))
            work = [pltpu.VMEM((4, rows, width), BF16)] * 3
            work += [pltpu.VMEM((3, rows // 2, width), BF16)] * 2
            for v, w in zip(lefts, rights):
                work.append(pltpu.VMEM(w.shape if turned else (width, v.shape[1]), BF16))
            for v in lefts:
                block = (v.shape[0], rows) if turned else (rows, v.shape[1])
                work.append(pltpu.VMEM((layer,) + block, BF16))
            scratch += work
            sizes.append(many)
            shapes.append(local)
            local += many * (layer + 1)
            args += [*lefts, *rights]
        copies = 10 * len(jobs)
        if sums:
            all_sum, part = sums
            stages = len(self.outer_steps())
            size, lanes = all_sum.shape[0] + part.shape[0], part.shape[1]
            outs += [
                ((all_sum.shape[0] + 24, layer * lanes), BF16, pltpu.VMEM),
                ((layer, part.shape[0] - 16, lanes), BF16, pltpu.VMEM),
            ]
            scratch += [
                pltpu.VMEM((layer, all_sum.shape[0], lanes), F32),
                pltpu.VMEM((stages, size, lanes), F32),
                pltpu.VMEM((size, lanes), F32),
                pltpu.VMEM((size + 8, lanes), BF16),
            ]
            copies += stages + 3 * (layer - 1)
            local += 2

        def kernel(*refs):
            refs = list(refs)

            def take(n):
                got = refs[:n]
                del refs[:n]
                return got

            given = [(take(n), take(n)) for n in sizes]
            given_sums = take(len(sums))
            made = take(len(jobs))
            made_sums = take(2 if sums else 0)
            sends, recvs, local_sems = take(3)
            post = Post(sends, recvs)
            runs = []
            for (lefts, rights), out, n, first, job in zip(given, made, sizes, shapes, jobs):
                work = take(5) + [take(n), take(n)]
                runs.append(
                    self.scatter_job(
                        post, (lefts, rights, out, work), job[2], job[2] is None, local_sems, first
                    )
                )
                next(runs[-1])
            if sums:
                self.meet(
                    [self.flip(r)[0] for r in range(1, layer)] + self.outer_partners()
                )
                runs.append(
                    self.sum_steps(post, given_sums, made_sums, refs, local_sems, local - 2)
                )
                next(runs[-1])
            else:
                self.meet([self.flip(i)[0] for i in (1, 2, 4)])
            if sums and len(jobs) == 2:
                order = (0, 0, 1, 0, 2, 1, 0, 1, 0, 2, 0, 1, 2, 1, 1, 0, 2, 1)
            else:
                order = [n for _ in range(7) for n in range(len(runs))]
            for n in order:
                next(runs[n], None)
            for run in runs:
                for _ in run:
                    pass
            post.finish()

        return self.call(
            kernel, outs, (*args, *sums), copies, scratch, local=local, vmem=60,
            time=4 * len(jobs),
        )

    def outer_steps(self):
        steps = []
        while 1 << len(steps) < self.outer:
            steps.append(2 << len(steps))
        return steps

    def outer_partners(self):
        dp = lax.axis_index("dp")
        return [{"dp": dp + step - 2 * step * ((dp // step) % 2)} for step in self.outer_steps()]

    def sum_steps(self, post, given, outs, scratch, local, used):
        all_sum, part = given
        columns, others = outs
        pieces, got, mine, rounded = scratch
        rank = self.flip(0)[1]
        share, lanes = pieces.shape[1], pieces.shape[2]
        split = share + 24

        def columns_of(r):
            return pl.ds(pl.multiple_of(r * lanes, lanes), lanes)

        copies = [
            pltpu.make_async_copy(all_sum.at[:, columns_of(rank)], pieces.at[rank], local.at[used]),
            pltpu.make_async_copy(
                part, mine.at[pl.ds(share, part.shape[0])], local.at[used + 1]
            ),
        ]
        for copy in copies:
            copy.start()
        ids = []
        for r in range(1, self.layer):
            device, target = self.flip(r)
            ids.append(post.send(all_sum.at[:, columns_of(target)], pieces.at[rank], device))
        yield
        for copy in copies:
            copy.wait()
        for i in ids:
            post.arrived(i)
        total = pieces[0]
        for r in range(1, self.layer):
            total = total + pieces[r]
        mine[:share] = total
        for n, device in enumerate(self.outer_partners()):
            i = post.send(mine, got.at[n], device)
            yield
            post.arrived(i)
            post.copies[i].wait_send()
            post.sent.add(i)
            mine[...] = mine[...] + got[n]
        rounded[: split - 8] = mine[: split - 8].astype(BF16)
        rounded[split - 8 : split] = jnp.zeros((8, lanes), BF16)
        rounded[split:] = mine[split - 8 :].astype(BF16)
        for r in range(1, self.layer):
            device = self.flip(r)[0]
            post.send(rounded.at[pl.ds(0, split)], columns.at[:, columns_of(rank)], device)
            post.send(rounded.at[pl.ds(split, others.shape[1])], others.at[rank], device)
        columns[:, columns_of(rank)] = rounded[:split]
        others[rank] = rounded[split:]
        yield

    def exchange_copies(self, v, out, sends, recvs, local, held):
        rank = self.flip(0)[1]

        def run(test, action):
            if held is None:
                action()
            else:
                pl.when(test)(action)

        own = pltpu.make_async_copy(v.at[rank], out.at[rank], local.at[0])
        copies = []
        for i, r in enumerate((6, 7, 4, 5, 2, 3, 1)):
            device, target = self.flip(r)
            copy = pltpu.make_async_remote_copy(
                src_ref=v.at[target],
                dst_ref=out.at[rank],
                send_sem=sends.at[i],
                recv_sem=recvs.at[i],
                device_id=device,
                device_id_type=MESH,
            )
            copies.append((target, copy))

        def start():
            own.start()
            for target, copy in copies:
                run(held and held(rank, target), copy.start)

        def wait():
            for target, copy in copies:
                run(held and held(target, rank), copy.wait_recv)
                run(held and held(rank, target), copy.wait_send)
            own.wait()

        return start, wait

    def exchange(self, v):
        def kernel(v, out, sends, recvs, local):
            self.meet([self.flip(r)[0] for r in range(1, self.layer)])
            start, wait = self.exchange_copies(v, out, sends, recvs, local, None)
            start()
            wait()

        return self.call(kernel, [(v.shape, v.dtype, pl.ANY)], (v,), 7, time=9)[0]

    def between(self, v, pieces, held):
        n = self.outer

        def kernel(v, pieces, out, got, sends, recvs, local):
            dp = lax.axis_index("dp")
            devices = [{"dp": (dp + 2 * d) % self.dp} for d in range(1, n)]
            self.meet(devices + [self.flip(r)[0] for r in range(1, self.layer)])
            post = Post(sends, recvs)
            for d, device in enumerate(devices):
                post.send(v, out.at[d], device)
            after_those = pl.ds(n - 1, 7)
            start, wait = self.exchange_copies(
                pieces, got, sends.at[after_those], recvs.at[after_those], local, held
            )
            start()
            post.finish()
            wait()

        outs = [((n - 1,) + v.shape, v.dtype, pl.ANY), (pieces.shape, pieces.dtype, pl.ANY)]
        return self.call(kernel, outs, (v, pieces), n - 1 + 7, time=20)


    def groups(self):
        return [[2 * o + b for o in range(self.outer)] for b in range(2)]

    def gather_outer(self, v):
        return lax.all_gather(v, "dp", axis_index_groups=self.groups(), tiled=True)

    def scatter_outer(self, v):
        return lax.psum_scatter(v, "dp", axis_index_groups=self.groups(), tiled=True)

    def other_side(self, v):
        return lax.ppermute(v, "dp", [(i, i ^ 1) for i in range(self.dp)])


def stable_maps(logits):
    plus = jnp.exp(logits - jnp.max(logits, 0, keepdims=True))
    minus = jnp.exp(jnp.min(logits, 0, keepdims=True) - logits)
    plus = plus * (1.0 / jnp.sum(plus, 0, keepdims=True))
    minus = minus * (1.0 / jnp.sum(minus, 0, keepdims=True))
    return plus, minus


def maps_back(grad, plus, minus):
    up, down = grad[:HEAD], grad[HEAD:]
    out = plus * (up - jnp.sum(plus * up, 0, keepdims=True))
    return (out - minus * (down - jnp.sum(minus * down, 0, keepdims=True))).astype(BF16)


def heads_wide(v, group):
    return jnp.concatenate([v[h * HEAD : (h + 1) * HEAD] for h in range(group)], 1)


def first_window(lanes):
    return lax.broadcasted_iota(jnp.int32, (1, lanes), 1) % TILE < WINDOW


def window_scores(keys, queries):
    lanes = queries.shape[1]
    scores = dot_tn(keys, queries) * (1.0 / math.sqrt(HEAD))
    j = lax.broadcasted_iota(jnp.int32, (TILE, lanes), 0)
    t = lax.broadcasted_iota(jnp.int32, (TILE, lanes), 1) % TILE
    seen = (j <= t) & (j // WINDOW == t // WINDOW)
    masked = jnp.where(seen, scores, FLOOR_SCORE)
    top = jnp.max(masked, 0, keepdims=True)
    return jnp.where(seen, jnp.exp(masked - top), 0.0), top


def key_kernel(keys, values, map_t, mask, feats, summary):
    summary[...] = jnp.zeros_like(summary)
    step = 2 * TILE

    @pl.loop(0, keys.shape[1] // step)
    def _(i):
        at = pl.ds(pl.multiple_of(i * step, step), step)
        plus, minus = stable_maps(dot(map_t[...], keys[:, at]))
        feat = jnp.concatenate([plus, minus], 0).astype(BF16)
        feats[:, at] = feat
        kept = (feat.astype(F32) * mask[:, at]).astype(BF16)
        summary[...] += dot_nt(kept, values[:, at])


def forward_kernel(
    keep, queries, keys, values, feats, map_t, carry, attended, ratios, denoms, states, state
):
    i = pl.program_id(0)
    group = map_t.shape[0]

    @pl.when(i == 0)
    def _():
        state[...] = carry[...]

    feat_k, vals = feats[...], values[...]
    one = state[...] * keep[2 * i]
    two = (one + dot_nt(feat_k[:, :WINDOW], vals[:, :WINDOW])) * keep[2 * i + 1]
    state[...] = two + dot_nt(feat_k[:, WINDOW:], vals[:, WINDOW:])
    one, two = one.astype(BF16), two.astype(BF16)
    states[0], states[1] = one, two
    rows = queries[...]
    wide = heads_wide(rows, group)
    logits = jnp.concatenate(
        [dot(map_t[h], rows[h * HEAD : (h + 1) * HEAD]) for h in range(group)], 1
    )
    feat_q = jnp.concatenate(stable_maps(logits), 0).astype(BF16)
    expo, top = window_scores(keys[...], wide)
    shrink = jnp.exp(-top)
    window = dot(vals[:HEAD], expo.astype(BF16))
    linear = jnp.where(first_window(wide.shape[1]), dot_tn(one, feat_q), dot_tn(two, feat_q))
    numer = window + shrink * linear[:HEAD]
    denom = jnp.sum(expo, 0, keepdims=True) + shrink * linear[HEAD : HEAD + 1]
    ratio = numer * (1.0 / denom)
    denoms[0] = denom
    for h in range(group):
        part = ratio[:, h * TILE : (h + 1) * TILE]
        ratios[h * HEAD : (h + 1) * HEAD] = part
        attended[h * HEAD : (h + 1) * HEAD] = part.astype(BF16)


def query_tile(tile, first, on, grad_t, outs):
    grads, window_kv, grad_states, part, summary = outs
    map_t, maps, states = on["map_t"], on["maps"], on["states"]
    group = map_t.shape[0]
    at = pl.ds(pl.multiple_of(tile * TILE, TILE), TILE)
    rows, key_rows, vals = on["queries"][:, at], on["keys"][:, at], on["values"][:, at]
    wide = heads_wide(rows, group)
    lanes = wide.shape[1]
    grad, ratio = heads_wide(grad_t[:, at], group), heads_wide(on["ratios"][:, at], group)
    inverse = 1.0 / on["denoms"][tile]
    grad_num = (grad * inverse).astype(BF16)
    grad_den = -jnp.sum(grad * ratio, 0, keepdims=True) * inverse
    expo, top = window_scores(key_rows, wide)
    shrink = jnp.exp(-top)
    grad_scores = (expo * (dot_tn(vals[:HEAD], grad_num) + grad_den)).astype(BF16)
    scale = 1.0 / math.sqrt(HEAD)
    window_kv[:HEAD, at] = dot_nt(wide, grad_scores) * scale
    window_kv[HEAD:, at] = dot_nt(grad_num, expo.astype(BF16))
    logits = jnp.concatenate(
        [dot(map_t[h], rows[h * HEAD : (h + 1) * HEAD]) for h in range(group)], 1
    )
    plus, minus = stable_maps(logits)
    feat_q = jnp.concatenate([plus, minus], 0).astype(BF16)
    both = jnp.concatenate(
        [
            grad_num.astype(F32) * shrink,
            grad_den * shrink,
            jnp.zeros((2 * HEAD - HEAD - 1, lanes), F32),
        ],
        0,
    )
    early = first_window(lanes)
    state_one = dot_nt(feat_q, jnp.where(early, both, 0.0).astype(BF16))
    state_two = dot_nt(feat_q, jnp.where(early, 0.0, both).astype(BF16))
    grad_states[2 * tile], grad_states[2 * tile + 1] = state_one, state_two
    summary[...] += state_one * first[2 * tile] + state_two * first[2 * tile + 1]
    both = both.astype(BF16)
    grad_feat = jnp.where(early, dot(states[2 * tile], both), dot(states[2 * tile + 1], both))
    grad_logits = maps_back(grad_feat, plus, minus)
    window = dot(key_rows, grad_scores) * scale
    grad_maps = []
    for h in range(group):
        head, cut = slice(h * HEAD, (h + 1) * HEAD), slice(h * TILE, (h + 1) * TILE)
        grads[head, at] = (window[:, cut] + dot(maps[h], grad_logits[:, cut])).astype(BF16)
        grad_maps.append(dot_nt(rows[head], grad_logits[:, cut]))
    part[16 : 16 + HEAD] += jnp.concatenate(grad_maps, 1)


def key_tile(tile, keep, on, window, grad_states, state, grads, part):
    at = pl.ds(pl.multiple_of(tile * TILE, TILE), TILE)
    two = state[...]
    one = (two + grad_states[2 * tile + 1]) * keep[2 * tile + 1]
    state[...] = (one + grad_states[2 * tile]) * keep[2 * tile]
    one, two = one.astype(BF16), two.astype(BF16)
    key_rows, vals, feat = on["keys"][:, at], on["values"][:, at], on["feats"][:, at]
    early = first_window(TILE)
    grad_feat = jnp.where(early, dot(one, vals), dot(two, vals))
    linear = jnp.where(early, dot_tn(one, feat), dot_tn(two, feat))[:HEAD]
    plus, minus = stable_maps(dot(on["map_k_t"][...], key_rows))
    grad_logits = maps_back(grad_feat, plus, minus)
    start = grads.shape[0] - on["seconds"].shape[0] - 2 * HEAD
    grads[start : start + HEAD, at] = (
        window[:HEAD, at] + dot(on["map_k"][...], grad_logits)
    ).astype(BF16)
    grads[start + HEAD : start + 2 * HEAD, at] = (window[HEAD:, at] + linear).astype(BF16)
    part[16 + HEAD : 16 + 2 * HEAD, :HEAD] += dot_nt(key_rows, grad_logits)


def local_call(kernel, outs, args, time=10, vmem=32, **kwargs):
    return pl.pallas_call(
        kernel,
        out_shape=[jax.ShapeDtypeStruct(s, t) for s, t in outs],
        cost_estimate=takes(time),
        compiler_params=pltpu.CompilerParams(vmem_limit_bytes=vmem * 2**20),
        **kwargs,
    )(*args)


def hidden_units(gate, upper, grad_hidden):
    sigmoid = 1.0 / (1.0 + jnp.exp(-gate))
    silu = gate * sigmoid
    grad_gate = grad_hidden * upper * sigmoid * (1.0 + gate * (1.0 - sigmoid))
    return (silu * upper).astype(BF16), grad_gate.astype(BF16), (grad_hidden * silu).astype(BF16)


def feedforward_kernel(
    rows, grads, gate_w, up_w, down_w, hidden, grad_gate, grad_up, grad_w, both_t, hidden_t
):
    step = 512
    tile = gate_w.shape[1]

    @pl.loop(0, rows.shape[0] // step)
    def _(i):
        at = pl.ds(pl.multiple_of(i * step, step), step)
        gate = dot(rows[at, :], gate_w[...])
        upper = dot(rows[at, :], up_w[...])
        grad_hidden = dot(grads[at, :], down_w[...])
        inner, one, two = hidden_units(gate, upper, grad_hidden)
        hidden[at, :], grad_gate[at, :], grad_up[at, :] = inner, one, two
        hidden_t[:, at] = inner.T
        both_t[:tile, at] = one.T
        both_t[tile:, at] = two.T

    wide = grad_w.shape[-1]

    @pl.loop(0, grad_w.shape[0])
    def _(z):
        at = pl.ds(pl.multiple_of(z * wide, wide), wide)
        both = dot(both_t[...], rows[:, at], BF16)
        grad_w[z, 0], grad_w[z, 1] = both[:tile], both[tile:]
        grad_w[z, 2] = dot(hidden_t[...], grads[:, at], BF16)


def feedforward(rows, grads, weights, chunk, outer):
    many, width = rows.shape
    tile = 256
    tiles, wide = chunk // tile, width // outer
    held = pl.BlockSpec((many, width), lambda j: (0, 0), pipeline_mode=pl.Buffered(1))

    def part(k):
        return pl.BlockSpec((width, tile), lambda j: (0, k * tiles + j))

    column = pl.BlockSpec((many, tile), lambda j: (0, j))
    return local_call(
        feedforward_kernel,
        [((many, chunk), BF16)] * 3 + [((outer, 3, chunk, wide), BF16)],
        (rows, grads, weights, weights, weights),
        time=35,
        vmem=60,
        grid=(tiles,),
        in_specs=[held, held, part(0), part(1), part(2)],
        out_specs=[column] * 3
        + [pl.BlockSpec((outer, 3, tile, wide), lambda j: (0, 0, j, 0))],
        scratch_shapes=[pltpu.VMEM((2 * tile, many), BF16), pltpu.VMEM((tile, many), BF16)],
    )


def whole(shape):
    return pl.BlockSpec(shape, lambda i: (0,) * len(shape))


SCALARS = pl.BlockSpec(memory_space=pltpu.SMEM)


def key_features(keys, values, map_t, mask):
    rows = keys.shape[1]
    return local_call(
        key_kernel,
        [((2 * HEAD, rows), BF16), ((2 * HEAD, 2 * HEAD), F32)],
        (keys, values, map_t, mask),
    )


def attention_forward(keep, queries, keys, values, feats, map_t, carry):
    group, rows = map_t.shape[0], keys.shape[1]
    tiles = rows // TILE
    cols = lambda n: pl.BlockSpec((n, TILE), lambda i: (0, i))
    return local_call(
        forward_kernel,
        [
            ((group * HEAD, rows), BF16),
            ((group * HEAD, rows), F32),
            ((tiles, 1, group * TILE), F32),
            ((2 * tiles, 2 * HEAD, 2 * HEAD), BF16),
        ],
        (keep, queries, keys, values, feats, map_t, carry),
        grid=(tiles,),
        in_specs=[
            SCALARS, cols(group * HEAD), cols(HEAD), cols(2 * HEAD), cols(2 * HEAD),
            whole(map_t.shape), whole(carry.shape),
        ],
        out_specs=[
            cols(group * HEAD),
            cols(group * HEAD),
            pl.BlockSpec((1, 1, group * TILE), lambda i: (i, 0, 0)),
            pl.BlockSpec((2, 2 * HEAD, 2 * HEAD), lambda i: (i, 0, 0)),
        ],
        scratch_shapes=[pltpu.VMEM((2 * HEAD, 2 * HEAD), F32)],
    )


def shards(
    links,
    hidden_input,
    output_gradient,
    lengths,
    attention_norm_gain,
    query_weight,
    key_weight,
    value_weight,
    output_weight,
    query_adapter_first,
    query_adapter_second,
    key_adapter_first,
    key_adapter_second,
    value_adapter_first,
    value_adapter_second,
    output_adapter_first,
    output_adapter_second,
    query_feature_weight,
    key_feature_weight,
    feedforward_norm_gain,
    gate_weight,
    up_weight,
    down_weight,
):
    links.coords()
    place, side, rank = links.place, links.side, links.rank
    outer, layer = links.outer, links.layer
    rows, width = hidden_input.shape
    layer_rows = rows * layer
    windows = layer_rows // WINDOW
    kv_heads = key_feature_weight.shape[0]
    group = query_feature_weight.shape[0] // kv_heads
    q_wide = group * HEAD

    spans = (lengths + WINDOW - 1) // WINDOW
    seq_ends = jnp.cumsum(spans)
    seq_begins = seq_ends - spans

    def sequence_of(span):
        return jnp.sum((span[..., None] >= seq_ends).astype(jnp.int32), -1)

    local = jnp.arange(windows, dtype=jnp.int32)
    span_seq = sequence_of(place * windows + local)
    seq_first, seq_last = span_seq[0], span_seq[-1]
    same_next = (span_seq[1:] == span_seq[:-1]).astype(F32)
    keep = jnp.concatenate([jnp.ones((1,), F32), same_next])
    first_mask = (span_seq == seq_first).astype(F32)
    last_mask = (span_seq == seq_last).astype(F32)
    token_ids = (place * layer + rank) * rows + jnp.arange(rows, dtype=jnp.int32)
    token_seq = sequence_of(token_ids // WINDOW)
    onehot = (token_seq[:, None] == jnp.arange(lengths.shape[0], dtype=jnp.int32)).astype(jnp.int32)
    offset = jnp.sum(onehot * seq_begins * WINDOW, 1)
    limit = jnp.sum(onehot * lengths, 1)
    valid = (token_ids - offset < limit).astype(F32)[:, None]

    def own(v, axis, size):
        return lax.dynamic_slice_in_dim(v, rank * size, size, axis)

    inputs_full = hidden_input.astype(F32)
    gain_one = attention_norm_gain.astype(F32)
    gain_two = feedforward_norm_gain.astype(F32)
    normed_one, inv_one, first_rows = rms_forward(inputs_full, gain_one)

    row_part = query_weight.shape[0]
    rank_size = query_adapter_first.shape[1]
    kv_end = q_wide + 2 * HEAD
    per_head = outer
    many = max(1, per_head // layer)
    parts = jnp.concatenate(
        [w.reshape(row_part, layer, -1) for w in (query_weight, key_weight, value_weight)], -1
    )
    parts = links.exchange(parts.transpose(1, 0, 2))
    heads_part = jnp.concatenate(
        [
            parts.reshape(layer * row_part, kv_end),
            output_weight.reshape(layer * row_part, width // layer),
        ],
        1,
    )
    gathered = links.gather_outer(heads_part)

    hidden_part = gate_weight.shape[1] // 2
    chunk = hidden_part // CHUNKS
    third = gate_weight.shape[0]

    halves = links.swap_sides(
        (gate_weight, up_weight, after(down_weight.T, parts)), chunk
    )
    blocks = [links.gather_outer(v.reshape(2 * third, 3 * chunk)) for v in halves]
    first_all = links.gather_rows(after(first_rows, *halves))

    def held(source, head):
        return (source // per_head) == head % (layer // per_head)

    out_rows = gathered[:, kv_end:].reshape(outer, row_part, width)
    out_parts = out_rows[jnp.arange(layer)[:, None] * per_head // layer + jnp.arange(many)[None, :]]
    adapters = jnp.concatenate([query_adapter_first, key_adapter_first, value_adapter_first], 1)
    adapters = jnp.pad(adapters, ((0, 0), (0, -3 * rank_size % 16)))
    qkv_weight = jnp.concatenate([gathered[:, :kv_end], adapters], 1)
    second_q = own(query_adapter_second, 1, q_wide)
    second_k = own(key_adapter_second, 1, HEAD)
    second_v = own(value_adapter_second, 1, HEAD)
    oa_own = own(output_adapter_first, 0, q_wide)

    projected = dot_tt(qkv_weight, first_all)
    low_rank = projected[kv_end:].astype(BF16)
    low_q, low_k, low_v = (low_rank[i * rank_size : (i + 1) * rank_size] for i in range(3))
    queries = (projected[:q_wide] + dot_tn(second_q, low_q)).astype(BF16)
    keys = (projected[q_wide : q_wide + HEAD] + dot_tn(second_k, low_k)).astype(BF16)
    values = (projected[q_wide + HEAD : kv_end] + dot_tn(second_v, low_v)).astype(BF16)
    values = jnp.concatenate(
        [values, jnp.ones((1, layer_rows), BF16), jnp.zeros((HEAD - 1, layer_rows), BF16)], 0
    )
    maps_q = lax.dynamic_slice_in_dim(query_feature_weight, rank * group, group, 0)
    map_k = lax.dynamic_slice_in_dim(key_feature_weight, rank, 1, 0)[0]
    maps_q_turned, map_k_turned = maps_q.transpose(0, 2, 1), map_k.T

    def carry_forward(summary):
        got, out_own = links.between(summary, out_parts, held if per_head < layer else None)
        total = jnp.zeros_like(summary)
        for d in range(1, outer):
            joined = sequence_of((place - d + 1) * windows - 1) == seq_first
            total = total + jnp.where(joined & (place >= d), got[d - 1], 0.0)
        return total, out_own

    last_tokens = jnp.repeat(last_mask, WINDOW)[None]
    feats, summary = key_features(keys, values, map_k_turned, last_tokens)
    carried, out_parts = carry_forward(summary)
    if per_head >= layer:
        out_own = out_parts.transpose(1, 0, 2, 3).reshape(-1, width)
    else:
        start = (rank % (layer // per_head)) * per_head
        out_own = lax.dynamic_slice_in_dim(out_parts, start, per_head, 0).reshape(-1, width)
    attended, ratios, denoms, states = attention_forward(
        keep, queries, keys, values, feats, maps_q_turned, carried
    )
    low_out = dot_tn(oa_own, attended, BF16)
    pad = 16 - rank_size
    out_both = jnp.concatenate([out_own, output_adapter_second, jnp.zeros((pad, width), BF16)], 0)
    attended_both = jnp.concatenate([attended, low_out, jnp.zeros((pad, layer_rows), BF16)], 0)
    resid = inputs_full + links.scatter_products(([attended_both], [out_both], None))[0]

    normed_two, inv_two, rows_two = rms_forward(resid, gain_two)
    rows_two = after(rows_two, blocks[0])
    grad_y = output_gradient.astype(F32) * valid
    hiddens, grads_two, block_sums = [], [], []
    for c in range(CHUNKS):
        if c == 0:
            two_all, grad_all, *made = links.gather_feedforward(
                rows_two, grad_y.astype(BF16), blocks[c], chunk
            )
        else:
            made = feedforward(two_all, grad_all, blocks[c], chunk, outer)
        hidden, grad_gate, grad_up, grad_block = made
        hiddens.append(hidden)
        grads_two += [grad_gate, grad_up]
        block_sums.append(links.scatter_outer(grad_block.reshape(outer * 3 * chunk, -1)))
    (grad_rows_two,) = links.scatter_products(
        (grads_two, [blocks[i // 2] for i in range(2 * CHUNKS)], [0, chunk] * CHUNKS)
    )

    grad_gain_two = jnp.sum(grad_rows_two * normed_two, 0)
    grad_resid = grad_y + rms_backward(grad_rows_two, normed_two, inv_two, gain_two)
    weight_t = qkv_weight.T
    seconds = jnp.zeros((weight_t.shape[0] - kv_end, kv_end), BF16)
    seconds = seconds.at[:rank_size, :q_wide].set(second_q)
    seconds = seconds.at[rank_size : 2 * rank_size, q_wide : q_wide + HEAD].set(second_k)
    seconds = seconds.at[2 * rank_size : 3 * rank_size, q_wide + HEAD :].set(second_v)
    joined = [
        (sequence_of((place + d) * windows) == seq_last) & (place + d < outer)
        for d in range(outer - 1, 0, -1)
    ]
    grads_all, sums, all_sum, part = links.backward_rows(
        (first_mask, keep, jnp.stack(joined).astype(F32)),
        grad_resid.astype(BF16),
        first_all,
        {
            "out_w": out_both,
            "attended": attended_both,
            "adapter": jnp.pad(oa_own, ((0, 0), (0, pad))),
            "queries": queries,
            "keys": keys,
            "values": values,
            "map_t": maps_q_turned,
            "maps": maps_q,
            "map_k_t": map_k_turned,
            "map_k": map_k,
            "states": states,
            "ratios": ratios,
            "denoms": denoms,
            "feats": feats,
            "seconds": seconds,
            "low_all": low_rank,
            "weight_t": weight_t,
            "gains": jnp.pad(jnp.stack([gain_one, grad_gain_two]), ((0, 6), (0, 0))),
        },
        held if per_head < layer else None,
        row_part,
    )
    sums = after(sums, block_sums[0])
    grads_all = after(grads_all, sums)
    sums = links.scatter_outer(sums.reshape(-1, sums.shape[-1]))
    mlp_out, grad_rows_one, columns, others = links.scatter_products(
        (hiddens, blocks, [2 * chunk] * CHUNKS),
        ([grads_all], [weight_t], None),
        sums=(all_sum, part),
    )
    small_done = grad_rows_one
    wide = width // outer
    grad_out_sh = sums[kv_end:].reshape(outer, row_part, wide).transpose(1, 0, 2)
    grad_out_sh = grad_out_sh.reshape(row_part, width).astype(F32)
    sums = after(sums[:kv_end].T, grad_rows_one)
    got = links.exchange(sums.reshape(layer, row_part, kv_end))
    mlp_out, grad_rows_one, columns, others, got = lax.optimization_barrier(
        (mlp_out, grad_rows_one, columns, others, got)
    )
    got, columns, others = got.astype(F32), columns.astype(F32), others.astype(F32)
    grad_query_sh = got[:, :, :q_wide].transpose(1, 0, 2).reshape(row_part, -1)
    grad_key_sh = got[:, :, q_wide : q_wide + HEAD].transpose(1, 0, 2).reshape(row_part, -1)
    grad_value_sh = got[:, :, q_wide + HEAD :].transpose(1, 0, 2).reshape(row_part, -1)

    block_out = (valid * (resid + mlp_out)).astype(BF16)
    in_grad = grad_resid + rms_backward(grad_rows_one, normed_one, inv_one, gain_one)

    grad_qa, grad_ka, grad_va = (
        columns[i * rank_size : (i + 1) * rank_size].T for i in range(3)
    )
    grad_ob, grad_gain_one, grad_gain_two = columns[24:32], columns[32], columns[33]
    grad_qb, grad_oa = columns[40:48], columns[48:56].T
    grad_map_q = others[:, :HEAD].reshape(layer, HEAD, group, HEAD).transpose(0, 2, 1, 3)
    grad_map_q = grad_map_q.reshape(-1, HEAD, HEAD)
    grad_map_k = others[:, HEAD : 2 * HEAD, :HEAD]
    grad_kb, grad_vb = (
        others[:, HEAD : HEAD + rank_size, 128 + i * HEAD : 128 + (i + 1) * HEAD]
        .transpose(1, 0, 2)
        .reshape(rank_size, -1)
        for i in range(2)
    )

    mine, theirs = [], []
    for summed in block_sums:
        summed = after(summed, small_done)
        mine.append(lax.dynamic_slice_in_dim(summed, side * third, third, 1))
        got = links.other_side(lax.dynamic_slice_in_dim(summed, (1 - side) * third, third, 1))
        theirs.append(after(got, in_grad))

    def units(k):
        own, other = (
            jnp.concatenate([v[k * chunk : (k + 1) * chunk] for v in many], 0)
            for many in (mine, theirs)
        )
        return jnp.concatenate(
            [jnp.where(side == 0, own, other), jnp.where(side == 0, other, own)], 0
        )

    grad_gate_sh, grad_up_sh = units(0).T.astype(F32), units(1).T.astype(F32)
    grad_down_sh = units(2).astype(F32)
    return (
        block_out,
        in_grad,
        grad_gain_one,
        grad_query_sh,
        grad_key_sh,
        grad_value_sh,
        grad_out_sh,
        grad_qa,
        grad_qb,
        grad_ka,
        grad_kb,
        grad_va,
        grad_vb,
        grad_oa,
        grad_ob,
        grad_map_q,
        grad_map_k,
        grad_gain_two,
        grad_gate_sh,
        grad_up_sh,
        grad_down_sh,
    )


def solution(mesh):
    rows = P(("dp", "tensor"), None)
    gate = P("dp", "tensor")
    down = P("tensor", "dp")
    links = Links(mesh)
    return jax.shard_map(
        lambda *args: shards(links, *args),
        mesh=mesh,
        in_specs=(rows, rows, P(), P(), rows, rows, rows, rows)
        + (P(),) * 11
        + (gate, gate, down),
        out_specs=(rows, rows, P(), rows, rows, rows, rows)
        + (P(),) * 11
        + (gate, gate, down),
        check_vma=False,
    )
```

```python
import math

import jax
import jax.numpy as jnp
from jax import lax
from jax.experimental import pallas as pl
from jax.experimental.pallas import tpu as pltpu
from jax.sharding import PartitionSpec as P

HEAD = 64
WINDOW = 64
EPSILON = 1e-05
FLOOR_SCORE = -1e30
HIGHEST = lax.Precision.HIGHEST
F32 = jnp.float32
BF16 = jnp.bfloat16
CHUNKS = 2
TILE = 2 * WINDOW


def dot(a, b, out=F32):
    return jnp.dot(a, b, preferred_element_type=F32).astype(out)


def dot_nt(a, b, out=F32):
    return lax.dot_general(a, b, (((1,), (1,)), ((), ())), preferred_element_type=F32).astype(out)


def dot_tt(a, b, out=F32):
    return lax.dot_general(a, b, (((0,), (1,)), ((), ())), preferred_element_type=F32).astype(out)


def dot_tn(a, b, out=F32):
    return lax.dot_general(a, b, (((0,), (0,)), ((), ())), preferred_element_type=F32).astype(out)


def after(v, *others):
    return lax.optimization_barrier((v, *others))[0]


def rms_forward(v, gain):
    inv_root = lax.rsqrt(jnp.mean(v * v, -1, keepdims=True) + EPSILON)
    normed = v * inv_root
    return normed, inv_root, (normed * gain).astype(BF16)


def rms_backward(grad_out, normed, inv_root, gain):
    scaled = grad_out * gain
    return inv_root * (scaled - normed * jnp.mean(scaled * normed, -1, keepdims=True))


MESH = pl.DeviceIdType.MESH


def takes(microseconds):
    return pl.CostEstimate(
        flops=int(microseconds * 1e9),
        bytes_accessed=int(microseconds * 3.3e6),
        transcendentals=0,
    )


class Post:
    def __init__(self, sends, recvs):
        self.sends, self.recvs, self.copies = sends, recvs, []
        self.received, self.sent = set(), set()

    def send(self, src, dst, device):
        i = len(self.copies)
        copy = pltpu.make_async_remote_copy(
            src_ref=src,
            dst_ref=dst,
            send_sem=self.sends.at[i],
            recv_sem=self.recvs.at[i],
            device_id=device,
            device_id_type=MESH,
        )
        copy.start()
        self.copies.append(copy)
        return i

    def arrived(self, i):
        if i not in self.received:
            self.received.add(i)
            self.copies[i].wait_recv()

    def finish(self):
        for i in range(len(self.copies)):
            self.arrived(i)
        for i, copy in enumerate(self.copies):
            if i not in self.sent:
                copy.wait_send()


class Gather:
    def __init__(self, links, post, v, out, local):
        self.post, self.v, self.out = post, v, out
        self.devices = [links.flip(i)[0] for i in range(8)]
        self.ranks = [links.flip(i)[1] for i in range(8)]
        self.rows = v.shape[0]
        self.half = self.rows // 2
        self.own = pltpu.make_async_copy(v, out.at[self.block(0)], local)
        self.ids = {}

    def block(self, offset):
        return pl.ds(pl.multiple_of(self.ranks[offset] * self.rows, self.rows), self.rows)

    def pair(self, offset):
        first = self.ranks[offset] // 2
        return pl.ds(pl.multiple_of(first * 2 * self.rows, 2 * self.rows), 2 * self.rows), first

    def have_pair(self, offset):
        self.have(offset)
        self.have(offset + 1)

    def send(self, offset, part, to):
        half = self.half
        start = pl.multiple_of(self.ranks[offset] * self.rows + part * half, half)
        there = self.out.at[pl.ds(start, half)]
        here = self.v.at[pl.ds(part * half, half)] if offset == 0 else there
        self.ids[offset ^ to, part] = self.post.send(here, there, self.devices[to])

    def start(self):
        self.own.start()
        self.send(0, 0, 4)
        self.send(0, 1, 2)
        self.send(0, 1, 4)
        self.send(0, 0, 2)
        self.send(0, 0, 1)
        self.send(0, 1, 1)

    def have(self, offset, *parts):
        if offset == 0:
            self.own.wait()
        for part in parts or ((0, 1) if offset else ()):
            self.post.arrived(self.ids[offset, part])

    def near(self):
        self.have(4, 0)
        self.send(4, 0, 2)
        self.send(4, 0, 1)
        self.have(2, 1)
        self.send(2, 1, 4)
        self.send(2, 1, 1)

    def middle(self):
        self.have(4, 1)
        self.send(4, 1, 1)
        self.have(2, 0)
        self.send(2, 0, 1)

    def last(self):
        self.have(6)
        self.send(6, 0, 1)
        self.send(6, 1, 1)

    COPIES = 14


class Links:
    def __init__(self, mesh):
        self.dp = mesh.shape["dp"]
        self.tensor = mesh.shape["tensor"]
        self.outer = self.dp // 2
        self.layer = 2 * self.tensor
        self.calls = 0

    def coords(self):
        dp = lax.axis_index("dp")
        tensor = lax.axis_index("tensor")
        self.place = dp // 2
        self.side = dp % 2
        self.rank = self.side * self.tensor + tensor


    def flip(self, offset):
        dp = lax.axis_index("dp")
        tensor = lax.axis_index("tensor")
        if offset & 4:
            dp = dp + 1 - 2 * (dp % 2)
        if offset & 2:
            tensor = tensor + 2 - 4 * ((tensor // 2) % 2)
        if offset & 1:
            tensor = tensor + 1 - 2 * (tensor % 2)
        return {"dp": dp, "tensor": tensor}, (dp % 2) * self.tensor + tensor

    def meet(self, devices):
        barrier = pltpu.get_barrier_semaphore()
        for device in devices:
            pl.semaphore_signal(barrier, inc=1, device_id=device, device_id_type=MESH)
        pl.semaphore_wait(barrier, len(devices))

    def call(self, kernel, outs, args, copies, scratch=(), local=0, vmem=48, time=40, specs=()):
        self.calls += 1
        sems = [pltpu.SemaphoreType.DMA((copies,)), pltpu.SemaphoreType.DMA((copies,))]
        sems += [pltpu.SemaphoreType.DMA((max(local, 1),))]
        return pl.pallas_call(
            kernel,
            out_shape=[jax.ShapeDtypeStruct(s, t) for s, t, _ in outs],
            in_specs=list(specs)
            + [pl.BlockSpec(memory_space=pl.ANY)] * (len(args) - len(specs)),
            out_specs=[pl.BlockSpec(memory_space=space) for _, _, space in outs],
            scratch_shapes=sems + list(scratch),
            cost_estimate=takes(time),
            compiler_params=pltpu.CompilerParams(
                collective_id=self.calls, has_side_effects=True, vmem_limit_bytes=vmem * 2**20
            ),
        )(*args)

    def gather_rows(self, v):
        def kernel(v, out, sends, recvs, local):
            post = Post(sends, recvs)
            self.meet([self.flip(i)[0] for i in (1, 2, 4)])
            gather = Gather(self, post, v, out, local.at[0])
            gather.start()
            gather.near()
            gather.middle()
            gather.last()
            gather.have(0)
            post.finish()

        outs = [((self.layer * v.shape[0], v.shape[1]), v.dtype, pl.ANY)]
        return self.call(kernel, outs, (v,), Gather.COPIES, time=38)[0]

    def gather_feedforward(self, v, grad, weights, chunk):
        layer, outer = self.layer, self.outer
        rows, width = v.shape
        many = layer * rows
        wide = width // outer

        def kernel(v, grad, w, all_rows, all_grads, hidden, grad_gate, grad_up, grad_w, *refs):
            sends, recvs, local, rows_in, grads_in, weight, both, both_t, hidden_t = refs
            post = Post(sends, recvs)
            load = pltpu.make_async_copy(w, weight, local.at[2])
            load.start()
            self.meet([self.flip(i)[0] for i in (1, 2, 4)])
            one = Gather(self, post, v, rows_in, local.at[0])
            two = Gather(self, post, grad, grads_in, local.at[1])
            one.start()
            load.wait()

            def forward(*offsets):
                for offset in offsets:
                    one.have_pair(offset)
                    at, _ = one.pair(offset)
                    both[at, :] = dot(rows_in[at, :], weight[:, : 2 * chunk])

            def backward(*offsets):
                for offset in offsets:
                    two.have_pair(offset)
                    at, _ = two.pair(offset)
                    grad_hidden = dot(grads_in[at, :], weight[:, 2 * chunk :])
                    inner, grad_g, grad_u = hidden_units(
                        both[at, :chunk], both[at, chunk:], grad_hidden
                    )
                    hidden[at, :], grad_gate[at, :], grad_up[at, :] = inner, grad_g, grad_u
                    hidden_t[:, at] = inner.T
                    both_t[:chunk, at] = grad_g.T
                    both_t[chunk:, at] = grad_u.T

            forward(0)
            one.near()
            one.middle()
            two.start()
            forward(4, 2)
            one.last()
            forward(6)
            out = [pltpu.make_async_copy(rows_in, all_rows, local.at[3])]
            out[0].start()
            backward(0)
            two.near()
            two.middle()
            backward(4, 2)
            two.last()
            backward(6)
            out.append(pltpu.make_async_copy(grads_in, all_grads, local.at[4]))
            out[1].start()

            @pl.loop(0, outer)
            def _(z):
                at = pl.ds(pl.multiple_of(z * wide, wide), wide)
                pair = dot(both_t[...], rows_in[:, at], BF16)
                grad_w[z, 0], grad_w[z, 1] = pair[:chunk], pair[chunk:]
                grad_w[z, 2] = dot(hidden_t[...], grads_in[:, at], BF16)

            post.finish()
            for copy in out:
                copy.wait()

        outs = [((many, width), BF16, pl.ANY)] * 2
        outs += [((many, chunk), BF16, pltpu.VMEM)] * 3
        outs += [((outer, 3, chunk, wide), BF16, pltpu.VMEM)]
        scratch = [
            pltpu.VMEM((many, width), BF16),
            pltpu.VMEM((many, width), BF16),
            pltpu.VMEM((width, 3 * chunk), BF16),
            pltpu.VMEM((many, 2 * chunk), F32),
            pltpu.VMEM((2 * chunk, many), BF16),
            pltpu.VMEM((chunk, many), BF16),
        ]
        return self.call(
            kernel, outs, (v, grad, weights), 2 * Gather.COPIES, scratch, local=5, vmem=62, time=90
        )

    def backward_rows(self, scalars, v, first_rows, arrays, held, row_part, job):
        layer, outer = self.layer, self.outer
        rows, width = v.shape
        many = layer * rows
        group = arrays["map_t"].shape[0]
        q_wide = group * HEAD
        kv_end = q_wide + 2 * HEAD
        names = list(arrays)
        inputs = len(names)
        wide = width // outer
        per_head = outer
        pieces = max(1, per_head // layer)
        tiles = many // TILE
        all_rows = arrays["weight_t"].shape[0]
        lefts, rights, job_columns = job
        jobs = len(lefts)
        job_scratch = self.job_scratch(job)

        def kernel(first, keep, joined, v, first_rows, *refs):
            refs = list(refs)

            def take(n):
                got = refs[:n]
                del refs[:n]
                return got

            given = take(inputs)
            job_refs = take(jobs), take(jobs)
            grads, sums, all_sum, part, job_out = take(5)
            sends, recvs, local = take(3)
            (rows_in, grad_t, window, grad_states, grad_low, grad_out, summary, got_s, state) = take(9)
            out_pieces, got_pieces = take(2)
            on = dict(zip(names, take(inputs)))
            work = take(4) + [take(jobs), take(jobs)]
            post = Post(sends, recvs)
            run_job = self.scatter_job(
                post, (*job_refs, job_out, work), job_columns, False, local, 2 + inputs
            )
            loads = []
            for i, (name, a) in enumerate(zip(names, given)):
                loads.append(pltpu.make_async_copy(a, on[name], local.at[2 + i]))
                loads[-1].start()
            dp = lax.axis_index("dp")
            others = [{"dp": (dp + 2 * d) % self.dp} for d in range(1, outer)]
            self.meet([self.flip(r)[0] for r in range(1, layer)] + others)
            gather = Gather(self, post, v, rows_in, local.at[0])
            gather.start()
            next(run_job)
            part[...] = jnp.zeros_like(part)
            summary[...] = jnp.zeros_like(summary)
            grad_out[...] = jnp.zeros_like(grad_out)
            for load in loads:
                load.wait()

            def pair(offset):
                gather.have_pair(offset)
                at, number = gather.pair(offset)
                back = dot_nt(on["out_w"][...], rows_in[at, :])
                low = back[q_wide:].astype(BF16)
                grad_low[:, at] = low
                grad_t[:, at] = back[:q_wide] + dot(on["adapter"][...], low)

                @pl.loop(0, outer)
                def _(j):
                    cut = pl.ds(pl.multiple_of(j * wide, wide), wide)
                    grad_out[:, cut] += dot(on["attended"][:, at], rows_in[at, cut])

                each = 2 * rows // TILE

                @pl.loop(0, each)
                def _(k):
                    query_tile(
                        number * each + k, first, on, grad_t,
                        (grads, window, grad_states, part, summary),
                    )

            pair(0)
            gather.near()
            gather.middle()
            pair(4)
            pair(2)
            gather.last()
            pair(6)

            for d, device in enumerate(others):
                post.send(summary, got_s.at[d], device)
            marks = list(range(len(post.copies) - len(others), len(post.copies)))
            for n in range(marks[0]):
                post.copies[n].wait_send()
                post.sent.add(n)
            load = pltpu.make_async_copy(first_rows, rows_in, local.at[1])
            load.start()
            out_pieces[...] = grad_out[:q_wide, :].astype(BF16)
            rank = self.flip(0)[1]

            def rows_for(target, i):
                index = (i * layer + target) % per_head
                return pl.ds(pl.multiple_of(index * row_part, row_part), row_part)

            def run(test, action):
                if held is None:
                    action()
                else:
                    pl.when(test)(action)

            begun = Gather.COPIES + outer - 1 + 10
            moves = []
            for r in range(1, layer):
                device, target = self.flip(r)
                for i in range(pieces):
                    n = begun + len(moves)
                    copy = pltpu.make_async_remote_copy(
                        src_ref=out_pieces.at[rows_for(target, i)],
                        dst_ref=got_pieces.at[rank, i],
                        send_sem=sends.at[n],
                        recv_sem=recvs.at[n],
                        device_id=device,
                        device_id_type=MESH,
                    )
                    run(held and held(target, rank), copy.start)
                    moves.append((target, copy))
            for i in range(pieces):
                got_pieces[rank, i] = out_pieces[rows_for(rank, i), :]
            next(run_job)
            next(run_job)
            next(run_job)
            for mark in marks:
                post.arrived(mark)
            later = jnp.zeros_like(summary)
            for e in range(outer - 1):
                later = later + got_s[e] * joined[e]
            state[...] = later

            @pl.loop(0, tiles)
            def _(i):
                key_tile(tiles - 1 - i, keep, on, window, grad_states, state, grads, part)

            next(run_job)
            next(run_job)
            grads[kv_end:, :] = dot(on["seconds"][...], grads[:kv_end, :], BF16)
            both = dot_nt(on["low_all"][...], grads[:kv_end, :])
            part[:8] = both[:8, :q_wide]
            part[8:16] = dot_nt(grad_low[...], on["attended"][:q_wide, :])[:8]
            part[80:88, 128 : 128 + HEAD] = both[8:16, q_wide : q_wide + HEAD]
            part[80:88, 128 + HEAD :] = both[16:24, q_wide + HEAD :]
            load.wait()

            @pl.loop(0, outer)
            def _(z):
                at = pl.ds(pl.multiple_of(z * wide, wide), wide)
                total = dot(grads[...], rows_in[:, at])
                sums[z, :kv_end] = total[:kv_end].astype(BF16)
                all_sum[:24, at] = total[kv_end : kv_end + 24]
                all_sum[24:32, at] = grad_out[q_wide : q_wide + 8, at]
                gain = jnp.sum(total * on["weight_t"][:, at].astype(F32), 0, keepdims=True)
                gains = on["gains"][:, at]
                line = lax.broadcasted_iota(jnp.int32, (8, wide), 0)
                gain = gain / gains[:1]
                all_sum[32:, at] = jnp.where(
                    line == 0, gain, jnp.where(line == 1, gains[1:2], 0.0)
                )

            next(run_job)
            for target, copy in moves:
                run(held and held(rank, target), copy.wait_recv)
                run(held and held(target, rank), copy.wait_send)
            for o in range(outer):
                if per_head >= layer:
                    head, i = o // pieces, o % pieces
                else:
                    head, i = o * (layer // per_head) + rank // per_head, 0
                for j in range(outer):
                    sums[o, kv_end + j * row_part : kv_end + (j + 1) * row_part] = got_pieces[
                        head, i, :, j * wide : (j + 1) * wide
                    ]
            for _ in run_job:
                pass
            post.finish()

        outs = [
            ((all_rows, many), BF16, pltpu.VMEM),
            ((outer, kv_end + outer * row_part, wide), BF16, pltpu.VMEM),
            ((40, width), F32, pltpu.VMEM),
            ((144, q_wide), F32, pltpu.VMEM),
            (v.shape, F32, pltpu.VMEM),
        ]
        scratch = [
            pltpu.VMEM((many, width), BF16),
            pltpu.VMEM((q_wide, many), F32),
            pltpu.VMEM((2 * HEAD, many), F32),
            pltpu.VMEM((2 * tiles, 2 * HEAD, 2 * HEAD), F32),
            pltpu.VMEM((arrays["adapter"].shape[1], many), BF16),
            pltpu.VMEM(arrays["out_w"].shape, F32),
            pltpu.VMEM((2 * HEAD, 2 * HEAD), F32),
            pltpu.VMEM((outer - 1, 2 * HEAD, 2 * HEAD), F32),
            pltpu.VMEM((2 * HEAD, 2 * HEAD), F32),
            pltpu.VMEM((q_wide, width), BF16),
            pltpu.VMEM((layer, pieces, row_part, width), BF16),
        ]
        scratch += [pltpu.VMEM(a.shape, a.dtype) for a in arrays.values()]
        copies = Gather.COPIES + outer - 1 + 10 + pieces * (layer - 1)
        args = (*scalars, v, first_rows, *arrays.values(), *lefts, *rights)
        return self.call(
            kernel, outs, args, copies, scratch + job_scratch,
            local=2 + inputs + jobs * (layer + 1), vmem=62, time=8, specs=[SCALARS] * 3,
        )

    def swap_sides(self, arrays, chunk):
        many = len(arrays)
        rows, columns = arrays[0].shape
        half = columns // 2
        chunks = half // chunk

        def kernel(*refs):
            ins, blocks = refs[:many], refs[many : many + chunks]
            sends, recvs, local = refs[many + chunks :]
            post = Post(sends, recvs)
            device = self.flip(4)[0]
            self.meet([device])
            side = lax.axis_index("dp") % 2
            own = []
            for c in range(chunks):
                for k, v in enumerate(ins):

                    def part(of):
                        start = pl.multiple_of(of * half + c * chunk, 128)
                        return v.at[:, pl.ds(start, chunk)]

                    out = blocks[c].at[side, :, pl.ds(k * chunk, chunk)]
                    post.send(part(1 - side), out, device)
                    own.append(pltpu.make_async_copy(part(side), out, local.at[len(own)]))
                    own[-1].start()
            post.finish()
            for copy in own:
                copy.wait()

        outs = [((2, rows, many * chunk), arrays[0].dtype, pl.ANY)] * chunks
        total = many * chunks
        return self.call(kernel, outs, tuple(arrays), total, local=total, time=36)

    def scatter_job(self, post, refs, columns, turned, local, loads):
        lefts, rights, out, work = refs
        both, got, xs, ys, weights, blocks = work
        layer, many, step = self.layer, len(lefts), 16
        rows, width = out.shape
        half, wide = rows // 2, min(width, 512)
        devs = [self.flip(i) for i in range(8)]
        dev_c, dev_y, dev_x = devs[1][0], devs[2][0], devs[4][0]
        used = 0

        def load(src, dst):
            nonlocal used
            copy = pltpu.make_async_copy(src, dst, local.at[loads + used])
            copy.start()
            used += 1
            return copy

        weight_loads = []
        for k, (v, w) in enumerate(zip(rights, weights)):
            part = v if turned else v.at[:, pl.ds(columns[k], w.shape[1])]
            weight_loads.append(load(part, w))
        block_loads = {}
        for i in range(layer // 2 - 1, -1, -1):
            at = pl.ds(pl.multiple_of(devs[2 * i][1] // 2 * 2 * rows, 2 * rows), 2 * rows)
            for k, v in enumerate(lefts):
                block_loads[i, k] = load(v.at[:, at] if turned else v.at[at], blocks[k].at[i])
        yield
        for copy in weight_loads:
            copy.wait()

        core = devs[0][1] % 2
        here = pl.ds(pl.multiple_of(core * rows, rows), rows)
        there = pl.ds(pl.multiple_of((1 - core) * rows, rows), rows)
        mine = [both.at[i, here] for i in range(layer // 2)]

        def product(i, dst):
            for k in range(many):
                block_loads[i, k].wait()

            @pl.loop(0, width // wide)
            def _(j):
                at = pl.ds(pl.multiple_of(j * wide, wide), wide)
                total = None
                for k in range(many):
                    if turned:
                        term = dot_tn(blocks[k][i], weights[k][:, at])
                    else:
                        term = dot_nt(blocks[k][i], weights[k][at, :])
                    total = term if total is None else total + term
                dst[:, at] = total.astype(BF16)

        def add(dst, one, two):
            @pl.loop(0, dst.shape[0] // step)
            def _(j):
                at = pl.ds(pl.multiple_of(j * step, step), step)
                total = one[at, :].astype(F32) + two[at, :].astype(F32)
                dst[at, :] = total.astype(dst.dtype)

        a, b = pl.ds(0, half), pl.ds(half, half)

        def begin(i):
            product(i, both.at[i])
            return post.send(both.at[i, there], got.at[i], dev_c)

        def end(i, arrive):
            post.arrived(arrive)
            add(mine[i], mine[i], got.at[i])

        end(3, begin(3))
        x1 = post.send(mine[3].at[a], xs.at[0], dev_x)
        y1 = post.send(mine[3].at[b], ys.at[0], dev_y)
        yield
        two = begin(2)
        one = begin(1)
        end(2, two)
        x2 = post.send(mine[2].at[a], xs.at[1], dev_x)
        yield
        end(1, one)
        y2 = post.send(mine[1].at[b], ys.at[1], dev_y)
        zero = begin(0)
        yield
        post.arrived(x1)
        add(mine[1].at[a], mine[1].at[a], xs.at[0])
        y3 = post.send(mine[1].at[a], ys.at[2], dev_y)
        post.arrived(y1)
        add(mine[2].at[b], mine[2].at[b], ys.at[0])
        x3 = post.send(mine[2].at[b], xs.at[2], dev_x)
        yield
        end(0, zero)
        yield
        low, high = out.at[a], out.at[b]
        post.arrived(x2)
        add(low, mine[0].at[a], xs.at[1])
        post.arrived(y2)
        add(high, mine[0].at[b], ys.at[1])
        yield
        post.arrived(y3)
        add(low, low, ys.at[2])
        post.arrived(x3)
        add(high, high, xs.at[2])
        yield

    def job_scratch(self, job):
        lefts, rights, columns = job
        turned = columns is None
        rows = lefts[0].shape[1 if turned else 0] // self.layer
        width = rights[0].shape[1 if turned else 0]
        pairs = self.layer // 2
        work = [pltpu.VMEM((pairs, 2 * rows, width), BF16), pltpu.VMEM((pairs, rows, width), BF16)]
        work += [pltpu.VMEM((3, rows // 2, width), BF16)] * 2
        for v, w in zip(lefts, rights):
            work.append(pltpu.VMEM(w.shape if turned else (width, v.shape[1]), BF16))
        for v in lefts:
            block = (v.shape[0], 2 * rows) if turned else (2 * rows, v.shape[1])
            work.append(pltpu.VMEM((pairs,) + block, BF16))
        return work

    def scatter_products(self, *jobs, sums=(), swap=()):
        layer = self.layer
        outs, scratch, sizes, shapes, args = [], [], [], [], []
        local = 0
        for lefts, rights, columns in jobs:
            turned = columns is None
            many = len(lefts)
            rows = lefts[0].shape[1 if turned else 0] // layer
            width = rights[0].shape[1 if turned else 0]
            outs.append(((rows, width), F32, pltpu.VMEM))
            scratch += self.job_scratch((lefts, rights, columns))
            sizes.append(many)
            shapes.append(local)
            local += many * (layer + 1)
            args += [*lefts, *rights]
        copies = 10 * len(jobs)
        if sums:
            all_sum, part = sums
            stages = len(self.outer_steps())
            size, lanes = all_sum.shape[0] + part.shape[0], part.shape[1]
            outs += [
                ((all_sum.shape[0] + 24, layer * lanes), BF16, pltpu.VMEM),
                ((layer, part.shape[0] - 16, lanes), BF16, pltpu.VMEM),
            ]
            scratch += [
                pltpu.VMEM((layer, all_sum.shape[0], lanes), F32),
                pltpu.VMEM((stages, size, lanes), F32),
                pltpu.VMEM((size, lanes), F32),
                pltpu.VMEM((size + 8, lanes), BF16),
            ]
            copies += stages + 3 * (layer - 1)
            local += 2

        for v in swap:
            outs.append(((v.shape[0], v.shape[1] // 2), v.dtype, pl.ANY))
            copies += 1

        def kernel(*refs):
            refs = list(refs)

            def take(n):
                got = refs[:n]
                del refs[:n]
                return got

            given = [(take(n), take(n)) for n in sizes]
            given_sums = take(len(sums))
            given_swap = take(len(swap))
            made = take(len(jobs))
            made_sums = take(2 if sums else 0)
            made_swap = take(len(swap))
            sends, recvs, local_sems = take(3)
            post = Post(sends, recvs)
            runs = []
            for (lefts, rights), out, n, first, job in zip(given, made, sizes, shapes, jobs):
                work = take(4) + [take(n), take(n)]
                runs.append(
                    self.scatter_job(
                        post, (lefts, rights, out, work), job[2], job[2] is None, local_sems, first
                    )
                )
                next(runs[-1])
            if sums:
                self.meet(
                    [self.flip(r)[0] for r in range(1, layer)] + self.outer_partners()
                )
                runs.append(
                    self.sum_steps(post, given_sums, made_sums, refs, local_sems, local - 2)
                )
                next(runs[-1])
            else:
                self.meet([self.flip(i)[0] for i in (1, 2, 4)])
            order = (0, 0, 0, 1, 0, 1, 0, 0, 1, 0, 1) if sums else (0,) * 7
            for n, run in enumerate(order):
                next(runs[run], None)
                if n == 3:
                    for v, out in zip(given_swap, made_swap):
                        third = out.shape[1]
                        start = pl.multiple_of((1 - lax.axis_index("dp") % 2) * third, third)
                        post.send(v.at[:, pl.ds(start, third)], out, self.flip(4)[0])
            for run in runs:
                for _ in run:
                    pass
            post.finish()

        return self.call(
            kernel, outs, (*args, *sums, *swap), copies, scratch, local=local, vmem=60,
            time=4 * len(jobs),
        )

    def outer_steps(self):
        steps = []
        while 1 << len(steps) < self.outer:
            steps.append(2 << len(steps))
        return steps

    def outer_partners(self):
        dp = lax.axis_index("dp")
        return [{"dp": dp + step - 2 * step * ((dp // step) % 2)} for step in self.outer_steps()]

    def sum_steps(self, post, given, outs, scratch, local, used):
        all_sum, part = given
        columns, others = outs
        pieces, got, mine, rounded = scratch
        rank = self.flip(0)[1]
        share, lanes = pieces.shape[1], pieces.shape[2]
        split = share + 24

        def columns_of(r):
            return pl.ds(pl.multiple_of(r * lanes, lanes), lanes)

        copies = [
            pltpu.make_async_copy(all_sum.at[:, columns_of(rank)], pieces.at[rank], local.at[used]),
            pltpu.make_async_copy(
                part, mine.at[pl.ds(share, part.shape[0])], local.at[used + 1]
            ),
        ]
        for copy in copies:
            copy.start()
        ids = []
        for r in range(1, self.layer):
            device, target = self.flip(r)
            ids.append(post.send(all_sum.at[:, columns_of(target)], pieces.at[rank], device))
        yield
        for copy in copies:
            copy.wait()
        for i in ids:
            post.arrived(i)
        total = pieces[0]
        for r in range(1, self.layer):
            total = total + pieces[r]
        mine[:share] = total
        for n, device in enumerate(self.outer_partners()):
            i = post.send(mine, got.at[n], device)
            yield
            post.arrived(i)
            post.copies[i].wait_send()
            post.sent.add(i)
            mine[...] = mine[...] + got[n]
        rounded[: split - 8] = mine[: split - 8].astype(BF16)
        rounded[split - 8 : split] = jnp.zeros((8, lanes), BF16)
        rounded[split:] = mine[split - 8 :].astype(BF16)
        for r in range(1, self.layer):
            device = self.flip(r)[0]
            post.send(rounded.at[pl.ds(0, split)], columns.at[:, columns_of(rank)], device)
            post.send(rounded.at[pl.ds(split, others.shape[1])], others.at[rank], device)
        columns[:, columns_of(rank)] = rounded[:split]
        others[rank] = rounded[split:]
        yield

    def exchange_copies(self, v, out, sends, recvs, local, held):
        rank = self.flip(0)[1]

        def run(test, action):
            if held is None:
                action()
            else:
                pl.when(test)(action)

        own = pltpu.make_async_copy(v.at[rank], out.at[rank], local.at[0])
        copies = []
        for i, r in enumerate((6, 7, 4, 5, 2, 3, 1)):
            device, target = self.flip(r)
            copy = pltpu.make_async_remote_copy(
                src_ref=v.at[target],
                dst_ref=out.at[rank],
                send_sem=sends.at[i],
                recv_sem=recvs.at[i],
                device_id=device,
                device_id_type=MESH,
            )
            copies.append((target, copy))

        def start():
            own.start()
            for target, copy in copies:
                run(held and held(rank, target), copy.start)

        def wait():
            for target, copy in copies:
                run(held and held(target, rank), copy.wait_recv)
                run(held and held(rank, target), copy.wait_send)
            own.wait()

        return start, wait

    def exchange(self, v):
        def kernel(v, out, sends, recvs, local):
            self.meet([self.flip(r)[0] for r in range(1, self.layer)])
            start, wait = self.exchange_copies(v, out, sends, recvs, local, None)
            start()
            wait()

        return self.call(kernel, [(v.shape, v.dtype, pl.ANY)], (v,), 7, time=9)[0]

    def between(self, v, gathered, row_part, held):
        n, layer = self.outer, self.layer
        per_head, width = n, gathered.shape[1]
        pieces = max(1, per_head // layer)
        each = gathered.shape[0] // n

        def kernel(v, gathered, out, got, sends, recvs, local):
            dp = lax.axis_index("dp")
            rank = self.flip(0)[1]
            devices = [{"dp": (dp + 2 * d) % self.dp} for d in range(1, n)]
            self.meet(devices + [self.flip(r)[0] for r in range(1, layer)])
            post = Post(sends, recvs)
            for d, device in enumerate(devices):
                post.send(v, out.at[d], device)

            def rows_for(target, i):
                place = target * per_head // layer + i
                start = pl.multiple_of(place * each + each - row_part, 16)
                return gathered.at[pl.ds(start, row_part)]

            def run(test, action):
                if held is None:
                    action()
                else:
                    pl.when(test)(action)

            own = []
            for i in range(pieces):
                own.append(
                    pltpu.make_async_copy(rows_for(rank, i), got.at[rank, i], local.at[i])
                )
                own[-1].start()
            moves = []
            for r in (6, 7, 4, 5, 2, 3, 1):
                device, target = self.flip(r)
                for i in range(pieces):
                    at = n - 1 + len(moves)
                    copy = pltpu.make_async_remote_copy(
                        src_ref=rows_for(target, i),
                        dst_ref=got.at[rank, i],
                        send_sem=sends.at[at],
                        recv_sem=recvs.at[at],
                        device_id=device,
                        device_id_type=MESH,
                    )
                    run(held and held(rank, target), copy.start)
                    moves.append((target, copy))
            post.finish()
            for target, copy in moves:
                run(held and held(target, rank), copy.wait_recv)
                run(held and held(rank, target), copy.wait_send)
            for copy in own:
                copy.wait()

        outs = [
            ((n - 1,) + v.shape, v.dtype, pl.ANY),
            ((layer, pieces, row_part, width), gathered.dtype, pl.ANY),
        ]
        copies = n - 1 + (layer - 1) * pieces
        return self.call(kernel, outs, (v, gathered), copies, local=pieces, time=5)


    def groups(self):
        return [[2 * o + b for o in range(self.outer)] for b in range(2)]

    def gather_outer(self, v):
        return lax.all_gather(v, "dp", axis_index_groups=self.groups(), tiled=True)

    def scatter_outer(self, v):
        return lax.psum_scatter(v, "dp", axis_index_groups=self.groups(), tiled=True)

    def other_side(self, v):
        return lax.ppermute(v, "dp", [(i, i ^ 1) for i in range(self.dp)])


def stable_maps(logits):
    plus = jnp.exp(logits - jnp.max(logits, 0, keepdims=True))
    minus = jnp.exp(jnp.min(logits, 0, keepdims=True) - logits)
    plus = plus * (1.0 / jnp.sum(plus, 0, keepdims=True))
    minus = minus * (1.0 / jnp.sum(minus, 0, keepdims=True))
    return plus, minus


def maps_back(grad, plus, minus):
    up, down = grad[:HEAD], grad[HEAD:]
    out = plus * (up - jnp.sum(plus * up, 0, keepdims=True))
    return (out - minus * (down - jnp.sum(minus * down, 0, keepdims=True))).astype(BF16)


def heads_wide(v, group):
    return jnp.concatenate([v[h * HEAD : (h + 1) * HEAD] for h in range(group)], 1)


def first_window(lanes):
    return lax.broadcasted_iota(jnp.int32, (1, lanes), 1) % TILE < WINDOW


def window_scores(keys, queries):
    lanes = queries.shape[1]
    scores = dot_tn(keys, queries) * (1.0 / math.sqrt(HEAD))
    j = lax.broadcasted_iota(jnp.int32, (TILE, lanes), 0)
    t = lax.broadcasted_iota(jnp.int32, (TILE, lanes), 1) % TILE
    seen = (j <= t) & (j // WINDOW == t // WINDOW)
    masked = jnp.where(seen, scores, FLOOR_SCORE)
    top = jnp.max(masked, 0, keepdims=True)
    return jnp.where(seen, jnp.exp(masked - top), 0.0), top


def key_kernel(keys, values, map_t, mask, feats, summary):
    summary[...] = jnp.zeros_like(summary)
    step = 2 * TILE

    @pl.loop(0, keys.shape[1] // step)
    def _(i):
        at = pl.ds(pl.multiple_of(i * step, step), step)
        plus, minus = stable_maps(dot(map_t[...], keys[:, at]))
        feat = jnp.concatenate([plus, minus], 0).astype(BF16)
        feats[:, at] = feat
        kept = (feat.astype(F32) * mask[:, at]).astype(BF16)
        summary[...] += dot_nt(kept, values[:, at])


def forward_kernel(
    keep, queries, keys, values, feats, map_t, carry, attended, ratios, denoms, states, state
):
    i = pl.program_id(0)
    group = map_t.shape[0]

    @pl.when(i == 0)
    def _():
        state[...] = carry[...]

    feat_k, vals = feats[...], values[...]
    one = state[...] * keep[2 * i]
    two = (one + dot_nt(feat_k[:, :WINDOW], vals[:, :WINDOW])) * keep[2 * i + 1]
    state[...] = two + dot_nt(feat_k[:, WINDOW:], vals[:, WINDOW:])
    one, two = one.astype(BF16), two.astype(BF16)
    states[0], states[1] = one, two
    rows = queries[...]
    wide = heads_wide(rows, group)
    logits = jnp.concatenate(
        [dot(map_t[h], rows[h * HEAD : (h + 1) * HEAD]) for h in range(group)], 1
    )
    feat_q = jnp.concatenate(stable_maps(logits), 0).astype(BF16)
    expo, top = window_scores(keys[...], wide)
    shrink = jnp.exp(-top)
    window = dot(vals[:HEAD], expo.astype(BF16))
    linear = jnp.where(first_window(wide.shape[1]), dot_tn(one, feat_q), dot_tn(two, feat_q))
    numer = window + shrink * linear[:HEAD]
    denom = jnp.sum(expo, 0, keepdims=True) + shrink * linear[HEAD : HEAD + 1]
    ratio = numer * (1.0 / denom)
    denoms[0] = denom
    for h in range(group):
        part = ratio[:, h * TILE : (h + 1) * TILE]
        ratios[h * HEAD : (h + 1) * HEAD] = part
        attended[h * HEAD : (h + 1) * HEAD] = part.astype(BF16)


def query_tile(tile, first, on, grad_t, outs):
    grads, window_kv, grad_states, part, summary = outs
    map_t, maps, states = on["map_t"], on["maps"], on["states"]
    group = map_t.shape[0]
    at = pl.ds(pl.multiple_of(tile * TILE, TILE), TILE)
    rows, key_rows, vals = on["queries"][:, at], on["keys"][:, at], on["values"][:, at]
    wide = heads_wide(rows, group)
    lanes = wide.shape[1]
    grad, ratio = heads_wide(grad_t[:, at], group), heads_wide(on["ratios"][:, at], group)
    inverse = 1.0 / on["denoms"][tile]
    grad_num = (grad * inverse).astype(BF16)
    grad_den = -jnp.sum(grad * ratio, 0, keepdims=True) * inverse
    expo, top = window_scores(key_rows, wide)
    shrink = jnp.exp(-top)
    grad_scores = (expo * (dot_tn(vals[:HEAD], grad_num) + grad_den)).astype(BF16)
    scale = 1.0 / math.sqrt(HEAD)
    window_kv[:HEAD, at] = dot_nt(wide, grad_scores) * scale
    window_kv[HEAD:, at] = dot_nt(grad_num, expo.astype(BF16))
    logits = jnp.concatenate(
        [dot(map_t[h], rows[h * HEAD : (h + 1) * HEAD]) for h in range(group)], 1
    )
    plus, minus = stable_maps(logits)
    feat_q = jnp.concatenate([plus, minus], 0).astype(BF16)
    both = jnp.concatenate(
        [
            grad_num.astype(F32) * shrink,
            grad_den * shrink,
            jnp.zeros((2 * HEAD - HEAD - 1, lanes), F32),
        ],
        0,
    )
    early = first_window(lanes)
    state_one = dot_nt(feat_q, jnp.where(early, both, 0.0).astype(BF16))
    state_two = dot_nt(feat_q, jnp.where(early, 0.0, both).astype(BF16))
    grad_states[2 * tile], grad_states[2 * tile + 1] = state_one, state_two
    summary[...] += state_one * first[2 * tile] + state_two * first[2 * tile + 1]
    both = both.astype(BF16)
    grad_feat = jnp.where(early, dot(states[2 * tile], both), dot(states[2 * tile + 1], both))
    grad_logits = maps_back(grad_feat, plus, minus)
    window = dot(key_rows, grad_scores) * scale
    grad_maps = []
    for h in range(group):
        head, cut = slice(h * HEAD, (h + 1) * HEAD), slice(h * TILE, (h + 1) * TILE)
        grads[head, at] = (window[:, cut] + dot(maps[h], grad_logits[:, cut])).astype(BF16)
        grad_maps.append(dot_nt(rows[head], grad_logits[:, cut]))
    part[16 : 16 + HEAD] += jnp.concatenate(grad_maps, 1)


def key_tile(tile, keep, on, window, grad_states, state, grads, part):
    at = pl.ds(pl.multiple_of(tile * TILE, TILE), TILE)
    two = state[...]
    one = (two + grad_states[2 * tile + 1]) * keep[2 * tile + 1]
    state[...] = (one + grad_states[2 * tile]) * keep[2 * tile]
    one, two = one.astype(BF16), two.astype(BF16)
    key_rows, vals, feat = on["keys"][:, at], on["values"][:, at], on["feats"][:, at]
    early = first_window(TILE)
    grad_feat = jnp.where(early, dot(one, vals), dot(two, vals))
    linear = jnp.where(early, dot_tn(one, feat), dot_tn(two, feat))[:HEAD]
    plus, minus = stable_maps(dot(on["map_k_t"][...], key_rows))
    grad_logits = maps_back(grad_feat, plus, minus)
    start = grads.shape[0] - on["seconds"].shape[0] - 2 * HEAD
    grads[start : start + HEAD, at] = (
        window[:HEAD, at] + dot(on["map_k"][...], grad_logits)
    ).astype(BF16)
    grads[start + HEAD : start + 2 * HEAD, at] = (window[HEAD:, at] + linear).astype(BF16)
    part[16 + HEAD : 16 + 2 * HEAD, :HEAD] += dot_nt(key_rows, grad_logits)


def local_call(kernel, outs, args, time=10, vmem=32, **kwargs):
    return pl.pallas_call(
        kernel,
        out_shape=[jax.ShapeDtypeStruct(s, t) for s, t in outs],
        cost_estimate=takes(time),
        compiler_params=pltpu.CompilerParams(vmem_limit_bytes=vmem * 2**20),
        **kwargs,
    )(*args)


def hidden_units(gate, upper, grad_hidden):
    sigmoid = 1.0 / (1.0 + jnp.exp(-gate))
    silu = gate * sigmoid
    grad_gate = grad_hidden * upper * sigmoid * (1.0 + gate * (1.0 - sigmoid))
    return (silu * upper).astype(BF16), grad_gate.astype(BF16), (grad_hidden * silu).astype(BF16)


def feedforward_kernel(
    rows, grads, gate_w, up_w, down_w, hidden, grad_gate, grad_up, grad_w, both_t, hidden_t
):
    step = 512
    tile = gate_w.shape[1]

    @pl.loop(0, rows.shape[0] // step)
    def _(i):
        at = pl.ds(pl.multiple_of(i * step, step), step)
        gate = dot(rows[at, :], gate_w[...])
        upper = dot(rows[at, :], up_w[...])
        grad_hidden = dot(grads[at, :], down_w[...])
        inner, one, two = hidden_units(gate, upper, grad_hidden)
        hidden[at, :], grad_gate[at, :], grad_up[at, :] = inner, one, two
        hidden_t[:, at] = inner.T
        both_t[:tile, at] = one.T
        both_t[tile:, at] = two.T

    wide = grad_w.shape[-1]

    @pl.loop(0, grad_w.shape[0])
    def _(z):
        at = pl.ds(pl.multiple_of(z * wide, wide), wide)
        both = dot(both_t[...], rows[:, at], BF16)
        grad_w[z, 0], grad_w[z, 1] = both[:tile], both[tile:]
        grad_w[z, 2] = dot(hidden_t[...], grads[:, at], BF16)


def feedforward(rows, grads, weights, chunk, outer):
    many, width = rows.shape
    tile = 256
    tiles, wide = chunk // tile, width // outer
    held = pl.BlockSpec((many, width), lambda j: (0, 0), pipeline_mode=pl.Buffered(1))

    def part(k):
        return pl.BlockSpec((width, tile), lambda j: (0, k * tiles + j))

    column = pl.BlockSpec((many, tile), lambda j: (0, j))
    return local_call(
        feedforward_kernel,
        [((many, chunk), BF16)] * 3 + [((outer, 3, chunk, wide), BF16)],
        (rows, grads, weights, weights, weights),
        time=35,
        vmem=60,
        grid=(tiles,),
        in_specs=[held, held, part(0), part(1), part(2)],
        out_specs=[column] * 3
        + [pl.BlockSpec((outer, 3, tile, wide), lambda j: (0, 0, j, 0))],
        scratch_shapes=[pltpu.VMEM((2 * tile, many), BF16), pltpu.VMEM((tile, many), BF16)],
    )


def whole(shape):
    return pl.BlockSpec(shape, lambda i: (0,) * len(shape))


SCALARS = pl.BlockSpec(memory_space=pltpu.SMEM)


def key_features(keys, values, map_t, mask):
    rows = keys.shape[1]
    return local_call(
        key_kernel,
        [((2 * HEAD, rows), BF16), ((2 * HEAD, 2 * HEAD), F32)],
        (keys, values, map_t, mask),
    )


def attention_forward(keep, queries, keys, values, feats, map_t, carry):
    group, rows = map_t.shape[0], keys.shape[1]
    tiles = rows // TILE
    cols = lambda n: pl.BlockSpec((n, TILE), lambda i: (0, i))
    return local_call(
        forward_kernel,
        [
            ((group * HEAD, rows), BF16),
            ((group * HEAD, rows), F32),
            ((tiles, 1, group * TILE), F32),
            ((2 * tiles, 2 * HEAD, 2 * HEAD), BF16),
        ],
        (keep, queries, keys, values, feats, map_t, carry),
        grid=(tiles,),
        in_specs=[
            SCALARS, cols(group * HEAD), cols(HEAD), cols(2 * HEAD), cols(2 * HEAD),
            whole(map_t.shape), whole(carry.shape),
        ],
        out_specs=[
            cols(group * HEAD),
            cols(group * HEAD),
            pl.BlockSpec((1, 1, group * TILE), lambda i: (i, 0, 0)),
            pl.BlockSpec((2, 2 * HEAD, 2 * HEAD), lambda i: (i, 0, 0)),
        ],
        scratch_shapes=[pltpu.VMEM((2 * HEAD, 2 * HEAD), F32)],
    )


def shards(
    links,
    hidden_input,
    output_gradient,
    lengths,
    attention_norm_gain,
    query_weight,
    key_weight,
    value_weight,
    output_weight,
    query_adapter_first,
    query_adapter_second,
    key_adapter_first,
    key_adapter_second,
    value_adapter_first,
    value_adapter_second,
    output_adapter_first,
    output_adapter_second,
    query_feature_weight,
    key_feature_weight,
    feedforward_norm_gain,
    gate_weight,
    up_weight,
    down_weight,
):
    links.coords()
    place, side, rank = links.place, links.side, links.rank
    outer, layer = links.outer, links.layer
    rows, width = hidden_input.shape
    layer_rows = rows * layer
    windows = layer_rows // WINDOW
    kv_heads = key_feature_weight.shape[0]
    group = query_feature_weight.shape[0] // kv_heads
    q_wide = group * HEAD

    spans = (lengths + WINDOW - 1) // WINDOW
    seq_ends = jnp.cumsum(spans)
    seq_begins = seq_ends - spans

    def sequence_of(span):
        return jnp.sum((span[..., None] >= seq_ends).astype(jnp.int32), -1)

    local = jnp.arange(windows, dtype=jnp.int32)
    span_seq = sequence_of(place * windows + local)
    seq_first, seq_last = span_seq[0], span_seq[-1]
    same_next = (span_seq[1:] == span_seq[:-1]).astype(F32)
    keep = jnp.concatenate([jnp.ones((1,), F32), same_next])
    first_mask = (span_seq == seq_first).astype(F32)
    last_mask = (span_seq == seq_last).astype(F32)
    token_ids = (place * layer + rank) * rows + jnp.arange(rows, dtype=jnp.int32)
    token_seq = sequence_of(token_ids // WINDOW)
    onehot = (token_seq[:, None] == jnp.arange(lengths.shape[0], dtype=jnp.int32)).astype(jnp.int32)
    offset = jnp.sum(onehot * seq_begins * WINDOW, 1)
    limit = jnp.sum(onehot * lengths, 1)
    valid = (token_ids - offset < limit).astype(F32)[:, None]

    def own(v, axis, size):
        return lax.dynamic_slice_in_dim(v, rank * size, size, axis)

    inputs_full = hidden_input.astype(F32)
    gain_one = attention_norm_gain.astype(F32)
    gain_two = feedforward_norm_gain.astype(F32)
    normed_one, inv_one, first_rows = rms_forward(inputs_full, gain_one)

    row_part = query_weight.shape[0]
    rank_size = query_adapter_first.shape[1]
    kv_end = q_wide + 2 * HEAD
    per_head = outer
    many = max(1, per_head // layer)
    parts = jnp.concatenate(
        [w.reshape(row_part, layer, -1) for w in (query_weight, key_weight, value_weight)], -1
    )
    parts = links.exchange(parts.transpose(1, 0, 2))
    lanes = 128
    packs = width // lanes
    deep = layer * row_part // packs
    packed = parts.reshape(packs, deep, kv_end // lanes, lanes).transpose(2, 1, 0, 3)
    packed = packed.reshape(deep * kv_end // lanes, width)
    packed = jnp.pad(packed, ((0, -packed.shape[0] % 16), (0, 0)))
    gathered = links.gather_outer(jnp.concatenate([packed, output_weight], 0))
    gathered_rows = gathered.reshape(outer, -1, width)
    head_weight = gathered_rows[:, : deep * kv_end // lanes]
    head_weight = head_weight.reshape(outer, kv_end // lanes, deep, packs, lanes)
    head_weight = head_weight.transpose(0, 3, 2, 1, 4).reshape(width, kv_end)

    hidden_part = gate_weight.shape[1] // 2
    chunk = hidden_part // CHUNKS
    third = gate_weight.shape[0]

    halves = links.swap_sides(
        (gate_weight, up_weight, after(down_weight.T, parts)), chunk
    )
    blocks = [links.gather_outer(v.reshape(2 * third, 3 * chunk)) for v in halves]
    first_all = links.gather_rows(after(first_rows, *halves))

    def held(source, head):
        return (source // per_head) == head % (layer // per_head)

    adapters = jnp.concatenate([query_adapter_first, key_adapter_first, value_adapter_first], 1)
    adapters = jnp.pad(adapters, ((0, 0), (0, -3 * rank_size % 16)))
    qkv_weight = jnp.concatenate([head_weight, adapters], 1)
    second_q = own(query_adapter_second, 1, q_wide)
    second_k = own(key_adapter_second, 1, HEAD)
    second_v = own(value_adapter_second, 1, HEAD)
    oa_own = own(output_adapter_first, 0, q_wide)

    projected = dot_tt(qkv_weight, first_all)
    low_rank = projected[kv_end:].astype(BF16)
    low_q, low_k, low_v = (low_rank[i * rank_size : (i + 1) * rank_size] for i in range(3))
    queries = (projected[:q_wide] + dot_tn(second_q, low_q)).astype(BF16)
    keys = (projected[q_wide : q_wide + HEAD] + dot_tn(second_k, low_k)).astype(BF16)
    values = (projected[q_wide + HEAD : kv_end] + dot_tn(second_v, low_v)).astype(BF16)
    values = jnp.concatenate(
        [values, jnp.ones((1, layer_rows), BF16), jnp.zeros((HEAD - 1, layer_rows), BF16)], 0
    )
    maps_q = lax.dynamic_slice_in_dim(query_feature_weight, rank * group, group, 0)
    map_k = lax.dynamic_slice_in_dim(key_feature_weight, rank, 1, 0)[0]
    maps_q_turned, map_k_turned = maps_q.transpose(0, 2, 1), map_k.T

    def carry_forward(summary):
        got, out_own = links.between(
            summary, gathered, row_part, held if per_head < layer else None
        )
        total = jnp.zeros_like(summary)
        for d in range(1, outer):
            joined = sequence_of((place - d + 1) * windows - 1) == seq_first
            total = total + jnp.where(joined & (place >= d), got[d - 1], 0.0)
        return total, out_own

    last_tokens = jnp.repeat(last_mask, WINDOW)[None]
    feats, summary = key_features(keys, values, map_k_turned, last_tokens)
    carried, out_parts = carry_forward(summary)
    if per_head >= layer:
        out_own = out_parts.transpose(1, 0, 2, 3).reshape(-1, width)
    else:
        start = (rank % (layer // per_head)) * per_head
        out_own = lax.dynamic_slice_in_dim(out_parts, start, per_head, 0).reshape(-1, width)
    attended, ratios, denoms, states = attention_forward(
        keep, queries, keys, values, feats, maps_q_turned, carried
    )
    low_out = dot_tn(oa_own, attended, BF16)
    pad = 16 - rank_size
    out_both = jnp.concatenate([out_own, output_adapter_second, jnp.zeros((pad, width), BF16)], 0)
    attended_both = jnp.concatenate([attended, low_out, jnp.zeros((pad, layer_rows), BF16)], 0)
    resid = inputs_full + links.scatter_products(([attended_both], [out_both], None))[0]

    normed_two, inv_two, rows_two = rms_forward(resid, gain_two)
    rows_two = after(rows_two, blocks[0])
    grad_y = output_gradient.astype(F32) * valid
    hiddens, grads_two, block_sums = [], [], []
    for c in range(CHUNKS):
        if c == 0:
            two_all, grad_all, *made = links.gather_feedforward(
                rows_two, grad_y.astype(BF16), blocks[c], chunk
            )
        else:
            made = feedforward(two_all, grad_all, blocks[c], chunk, outer)
        hidden, grad_gate, grad_up, grad_block = made
        hiddens.append(hidden)
        grads_two += [grad_gate, grad_up]
        block_sums.append(links.scatter_outer(grad_block.reshape(outer * 3 * chunk, -1)))
    (grad_rows_two,) = links.scatter_products(
        (grads_two, [blocks[i // 2] for i in range(2 * CHUNKS)], [0, chunk] * CHUNKS)
    )

    grad_gain_two = jnp.sum(grad_rows_two * normed_two, 0)
    grad_resid = grad_y + rms_backward(grad_rows_two, normed_two, inv_two, gain_two)
    weight_t = qkv_weight.T
    seconds = jnp.zeros((adapters.shape[1], kv_end), BF16)
    seconds = seconds.at[:rank_size, :q_wide].set(second_q)
    seconds = seconds.at[rank_size : 2 * rank_size, q_wide : q_wide + HEAD].set(second_k)
    seconds = seconds.at[2 * rank_size : 3 * rank_size, q_wide + HEAD :].set(second_v)
    joined = [
        (sequence_of((place + d) * windows) == seq_last) & (place + d < outer)
        for d in range(outer - 1, 0, -1)
    ]
    grads_all, sums, all_sum, part, mlp_out = links.backward_rows(
        (first_mask, keep, jnp.stack(joined).astype(F32)),
        grad_resid.astype(BF16),
        first_all,
        {
            "out_w": out_both,
            "attended": attended_both,
            "adapter": jnp.pad(oa_own, ((0, 0), (0, pad))),
            "queries": queries,
            "keys": keys,
            "values": values,
            "map_t": maps_q_turned,
            "maps": maps_q,
            "map_k_t": map_k_turned,
            "map_k": map_k,
            "states": states,
            "ratios": ratios,
            "denoms": denoms,
            "feats": feats,
            "seconds": seconds,
            "low_all": low_rank,
            "weight_t": weight_t,
            "gains": jnp.pad(jnp.stack([gain_one, grad_gain_two]), ((0, 6), (0, 0))),
        },
        held if per_head < layer else None,
        row_part,
        (hiddens, blocks, [2 * chunk] * CHUNKS),
    )
    sums = after(sums, block_sums[0])
    grads_all = after(grads_all, sums)
    sums = links.scatter_outer(sums.reshape(-1, sums.shape[-1]))
    early = block_sums[:1] if third % 128 == 0 else []
    grad_rows_one, columns, others, *theirs = links.scatter_products(
        ([grads_all], [weight_t], None), sums=(all_sum, part), swap=tuple(early)
    )
    small_done = grad_rows_one
    wide = width // outer
    grad_out_sh = sums[kv_end:].reshape(outer, row_part, wide).transpose(1, 0, 2)
    grad_out_sh = grad_out_sh.reshape(row_part, width).astype(F32)
    sums = after(sums[:kv_end].T, grad_rows_one)
    got = links.exchange(sums.reshape(layer, row_part, kv_end))
    columns, others, got = lax.optimization_barrier((columns, others, got))
    exchanged = got
    got, columns, others = got.astype(F32), columns.astype(F32), others.astype(F32)
    grad_query_sh = got[:, :, :q_wide].transpose(1, 0, 2).reshape(row_part, -1)
    grad_key_sh = got[:, :, q_wide : q_wide + HEAD].transpose(1, 0, 2).reshape(row_part, -1)
    grad_value_sh = got[:, :, q_wide + HEAD :].transpose(1, 0, 2).reshape(row_part, -1)

    block_out = (valid * (resid + mlp_out)).astype(BF16)
    in_grad = grad_resid + rms_backward(grad_rows_one, normed_one, inv_one, gain_one)

    grad_qa, grad_ka, grad_va = (
        columns[i * rank_size : (i + 1) * rank_size].T for i in range(3)
    )
    grad_ob, grad_gain_one, grad_gain_two = columns[24:32], columns[32], columns[33]
    grad_qb, grad_oa = columns[40:48], columns[48:56].T
    grad_map_q = others[:, :HEAD].reshape(layer, HEAD, group, HEAD).transpose(0, 2, 1, 3)
    grad_map_q = grad_map_q.reshape(-1, HEAD, HEAD)
    grad_map_k = others[:, HEAD : 2 * HEAD, :HEAD]
    grad_kb, grad_vb = (
        others[:, HEAD : HEAD + rank_size, 128 + i * HEAD : 128 + (i + 1) * HEAD]
        .transpose(1, 0, 2)
        .reshape(rank_size, -1)
        for i in range(2)
    )

    mine = [lax.dynamic_slice_in_dim(v, side * third, third, 1) for v in block_sums]
    for summed in block_sums[len(early) :]:
        summed = after(summed, small_done)
        far = links.other_side(lax.dynamic_slice_in_dim(summed, (1 - side) * third, third, 1))
        theirs.append(after(far, exchanged))

    def units(k):
        own, other = (
            jnp.concatenate([v[k * chunk : (k + 1) * chunk] for v in many], 0)
            for many in (mine, theirs)
        )
        return jnp.concatenate(
            [jnp.where(side == 0, own, other), jnp.where(side == 0, other, own)], 0
        )

    grad_gate_sh, grad_up_sh = units(0).T.astype(F32), units(1).T.astype(F32)
    grad_down_sh = units(2).astype(F32)
    return (
        block_out,
        in_grad,
        grad_gain_one,
        grad_query_sh,
        grad_key_sh,
        grad_value_sh,
        grad_out_sh,
        grad_qa,
        grad_qb,
        grad_ka,
        grad_kb,
        grad_va,
        grad_vb,
        grad_oa,
        grad_ob,
        grad_map_q,
        grad_map_k,
        grad_gain_two,
        grad_gate_sh,
        grad_up_sh,
        grad_down_sh,
    )


def solution(mesh):
    rows = P(("dp", "tensor"), None)
    gate = P("dp", "tensor")
    down = P("tensor", "dp")
    links = Links(mesh)
    return jax.shard_map(
        lambda *args: shards(links, *args),
        mesh=mesh,
        in_specs=(rows, rows, P(), P(), rows, rows, rows, rows)
        + (P(),) * 11
        + (gate, gate, down),
        out_specs=(rows, rows, P(), rows, rows, rows, rows)
        + (P(),) * 11
        + (gate, gate, down),
        check_vma=False,
    )
```

```python
import math

import jax
import jax.numpy as jnp
from jax import lax
from jax.experimental import pallas as pl
from jax.experimental.pallas import tpu as pltpu
from jax.sharding import PartitionSpec as P

HEAD = 64
WINDOW = 64
EPSILON = 1e-05
FLOOR_SCORE = -1e30
HIGHEST = lax.Precision.HIGHEST
F32 = jnp.float32
BF16 = jnp.bfloat16
CHUNKS = 2
TILE = 2 * WINDOW


def dot(a, b, out=F32):
    return jnp.dot(a, b, preferred_element_type=F32).astype(out)


def dot_nt(a, b, out=F32):
    return lax.dot_general(a, b, (((1,), (1,)), ((), ())), preferred_element_type=F32).astype(out)


def dot_tt(a, b, out=F32):
    return lax.dot_general(a, b, (((0,), (1,)), ((), ())), preferred_element_type=F32).astype(out)


def dot_tn(a, b, out=F32):
    return lax.dot_general(a, b, (((0,), (0,)), ((), ())), preferred_element_type=F32).astype(out)


def after(v, *others):
    return lax.optimization_barrier((v, *others))[0]


def rms_forward(v, gain):
    inv_root = lax.rsqrt(jnp.mean(v * v, -1, keepdims=True) + EPSILON)
    normed = v * inv_root
    return normed, inv_root, (normed * gain).astype(BF16)


def rms_backward(grad_out, normed, inv_root, gain):
    scaled = grad_out * gain
    return inv_root * (scaled - normed * jnp.mean(scaled * normed, -1, keepdims=True))


MESH = pl.DeviceIdType.MESH


def takes(microseconds):
    return pl.CostEstimate(
        flops=int(microseconds * 1e9),
        bytes_accessed=int(microseconds * 3.3e6),
        transcendentals=0,
    )


class Post:
    def __init__(self, sends, recvs):
        self.sends, self.recvs, self.copies = sends, recvs, []
        self.received, self.sent = set(), set()

    def send(self, src, dst, device):
        i = len(self.copies)
        copy = pltpu.make_async_remote_copy(
            src_ref=src,
            dst_ref=dst,
            send_sem=self.sends.at[i],
            recv_sem=self.recvs.at[i],
            device_id=device,
            device_id_type=MESH,
        )
        copy.start()
        self.copies.append(copy)
        return i

    def arrived(self, i):
        if i not in self.received:
            self.received.add(i)
            self.copies[i].wait_recv()

    def finish(self):
        for i in range(len(self.copies)):
            self.arrived(i)
        for i, copy in enumerate(self.copies):
            if i not in self.sent:
                copy.wait_send()


class Gather:
    def __init__(self, links, post, v, out, local):
        self.post, self.v, self.out = post, v, out
        self.devices = [links.flip(i)[0] for i in range(8)]
        self.ranks = [links.flip(i)[1] for i in range(8)]
        self.rows = v.shape[0]
        self.half = self.rows // 2
        self.own = pltpu.make_async_copy(v, out.at[self.block(0)], local)
        self.ids, self.made = {}, []

    def block(self, offset):
        return pl.ds(pl.multiple_of(self.ranks[offset] * self.rows, self.rows), self.rows)

    def pair(self, offset):
        first = self.ranks[offset] // 2
        return pl.ds(pl.multiple_of(first * 2 * self.rows, 2 * self.rows), 2 * self.rows), first

    def have_pair(self, offset):
        self.have(offset)
        self.have(offset + 1)

    def send(self, offset, part, to):
        half = self.half
        start = pl.multiple_of(self.ranks[offset] * self.rows + part * half, half)
        there = self.out.at[pl.ds(start, half)]
        here = self.v.at[pl.ds(part * half, half)] if offset == 0 else there
        self.ids[offset ^ to, part] = self.post.send(here, there, self.devices[to])
        self.made.append(self.ids[offset ^ to, part])

    def start(self):
        self.own.start()
        self.send(0, 0, 4)
        self.send(0, 1, 2)
        self.send(0, 1, 4)
        self.send(0, 0, 2)
        self.send(0, 0, 1)
        self.send(0, 1, 1)

    def have(self, offset, *parts):
        if offset == 0:
            self.own.wait()
        for part in parts or ((0, 1) if offset else ()):
            self.post.arrived(self.ids[offset, part])

    def near(self):
        self.have(4, 0)
        self.send(4, 0, 2)
        self.send(4, 0, 1)
        self.have(2, 1)
        self.send(2, 1, 4)
        self.send(2, 1, 1)

    def middle(self):
        self.have(4, 1)
        self.send(4, 1, 1)
        self.have(2, 0)
        self.send(2, 0, 1)

    def last(self):
        self.have(6)
        self.send(6, 0, 1)
        self.send(6, 1, 1)

    COPIES = 14


class Links:
    def __init__(self, mesh):
        self.dp = mesh.shape["dp"]
        self.tensor = mesh.shape["tensor"]
        self.outer = self.dp // 2
        self.layer = 2 * self.tensor
        self.calls = 0

    def coords(self):
        dp = lax.axis_index("dp")
        tensor = lax.axis_index("tensor")
        self.place = dp // 2
        self.side = dp % 2
        self.rank = self.side * self.tensor + tensor


    def flip(self, offset):
        dp = lax.axis_index("dp")
        tensor = lax.axis_index("tensor")
        if offset & 4:
            dp = dp + 1 - 2 * (dp % 2)
        if offset & 2:
            tensor = tensor + 2 - 4 * ((tensor // 2) % 2)
        if offset & 1:
            tensor = tensor + 1 - 2 * (tensor % 2)
        return {"dp": dp, "tensor": tensor}, (dp % 2) * self.tensor + tensor

    def meet(self, devices):
        barrier = pltpu.get_barrier_semaphore()
        for device in devices:
            pl.semaphore_signal(barrier, inc=1, device_id=device, device_id_type=MESH)
        pl.semaphore_wait(barrier, len(devices))

    def call(self, kernel, outs, args, copies, scratch=(), local=0, vmem=48, time=40, specs=()):
        self.calls += 1
        sems = [pltpu.SemaphoreType.DMA((copies,)), pltpu.SemaphoreType.DMA((copies,))]
        sems += [pltpu.SemaphoreType.DMA((max(local, 1),))]
        return pl.pallas_call(
            kernel,
            out_shape=[jax.ShapeDtypeStruct(s, t) for s, t, _ in outs],
            in_specs=list(specs)
            + [pl.BlockSpec(memory_space=pl.ANY)] * (len(args) - len(specs)),
            out_specs=[pl.BlockSpec(memory_space=space) for _, _, space in outs],
            scratch_shapes=sems + list(scratch),
            cost_estimate=takes(time),
            compiler_params=pltpu.CompilerParams(
                collective_id=self.calls, has_side_effects=True, vmem_limit_bytes=vmem * 2**20
            ),
        )(*args)

    def gather_rows(self, v):
        def kernel(v, out, sends, recvs, local):
            post = Post(sends, recvs)
            self.meet([self.flip(i)[0] for i in (1, 2, 4)])
            gather = Gather(self, post, v, out, local.at[0])
            gather.start()
            gather.near()
            gather.middle()
            gather.last()
            gather.have(0)
            post.finish()

        outs = [((self.layer * v.shape[0], v.shape[1]), v.dtype, pl.ANY)]
        return self.call(kernel, outs, (v,), Gather.COPIES, time=38)[0]

    def gather_feedforward(self, v, grad, weights, chunk):
        layer, outer = self.layer, self.outer
        rows, width = v.shape
        many = layer * rows
        wide = width // outer

        def kernel(v, grad, w, all_rows, all_grads, hidden, grad_gate, grad_up, grad_w, *refs):
            sends, recvs, local, rows_in, grads_in, weight, both, both_t, hidden_t = refs
            post = Post(sends, recvs)
            load = pltpu.make_async_copy(w, weight, local.at[2])
            load.start()
            self.meet([self.flip(i)[0] for i in (1, 2, 4)])
            one = Gather(self, post, v, rows_in, local.at[0])
            two = Gather(self, post, grad, grads_in, local.at[1])
            one.start()
            load.wait()

            def forward(*offsets):
                for offset in offsets:
                    one.have_pair(offset)
                    at, _ = one.pair(offset)
                    both[at, :] = dot(rows_in[at, :], weight[:, : 2 * chunk])

            def backward(*offsets):
                for offset in offsets:
                    two.have_pair(offset)
                    at, _ = two.pair(offset)
                    grad_hidden = dot(grads_in[at, :], weight[:, 2 * chunk :])
                    inner, grad_g, grad_u = hidden_units(
                        both[at, :chunk], both[at, chunk:], grad_hidden
                    )
                    hidden[at, :], grad_gate[at, :], grad_up[at, :] = inner, grad_g, grad_u
                    hidden_t[:, at] = inner.T
                    both_t[:chunk, at] = grad_g.T
                    both_t[chunk:, at] = grad_u.T

            forward(0)
            one.near()
            one.middle()
            two.start()
            forward(4, 2)
            one.last()
            forward(6)
            out = [pltpu.make_async_copy(rows_in, all_rows, local.at[3])]
            out[0].start()
            backward(0)
            two.near()
            two.middle()
            backward(4, 2)
            two.last()
            backward(6)
            out.append(pltpu.make_async_copy(grads_in, all_grads, local.at[4]))
            out[1].start()

            @pl.loop(0, outer)
            def _(z):
                at = pl.ds(pl.multiple_of(z * wide, wide), wide)
                pair = dot(both_t[...], rows_in[:, at], BF16)
                grad_w[z, 0], grad_w[z, 1] = pair[:chunk], pair[chunk:]
                grad_w[z, 2] = dot(hidden_t[...], grads_in[:, at], BF16)

            post.finish()
            for copy in out:
                copy.wait()

        outs = [((many, width), BF16, pl.ANY)] * 2
        outs += [((many, chunk), BF16, pltpu.VMEM)] * 3
        outs += [((outer, 3, chunk, wide), BF16, pltpu.VMEM)]
        scratch = [
            pltpu.VMEM((many, width), BF16),
            pltpu.VMEM((many, width), BF16),
            pltpu.VMEM((width, 3 * chunk), BF16),
            pltpu.VMEM((many, 2 * chunk), F32),
            pltpu.VMEM((2 * chunk, many), BF16),
            pltpu.VMEM((chunk, many), BF16),
        ]
        return self.call(
            kernel, outs, (v, grad, weights), 2 * Gather.COPIES, scratch, local=5, vmem=62, time=90
        )

    def backward_rows(self, scalars, v, first_rows, arrays, held, row_part, job):
        layer, outer = self.layer, self.outer
        rows, width = v.shape
        many = layer * rows
        group = arrays["map_t"].shape[0]
        q_wide = group * HEAD
        kv_end = q_wide + 2 * HEAD
        names = list(arrays)
        inputs = len(names)
        wide = width // outer
        per_head = outer
        pieces = max(1, per_head // layer)
        tiles = many // TILE
        all_rows = arrays["weight_t"].shape[0]
        lefts, rights, job_columns = job
        jobs = len(lefts)
        job_scratch = self.job_scratch(job)

        def kernel(first, keep, joined, v, first_rows, *refs):
            refs = list(refs)

            def take(n):
                got = refs[:n]
                del refs[:n]
                return got

            given = take(inputs)
            job_refs = take(jobs), take(jobs)
            grads, sums, all_sum, part, job_out = take(5)
            sends, recvs, local = take(3)
            (rows_in, grad_t, window, grad_states, grad_low, grad_out, summary, got_s, state) = take(9)
            out_pieces, got_pieces = take(2)
            on = dict(zip(names, take(inputs)))
            work = take(4) + [take(jobs), take(jobs)]
            post = Post(sends, recvs)
            run_job = self.scatter_job(
                post, (*job_refs, job_out, work), job_columns, False, local, 2 + inputs, True
            )
            loads = []
            for i, (name, a) in enumerate(zip(names, given)):
                loads.append(pltpu.make_async_copy(a, on[name], local.at[2 + i]))
                loads[-1].start()
            dp = lax.axis_index("dp")
            others = [{"dp": (dp + 2 * d) % self.dp} for d in range(1, outer)]
            self.meet([self.flip(r)[0] for r in range(1, layer)] + others)
            gather = Gather(self, post, v, rows_in, local.at[0])
            gather.start()
            next(run_job)
            part[...] = jnp.zeros_like(part)
            summary[...] = jnp.zeros_like(summary)
            grad_out[...] = jnp.zeros_like(grad_out)
            for load in loads:
                load.wait()

            def pair(offset):
                gather.have_pair(offset)
                at, number = gather.pair(offset)
                back = dot_nt(on["out_w"][...], rows_in[at, :])
                low = back[q_wide:].astype(BF16)
                grad_low[:, at] = low
                grad_t[:, at] = back[:q_wide] + dot(on["adapter"][...], low)

                @pl.loop(0, outer)
                def _(j):
                    cut = pl.ds(pl.multiple_of(j * wide, wide), wide)
                    grad_out[:, cut] += dot(on["attended"][:, at], rows_in[at, cut])

                each = 2 * rows // TILE

                @pl.loop(0, each)
                def _(k):
                    query_tile(
                        number * each + k, first, on, grad_t,
                        (grads, window, grad_states, part, summary),
                    )

            pair(0)
            next(run_job)
            gather.near()
            next(run_job)
            gather.middle()
            pair(4)
            pair(2)
            gather.last()
            next(run_job)
            pair(6)

            for d, device in enumerate(others):
                post.send(summary, got_s.at[d], device)
            marks = list(range(len(post.copies) - len(others), len(post.copies)))
            for n in gather.made:
                post.copies[n].wait_send()
                post.sent.add(n)
            load = pltpu.make_async_copy(first_rows, rows_in, local.at[1])
            load.start()
            out_pieces[...] = grad_out[:q_wide, :].astype(BF16)
            rank = self.flip(0)[1]

            def rows_for(target, i):
                index = (i * layer + target) % per_head
                return pl.ds(pl.multiple_of(index * row_part, row_part), row_part)

            def run(test, action):
                if held is None:
                    action()
                else:
                    pl.when(test)(action)

            begun = Gather.COPIES + outer - 1 + 10
            moves = []
            for r in range(1, layer):
                device, target = self.flip(r)
                for i in range(pieces):
                    n = begun + len(moves)
                    copy = pltpu.make_async_remote_copy(
                        src_ref=out_pieces.at[rows_for(target, i)],
                        dst_ref=got_pieces.at[rank, i],
                        send_sem=sends.at[n],
                        recv_sem=recvs.at[n],
                        device_id=device,
                        device_id_type=MESH,
                    )
                    run(held and held(target, rank), copy.start)
                    moves.append((target, copy))
            for i in range(pieces):
                got_pieces[rank, i] = out_pieces[rows_for(rank, i), :]
            next(run_job)
            for mark in marks:
                post.arrived(mark)
            later = jnp.zeros_like(summary)
            for e in range(outer - 1):
                later = later + got_s[e] * joined[e]
            state[...] = later

            @pl.loop(0, tiles)
            def _(i):
                key_tile(tiles - 1 - i, keep, on, window, grad_states, state, grads, part)

            next(run_job)
            next(run_job)
            grads[kv_end:, :] = dot(on["seconds"][...], grads[:kv_end, :], BF16)
            both = dot_nt(on["low_all"][...], grads[:kv_end, :])
            part[:8] = both[:8, :q_wide]
            part[8:16] = dot_nt(grad_low[...], on["attended"][:q_wide, :])[:8]
            part[80:88, 128 : 128 + HEAD] = both[8:16, q_wide : q_wide + HEAD]
            part[80:88, 128 + HEAD :] = both[16:24, q_wide + HEAD :]
            load.wait()

            @pl.loop(0, outer)
            def _(z):
                at = pl.ds(pl.multiple_of(z * wide, wide), wide)
                total = dot(grads[...], rows_in[:, at])
                sums[z, :kv_end] = total[:kv_end].astype(BF16)
                all_sum[:24, at] = total[kv_end : kv_end + 24]
                all_sum[24:32, at] = grad_out[q_wide : q_wide + 8, at]
                gain = jnp.sum(total * on["weight_t"][:, at].astype(F32), 0, keepdims=True)
                gains = on["gains"][:, at]
                line = lax.broadcasted_iota(jnp.int32, (8, wide), 0)
                gain = gain / gains[:1]
                all_sum[32:, at] = jnp.where(
                    line == 0, gain, jnp.where(line == 1, gains[1:2], 0.0)
                )

            next(run_job)
            for target, copy in moves:
                run(held and held(rank, target), copy.wait_recv)
                run(held and held(target, rank), copy.wait_send)
            for o in range(outer):
                if per_head >= layer:
                    head, i = o // pieces, o % pieces
                else:
                    head, i = o * (layer // per_head) + rank // per_head, 0
                for j in range(outer):
                    sums[o, kv_end + j * row_part : kv_end + (j + 1) * row_part] = got_pieces[
                        head, i, :, j * wide : (j + 1) * wide
                    ]
            for _ in run_job:
                pass
            post.finish()

        outs = [
            ((all_rows, many), BF16, pltpu.VMEM),
            ((outer, kv_end + outer * row_part, wide), BF16, pltpu.VMEM),
            ((40, width), F32, pltpu.VMEM),
            ((144, q_wide), F32, pltpu.VMEM),
            (v.shape, F32, pltpu.VMEM),
        ]
        scratch = [
            pltpu.VMEM((many, width), BF16),
            pltpu.VMEM((q_wide, many), F32),
            pltpu.VMEM((2 * HEAD, many), F32),
            pltpu.VMEM((2 * tiles, 2 * HEAD, 2 * HEAD), F32),
            pltpu.VMEM((arrays["adapter"].shape[1], many), BF16),
            pltpu.VMEM(arrays["out_w"].shape, F32),
            pltpu.VMEM((2 * HEAD, 2 * HEAD), F32),
            pltpu.VMEM((outer - 1, 2 * HEAD, 2 * HEAD), F32),
            pltpu.VMEM((2 * HEAD, 2 * HEAD), F32),
            pltpu.VMEM((q_wide, width), BF16),
            pltpu.VMEM((layer, pieces, row_part, width), BF16),
        ]
        scratch += [pltpu.VMEM(a.shape, a.dtype) for a in arrays.values()]
        copies = Gather.COPIES + outer - 1 + 10 + pieces * (layer - 1)
        args = (*scalars, v, first_rows, *arrays.values(), *lefts, *rights)
        return self.call(
            kernel, outs, args, copies, scratch + job_scratch,
            local=2 + inputs + jobs * (layer + 1), vmem=62, time=8, specs=[SCALARS] * 3,
        )

    def swap_sides(self, arrays, chunk):
        many = len(arrays)
        rows, columns = arrays[0].shape
        half = columns // 2
        chunks = half // chunk

        def kernel(*refs):
            ins, blocks = refs[:many], refs[many : many + chunks]
            sends, recvs, local = refs[many + chunks :]
            post = Post(sends, recvs)
            device = self.flip(4)[0]
            self.meet([device])
            side = lax.axis_index("dp") % 2
            own = []
            for c in range(chunks):
                for k, v in enumerate(ins):

                    def part(of):
                        start = pl.multiple_of(of * half + c * chunk, 128)
                        return v.at[:, pl.ds(start, chunk)]

                    out = blocks[c].at[side, :, pl.ds(k * chunk, chunk)]
                    post.send(part(1 - side), out, device)
                    own.append(pltpu.make_async_copy(part(side), out, local.at[len(own)]))
                    own[-1].start()
            post.finish()
            for copy in own:
                copy.wait()

        outs = [((2, rows, many * chunk), arrays[0].dtype, pl.ANY)] * chunks
        total = many * chunks
        return self.call(kernel, outs, tuple(arrays), total, local=total, time=36)

    def scatter_job(self, post, refs, columns, turned, local, loads, early=False):
        lefts, rights, out, work = refs
        both, got, xs, ys, weights, blocks = work
        layer, many, step = self.layer, len(lefts), 16
        rows, width = out.shape
        half, wide = rows // 2, min(width, 512)
        devs = [self.flip(i) for i in range(8)]
        dev_c, dev_y, dev_x = devs[1][0], devs[2][0], devs[4][0]
        used = 0

        def load(src, dst):
            nonlocal used
            copy = pltpu.make_async_copy(src, dst, local.at[loads + used])
            copy.start()
            used += 1
            return copy

        weight_loads = []
        for k, (v, w) in enumerate(zip(rights, weights)):
            part = v if turned else v.at[:, pl.ds(columns[k], w.shape[1])]
            weight_loads.append(load(part, w))
        block_loads = {}
        for i in range(layer // 2 - 1, -1, -1):
            at = pl.ds(pl.multiple_of(devs[2 * i][1] // 2 * 2 * rows, 2 * rows), 2 * rows)
            for k, v in enumerate(lefts):
                block_loads[i, k] = load(v.at[:, at] if turned else v.at[at], blocks[k].at[i])
        yield
        for copy in weight_loads:
            copy.wait()

        core = devs[0][1] % 2
        here = pl.ds(pl.multiple_of(core * rows, rows), rows)
        there = pl.ds(pl.multiple_of((1 - core) * rows, rows), rows)
        mine = [both.at[i, here] for i in range(layer // 2)]

        def product(i, dst):
            for k in range(many):
                block_loads[i, k].wait()

            @pl.loop(0, width // wide)
            def _(j):
                at = pl.ds(pl.multiple_of(j * wide, wide), wide)
                total = None
                for k in range(many):
                    if turned:
                        term = dot_tn(blocks[k][i], weights[k][:, at])
                    else:
                        term = dot_nt(blocks[k][i], weights[k][at, :])
                    total = term if total is None else total + term
                dst[:, at] = total.astype(BF16)

        def add(dst, one, two):
            @pl.loop(0, dst.shape[0] // step)
            def _(j):
                at = pl.ds(pl.multiple_of(j * step, step), step)
                total = one[at, :].astype(F32) + two[at, :].astype(F32)
                dst[at, :] = total.astype(dst.dtype)

        a, b = pl.ds(0, half), pl.ds(half, half)

        def begin(i):
            product(i, both.at[i])
            return post.send(both.at[i, there], got.at[i], dev_c)

        def end(i, arrive):
            post.arrived(arrive)
            add(mine[i], mine[i], got.at[i])

        end(3, begin(3))
        if early:
            yield
            end(2, begin(2))
            yield
        x1 = post.send(mine[3].at[a], xs.at[0], dev_x)
        y1 = post.send(mine[3].at[b], ys.at[0], dev_y)
        if not early:
            yield
            two = begin(2)
            one = begin(1)
            end(2, two)
        x2 = post.send(mine[2].at[a], xs.at[1], dev_x)
        yield
        if early:
            one = begin(1)
        end(1, one)
        y2 = post.send(mine[1].at[b], ys.at[1], dev_y)
        zero = begin(0)
        yield
        post.arrived(x1)
        add(mine[1].at[a], mine[1].at[a], xs.at[0])
        y3 = post.send(mine[1].at[a], ys.at[2], dev_y)
        post.arrived(y1)
        add(mine[2].at[b], mine[2].at[b], ys.at[0])
        x3 = post.send(mine[2].at[b], xs.at[2], dev_x)
        yield
        end(0, zero)
        yield
        low, high = out.at[a], out.at[b]
        post.arrived(x2)
        add(low, mine[0].at[a], xs.at[1])
        post.arrived(y2)
        add(high, mine[0].at[b], ys.at[1])
        yield
        post.arrived(y3)
        add(low, low, ys.at[2])
        post.arrived(x3)
        add(high, high, xs.at[2])
        yield

    def job_scratch(self, job):
        lefts, rights, columns = job
        turned = columns is None
        rows = lefts[0].shape[1 if turned else 0] // self.layer
        width = rights[0].shape[1 if turned else 0]
        pairs = self.layer // 2
        work = [pltpu.VMEM((pairs, 2 * rows, width), BF16), pltpu.VMEM((pairs, rows, width), BF16)]
        work += [pltpu.VMEM((3, rows // 2, width), BF16)] * 2
        for v, w in zip(lefts, rights):
            work.append(pltpu.VMEM(w.shape if turned else (width, v.shape[1]), BF16))
        for v in lefts:
            block = (v.shape[0], 2 * rows) if turned else (2 * rows, v.shape[1])
            work.append(pltpu.VMEM((pairs,) + block, BF16))
        return work

    def scatter_products(self, *jobs, sums=(), swap=()):
        layer = self.layer
        outs, scratch, sizes, shapes, args = [], [], [], [], []
        local = 0
        for lefts, rights, columns in jobs:
            turned = columns is None
            many = len(lefts)
            rows = lefts[0].shape[1 if turned else 0] // layer
            width = rights[0].shape[1 if turned else 0]
            outs.append(((rows, width), F32, pltpu.VMEM))
            scratch += self.job_scratch((lefts, rights, columns))
            sizes.append(many)
            shapes.append(local)
            local += many * (layer + 1)
            args += [*lefts, *rights]
        copies = 10 * len(jobs)
        if sums:
            all_sum, part = sums
            stages = len(self.outer_steps())
            size, lanes = all_sum.shape[0] + part.shape[0], part.shape[1]
            outs += [
                ((all_sum.shape[0] + 24, layer * lanes), BF16, pltpu.VMEM),
                ((layer, part.shape[0] - 16, lanes), BF16, pltpu.VMEM),
            ]
            scratch += [
                pltpu.VMEM((layer, all_sum.shape[0], lanes), F32),
                pltpu.VMEM((stages, size, lanes), F32),
                pltpu.VMEM((size, lanes), F32),
                pltpu.VMEM((size + 8, lanes), BF16),
            ]
            copies += stages + 3 * (layer - 1)
            local += 2

        for v in swap:
            outs.append(((v.shape[0], v.shape[1] // 2), v.dtype, pl.ANY))
            copies += 1

        def kernel(*refs):
            refs = list(refs)

            def take(n):
                got = refs[:n]
                del refs[:n]
                return got

            given = [(take(n), take(n)) for n in sizes]
            given_sums = take(len(sums))
            given_swap = take(len(swap))
            made = take(len(jobs))
            made_sums = take(2 if sums else 0)
            made_swap = take(len(swap))
            sends, recvs, local_sems = take(3)
            post = Post(sends, recvs)
            runs = []
            for (lefts, rights), out, n, first, job in zip(given, made, sizes, shapes, jobs):
                work = take(4) + [take(n), take(n)]
                runs.append(
                    self.scatter_job(
                        post, (lefts, rights, out, work), job[2], job[2] is None, local_sems, first
                    )
                )
                next(runs[-1])
            if sums:
                self.meet(
                    [self.flip(r)[0] for r in range(1, layer)] + self.outer_partners()
                )
                runs.append(
                    self.sum_steps(post, given_sums, made_sums, refs, local_sems, local - 2)
                )
                next(runs[-1])
            else:
                self.meet([self.flip(i)[0] for i in (1, 2, 4)])
            order = (0, 0, 0, 1, 0, 1, 0, 0, 1, 0, 1) if sums else (0,) * 7
            for n, run in enumerate(order):
                next(runs[run], None)
                if n == 3:
                    for v, out in zip(given_swap, made_swap):
                        third = out.shape[1]
                        start = pl.multiple_of((1 - lax.axis_index("dp") % 2) * third, third)
                        post.send(v.at[:, pl.ds(start, third)], out, self.flip(4)[0])
            for run in runs:
                for _ in run:
                    pass
            post.finish()

        return self.call(
            kernel, outs, (*args, *sums, *swap), copies, scratch, local=local, vmem=60,
            time=4 * len(jobs),
        )

    def outer_steps(self):
        steps = []
        while 1 << len(steps) < self.outer:
            steps.append(2 << len(steps))
        return steps

    def outer_partners(self):
        dp = lax.axis_index("dp")
        return [{"dp": dp + step - 2 * step * ((dp // step) % 2)} for step in self.outer_steps()]

    def sum_steps(self, post, given, outs, scratch, local, used):
        all_sum, part = given
        columns, others = outs
        pieces, got, mine, rounded = scratch
        rank = self.flip(0)[1]
        share, lanes = pieces.shape[1], pieces.shape[2]
        split = share + 24

        def columns_of(r):
            return pl.ds(pl.multiple_of(r * lanes, lanes), lanes)

        copies = [
            pltpu.make_async_copy(all_sum.at[:, columns_of(rank)], pieces.at[rank], local.at[used]),
            pltpu.make_async_copy(
                part, mine.at[pl.ds(share, part.shape[0])], local.at[used + 1]
            ),
        ]
        for copy in copies:
            copy.start()
        ids = []
        for r in range(1, self.layer):
            device, target = self.flip(r)
            ids.append(post.send(all_sum.at[:, columns_of(target)], pieces.at[rank], device))
        yield
        for copy in copies:
            copy.wait()
        for i in ids:
            post.arrived(i)
        total = pieces[0]
        for r in range(1, self.layer):
            total = total + pieces[r]
        mine[:share] = total
        for n, device in enumerate(self.outer_partners()):
            i = post.send(mine, got.at[n], device)
            yield
            post.arrived(i)
            post.copies[i].wait_send()
            post.sent.add(i)
            mine[...] = mine[...] + got[n]
        rounded[: split - 8] = mine[: split - 8].astype(BF16)
        rounded[split - 8 : split] = jnp.zeros((8, lanes), BF16)
        rounded[split:] = mine[split - 8 :].astype(BF16)
        for r in range(1, self.layer):
            device = self.flip(r)[0]
            post.send(rounded.at[pl.ds(0, split)], columns.at[:, columns_of(rank)], device)
            post.send(rounded.at[pl.ds(split, others.shape[1])], others.at[rank], device)
        columns[:, columns_of(rank)] = rounded[:split]
        others[rank] = rounded[split:]
        yield

    def exchange_copies(self, v, out, sends, recvs, local, held):
        rank = self.flip(0)[1]

        def run(test, action):
            if held is None:
                action()
            else:
                pl.when(test)(action)

        own = pltpu.make_async_copy(v.at[rank], out.at[rank], local.at[0])
        copies = []
        for i, r in enumerate((6, 7, 4, 5, 2, 3, 1)):
            device, target = self.flip(r)
            copy = pltpu.make_async_remote_copy(
                src_ref=v.at[target],
                dst_ref=out.at[rank],
                send_sem=sends.at[i],
                recv_sem=recvs.at[i],
                device_id=device,
                device_id_type=MESH,
            )
            copies.append((target, copy))

        def start():
            own.start()
            for target, copy in copies:
                run(held and held(rank, target), copy.start)

        def wait():
            for target, copy in copies:
                run(held and held(target, rank), copy.wait_recv)
                run(held and held(rank, target), copy.wait_send)
            own.wait()

        return start, wait

    def exchange(self, v):
        def kernel(v, out, sends, recvs, local):
            self.meet([self.flip(r)[0] for r in range(1, self.layer)])
            start, wait = self.exchange_copies(v, out, sends, recvs, local, None)
            start()
            wait()

        return self.call(kernel, [(v.shape, v.dtype, pl.ANY)], (v,), 7, time=9)[0]

    def between(self, v, gathered, row_part, held):
        n, layer = self.outer, self.layer
        per_head, width = n, gathered.shape[1]
        pieces = max(1, per_head // layer)
        each = gathered.shape[0] // n

        def kernel(v, gathered, out, got, sends, recvs, local):
            dp = lax.axis_index("dp")
            rank = self.flip(0)[1]
            devices = [{"dp": (dp + 2 * d) % self.dp} for d in range(1, n)]
            self.meet(devices + [self.flip(r)[0] for r in range(1, layer)])
            post = Post(sends, recvs)
            for d, device in enumerate(devices):
                post.send(v, out.at[d], device)

            def rows_for(target, i):
                place = target * per_head // layer + i
                start = pl.multiple_of(place * each + each - row_part, 16)
                return gathered.at[pl.ds(start, row_part)]

            def run(test, action):
                if held is None:
                    action()
                else:
                    pl.when(test)(action)

            own = []
            for i in range(pieces):
                own.append(
                    pltpu.make_async_copy(rows_for(rank, i), got.at[rank, i], local.at[i])
                )
                own[-1].start()
            moves = []
            for r in (6, 7, 4, 5, 2, 3, 1):
                device, target = self.flip(r)
                for i in range(pieces):
                    at = n - 1 + len(moves)
                    copy = pltpu.make_async_remote_copy(
                        src_ref=rows_for(target, i),
                        dst_ref=got.at[rank, i],
                        send_sem=sends.at[at],
                        recv_sem=recvs.at[at],
                        device_id=device,
                        device_id_type=MESH,
                    )
                    run(held and held(rank, target), copy.start)
                    moves.append((target, copy))
            post.finish()
            for target, copy in moves:
                run(held and held(target, rank), copy.wait_recv)
                run(held and held(rank, target), copy.wait_send)
            for copy in own:
                copy.wait()

        outs = [
            ((n - 1,) + v.shape, v.dtype, pl.ANY),
            ((layer, pieces, row_part, width), gathered.dtype, pl.ANY),
        ]
        copies = n - 1 + (layer - 1) * pieces
        return self.call(kernel, outs, (v, gathered), copies, local=pieces, time=5)


    def groups(self):
        return [[2 * o + b for o in range(self.outer)] for b in range(2)]

    def gather_outer(self, v):
        return lax.all_gather(v, "dp", axis_index_groups=self.groups(), tiled=True)

    def scatter_outer(self, v):
        return lax.psum_scatter(v, "dp", axis_index_groups=self.groups(), tiled=True)

    def other_side(self, v):
        return lax.ppermute(v, "dp", [(i, i ^ 1) for i in range(self.dp)])


def stable_maps(logits):
    plus = jnp.exp(logits - jnp.max(logits, 0, keepdims=True))
    minus = jnp.exp(jnp.min(logits, 0, keepdims=True) - logits)
    plus = plus * (1.0 / jnp.sum(plus, 0, keepdims=True))
    minus = minus * (1.0 / jnp.sum(minus, 0, keepdims=True))
    return plus, minus


def maps_back(grad, plus, minus):
    up, down = grad[:HEAD], grad[HEAD:]
    out = plus * (up - jnp.sum(plus * up, 0, keepdims=True))
    return (out - minus * (down - jnp.sum(minus * down, 0, keepdims=True))).astype(BF16)


def heads_wide(v, group):
    return jnp.concatenate([v[h * HEAD : (h + 1) * HEAD] for h in range(group)], 1)


def first_window(lanes):
    return lax.broadcasted_iota(jnp.int32, (1, lanes), 1) % TILE < WINDOW


def window_scores(keys, queries):
    lanes = queries.shape[1]
    scores = dot_tn(keys, queries) * (1.0 / math.sqrt(HEAD))
    j = lax.broadcasted_iota(jnp.int32, (TILE, lanes), 0)
    t = lax.broadcasted_iota(jnp.int32, (TILE, lanes), 1) % TILE
    seen = (j <= t) & (j // WINDOW == t // WINDOW)
    masked = jnp.where(seen, scores, FLOOR_SCORE)
    top = jnp.max(masked, 0, keepdims=True)
    return jnp.where(seen, jnp.exp(masked - top), 0.0), top


def key_kernel(keys, values, map_t, mask, feats, summary):
    summary[...] = jnp.zeros_like(summary)
    step = 2 * TILE

    @pl.loop(0, keys.shape[1] // step)
    def _(i):
        at = pl.ds(pl.multiple_of(i * step, step), step)
        plus, minus = stable_maps(dot(map_t[...], keys[:, at]))
        feat = jnp.concatenate([plus, minus], 0).astype(BF16)
        feats[:, at] = feat
        kept = (feat.astype(F32) * mask[:, at]).astype(BF16)
        summary[...] += dot_nt(kept, values[:, at])


def forward_kernel(
    keep, queries, keys, values, feats, map_t, carry, attended, ratios, denoms, states, state
):
    i = pl.program_id(0)
    group = map_t.shape[0]

    @pl.when(i == 0)
    def _():
        state[...] = carry[...]

    feat_k, vals = feats[...], values[...]
    one = state[...] * keep[2 * i]
    two = (one + dot_nt(feat_k[:, :WINDOW], vals[:, :WINDOW])) * keep[2 * i + 1]
    state[...] = two + dot_nt(feat_k[:, WINDOW:], vals[:, WINDOW:])
    one, two = one.astype(BF16), two.astype(BF16)
    states[0], states[1] = one, two
    rows = queries[...]
    wide = heads_wide(rows, group)
    logits = jnp.concatenate(
        [dot(map_t[h], rows[h * HEAD : (h + 1) * HEAD]) for h in range(group)], 1
    )
    feat_q = jnp.concatenate(stable_maps(logits), 0).astype(BF16)
    expo, top = window_scores(keys[...], wide)
    shrink = jnp.exp(-top)
    window = dot(vals[:HEAD], expo.astype(BF16))
    linear = jnp.where(first_window(wide.shape[1]), dot_tn(one, feat_q), dot_tn(two, feat_q))
    numer = window + shrink * linear[:HEAD]
    denom = jnp.sum(expo, 0, keepdims=True) + shrink * linear[HEAD : HEAD + 1]
    ratio = numer * (1.0 / denom)
    denoms[0] = denom
    for h in range(group):
        part = ratio[:, h * TILE : (h + 1) * TILE]
        ratios[h * HEAD : (h + 1) * HEAD] = part
        attended[h * HEAD : (h + 1) * HEAD] = part.astype(BF16)


def query_tile(tile, first, on, grad_t, outs):
    grads, window_kv, grad_states, part, summary = outs
    map_t, maps, states = on["map_t"], on["maps"], on["states"]
    group = map_t.shape[0]
    at = pl.ds(pl.multiple_of(tile * TILE, TILE), TILE)
    rows, key_rows, vals = on["queries"][:, at], on["keys"][:, at], on["values"][:, at]
    wide = heads_wide(rows, group)
    lanes = wide.shape[1]
    grad, ratio = heads_wide(grad_t[:, at], group), heads_wide(on["ratios"][:, at], group)
    inverse = 1.0 / on["denoms"][tile]
    grad_num = (grad * inverse).astype(BF16)
    grad_den = -jnp.sum(grad * ratio, 0, keepdims=True) * inverse
    expo, top = window_scores(key_rows, wide)
    shrink = jnp.exp(-top)
    grad_scores = (expo * (dot_tn(vals[:HEAD], grad_num) + grad_den)).astype(BF16)
    scale = 1.0 / math.sqrt(HEAD)
    window_kv[:HEAD, at] = dot_nt(wide, grad_scores) * scale
    window_kv[HEAD:, at] = dot_nt(grad_num, expo.astype(BF16))
    logits = jnp.concatenate(
        [dot(map_t[h], rows[h * HEAD : (h + 1) * HEAD]) for h in range(group)], 1
    )
    plus, minus = stable_maps(logits)
    feat_q = jnp.concatenate([plus, minus], 0).astype(BF16)
    both = jnp.concatenate(
        [
            grad_num.astype(F32) * shrink,
            grad_den * shrink,
            jnp.zeros((2 * HEAD - HEAD - 1, lanes), F32),
        ],
        0,
    )
    early = first_window(lanes)
    state_one = dot_nt(feat_q, jnp.where(early, both, 0.0).astype(BF16))
    state_two = dot_nt(feat_q, jnp.where(early, 0.0, both).astype(BF16))
    grad_states[2 * tile], grad_states[2 * tile + 1] = state_one, state_two
    summary[...] += state_one * first[2 * tile] + state_two * first[2 * tile + 1]
    both = both.astype(BF16)
    grad_feat = jnp.where(early, dot(states[2 * tile], both), dot(states[2 * tile + 1], both))
    grad_logits = maps_back(grad_feat, plus, minus)
    window = dot(key_rows, grad_scores) * scale
    grad_maps = []
    for h in range(group):
        head, cut = slice(h * HEAD, (h + 1) * HEAD), slice(h * TILE, (h + 1) * TILE)
        grads[head, at] = (window[:, cut] + dot(maps[h], grad_logits[:, cut])).astype(BF16)
        grad_maps.append(dot_nt(rows[head], grad_logits[:, cut]))
    part[16 : 16 + HEAD] += jnp.concatenate(grad_maps, 1)


def key_tile(tile, keep, on, window, grad_states, state, grads, part):
    at = pl.ds(pl.multiple_of(tile * TILE, TILE), TILE)
    two = state[...]
    one = (two + grad_states[2 * tile + 1]) * keep[2 * tile + 1]
    state[...] = (one + grad_states[2 * tile]) * keep[2 * tile]
    one, two = one.astype(BF16), two.astype(BF16)
    key_rows, vals, feat = on["keys"][:, at], on["values"][:, at], on["feats"][:, at]
    early = first_window(TILE)
    grad_feat = jnp.where(early, dot(one, vals), dot(two, vals))
    linear = jnp.where(early, dot_tn(one, feat), dot_tn(two, feat))[:HEAD]
    plus, minus = stable_maps(dot(on["map_k_t"][...], key_rows))
    grad_logits = maps_back(grad_feat, plus, minus)
    start = grads.shape[0] - on["seconds"].shape[0] - 2 * HEAD
    grads[start : start + HEAD, at] = (
        window[:HEAD, at] + dot(on["map_k"][...], grad_logits)
    ).astype(BF16)
    grads[start + HEAD : start + 2 * HEAD, at] = (window[HEAD:, at] + linear).astype(BF16)
    part[16 + HEAD : 16 + 2 * HEAD, :HEAD] += dot_nt(key_rows, grad_logits)


def local_call(kernel, outs, args, time=10, vmem=32, **kwargs):
    return pl.pallas_call(
        kernel,
        out_shape=[jax.ShapeDtypeStruct(s, t) for s, t in outs],
        cost_estimate=takes(time),
        compiler_params=pltpu.CompilerParams(vmem_limit_bytes=vmem * 2**20),
        **kwargs,
    )(*args)


def hidden_units(gate, upper, grad_hidden):
    sigmoid = 1.0 / (1.0 + jnp.exp(-gate))
    silu = gate * sigmoid
    grad_gate = grad_hidden * upper * sigmoid * (1.0 + gate * (1.0 - sigmoid))
    return (silu * upper).astype(BF16), grad_gate.astype(BF16), (grad_hidden * silu).astype(BF16)


def feedforward_kernel(
    rows, grads, gate_w, up_w, down_w, hidden, grad_gate, grad_up, grad_w, both_t, hidden_t
):
    step = 512
    tile = gate_w.shape[1]

    @pl.loop(0, rows.shape[0] // step)
    def _(i):
        at = pl.ds(pl.multiple_of(i * step, step), step)
        gate = dot(rows[at, :], gate_w[...])
        upper = dot(rows[at, :], up_w[...])
        grad_hidden = dot(grads[at, :], down_w[...])
        inner, one, two = hidden_units(gate, upper, grad_hidden)
        hidden[at, :], grad_gate[at, :], grad_up[at, :] = inner, one, two
        hidden_t[:, at] = inner.T
        both_t[:tile, at] = one.T
        both_t[tile:, at] = two.T

    wide = grad_w.shape[-1]

    @pl.loop(0, grad_w.shape[0])
    def _(z):
        at = pl.ds(pl.multiple_of(z * wide, wide), wide)
        both = dot(both_t[...], rows[:, at], BF16)
        grad_w[z, 0], grad_w[z, 1] = both[:tile], both[tile:]
        grad_w[z, 2] = dot(hidden_t[...], grads[:, at], BF16)


def feedforward(rows, grads, weights, chunk, outer):
    many, width = rows.shape
    tile = 256
    tiles, wide = chunk // tile, width // outer
    held = pl.BlockSpec((many, width), lambda j: (0, 0), pipeline_mode=pl.Buffered(1))

    def part(k):
        return pl.BlockSpec((width, tile), lambda j: (0, k * tiles + j))

    column = pl.BlockSpec((many, tile), lambda j: (0, j))
    return local_call(
        feedforward_kernel,
        [((many, chunk), BF16)] * 3 + [((outer, 3, chunk, wide), BF16)],
        (rows, grads, weights, weights, weights),
        time=35,
        vmem=60,
        grid=(tiles,),
        in_specs=[held, held, part(0), part(1), part(2)],
        out_specs=[column] * 3
        + [pl.BlockSpec((outer, 3, tile, wide), lambda j: (0, 0, j, 0))],
        scratch_shapes=[pltpu.VMEM((2 * tile, many), BF16), pltpu.VMEM((tile, many), BF16)],
    )


def whole(shape):
    return pl.BlockSpec(shape, lambda i: (0,) * len(shape))


SCALARS = pl.BlockSpec(memory_space=pltpu.SMEM)


def key_features(keys, values, map_t, mask):
    rows = keys.shape[1]
    return local_call(
        key_kernel,
        [((2 * HEAD, rows), BF16), ((2 * HEAD, 2 * HEAD), F32)],
        (keys, values, map_t, mask),
    )


def attention_forward(keep, queries, keys, values, feats, map_t, carry):
    group, rows = map_t.shape[0], keys.shape[1]
    tiles = rows // TILE
    cols = lambda n: pl.BlockSpec((n, TILE), lambda i: (0, i))
    return local_call(
        forward_kernel,
        [
            ((group * HEAD, rows), BF16),
            ((group * HEAD, rows), F32),
            ((tiles, 1, group * TILE), F32),
            ((2 * tiles, 2 * HEAD, 2 * HEAD), BF16),
        ],
        (keep, queries, keys, values, feats, map_t, carry),
        grid=(tiles,),
        in_specs=[
            SCALARS, cols(group * HEAD), cols(HEAD), cols(2 * HEAD), cols(2 * HEAD),
            whole(map_t.shape), whole(carry.shape),
        ],
        out_specs=[
            cols(group * HEAD),
            cols(group * HEAD),
            pl.BlockSpec((1, 1, group * TILE), lambda i: (i, 0, 0)),
            pl.BlockSpec((2, 2 * HEAD, 2 * HEAD), lambda i: (i, 0, 0)),
        ],
        scratch_shapes=[pltpu.VMEM((2 * HEAD, 2 * HEAD), F32)],
    )


def shards(
    links,
    hidden_input,
    output_gradient,
    lengths,
    attention_norm_gain,
    query_weight,
    key_weight,
    value_weight,
    output_weight,
    query_adapter_first,
    query_adapter_second,
    key_adapter_first,
    key_adapter_second,
    value_adapter_first,
    value_adapter_second,
    output_adapter_first,
    output_adapter_second,
    query_feature_weight,
    key_feature_weight,
    feedforward_norm_gain,
    gate_weight,
    up_weight,
    down_weight,
):
    links.coords()
    place, side, rank = links.place, links.side, links.rank
    outer, layer = links.outer, links.layer
    rows, width = hidden_input.shape
    layer_rows = rows * layer
    windows = layer_rows // WINDOW
    kv_heads = key_feature_weight.shape[0]
    group = query_feature_weight.shape[0] // kv_heads
    q_wide = group * HEAD

    spans = (lengths + WINDOW - 1) // WINDOW
    seq_ends = jnp.cumsum(spans)
    seq_begins = seq_ends - spans

    def sequence_of(span):
        return jnp.sum((span[..., None] >= seq_ends).astype(jnp.int32), -1)

    local = jnp.arange(windows, dtype=jnp.int32)
    span_seq = sequence_of(place * windows + local)
    seq_first, seq_last = span_seq[0], span_seq[-1]
    same_next = (span_seq[1:] == span_seq[:-1]).astype(F32)
    keep = jnp.concatenate([jnp.ones((1,), F32), same_next])
    first_mask = (span_seq == seq_first).astype(F32)
    last_mask = (span_seq == seq_last).astype(F32)
    token_ids = (place * layer + rank) * rows + jnp.arange(rows, dtype=jnp.int32)
    token_seq = sequence_of(token_ids // WINDOW)
    onehot = (token_seq[:, None] == jnp.arange(lengths.shape[0], dtype=jnp.int32)).astype(jnp.int32)
    offset = jnp.sum(onehot * seq_begins * WINDOW, 1)
    limit = jnp.sum(onehot * lengths, 1)
    valid = (token_ids - offset < limit).astype(F32)[:, None]

    def own(v, axis, size):
        return lax.dynamic_slice_in_dim(v, rank * size, size, axis)

    inputs_full = hidden_input.astype(F32)
    gain_one = attention_norm_gain.astype(F32)
    gain_two = feedforward_norm_gain.astype(F32)
    normed_one, inv_one, first_rows = rms_forward(inputs_full, gain_one)

    row_part = query_weight.shape[0]
    rank_size = query_adapter_first.shape[1]
    kv_end = q_wide + 2 * HEAD
    per_head = outer
    many = max(1, per_head // layer)
    parts = jnp.concatenate(
        [w.reshape(row_part, layer, -1) for w in (query_weight, key_weight, value_weight)], -1
    )
    parts = links.exchange(parts.transpose(1, 0, 2))
    lanes = 128
    packs = width // lanes
    deep = layer * row_part // packs
    packed = parts.reshape(packs, deep, kv_end // lanes, lanes).transpose(2, 1, 0, 3)
    packed = packed.reshape(deep * kv_end // lanes, width)
    packed = jnp.pad(packed, ((0, -packed.shape[0] % 16), (0, 0)))
    gathered = links.gather_outer(jnp.concatenate([packed, output_weight], 0))
    gathered_rows = gathered.reshape(outer, -1, width)
    head_weight = gathered_rows[:, : deep * kv_end // lanes]
    head_weight = head_weight.reshape(outer, kv_end // lanes, deep, packs, lanes)
    head_weight = head_weight.transpose(0, 3, 2, 1, 4).reshape(width, kv_end)

    hidden_part = gate_weight.shape[1] // 2
    chunk = hidden_part // CHUNKS
    third = gate_weight.shape[0]

    halves = links.swap_sides(
        (gate_weight, up_weight, after(down_weight.T, parts)), chunk
    )
    blocks = [links.gather_outer(v.reshape(2 * third, 3 * chunk)) for v in halves]
    first_all = links.gather_rows(after(first_rows, *halves))

    def held(source, head):
        return (source // per_head) == head % (layer // per_head)

    adapters = jnp.concatenate([query_adapter_first, key_adapter_first, value_adapter_first], 1)
    adapters = jnp.pad(adapters, ((0, 0), (0, -3 * rank_size % 16)))
    qkv_weight = jnp.concatenate([head_weight, adapters], 1)
    second_q = own(query_adapter_second, 1, q_wide)
    second_k = own(key_adapter_second, 1, HEAD)
    second_v = own(value_adapter_second, 1, HEAD)
    oa_own = own(output_adapter_first, 0, q_wide)

    projected = dot_tt(qkv_weight, first_all)
    low_rank = projected[kv_end:].astype(BF16)
    low_q, low_k, low_v = (low_rank[i * rank_size : (i + 1) * rank_size] for i in range(3))
    queries = (projected[:q_wide] + dot_tn(second_q, low_q)).astype(BF16)
    keys = (projected[q_wide : q_wide + HEAD] + dot_tn(second_k, low_k)).astype(BF16)
    values = (projected[q_wide + HEAD : kv_end] + dot_tn(second_v, low_v)).astype(BF16)
    values = jnp.concatenate(
        [values, jnp.ones((1, layer_rows), BF16), jnp.zeros((HEAD - 1, layer_rows), BF16)], 0
    )
    maps_q = lax.dynamic_slice_in_dim(query_feature_weight, rank * group, group, 0)
    map_k = lax.dynamic_slice_in_dim(key_feature_weight, rank, 1, 0)[0]
    maps_q_turned, map_k_turned = maps_q.transpose(0, 2, 1), map_k.T

    def carry_forward(summary):
        got, out_own = links.between(
            summary, gathered, row_part, held if per_head < layer else None
        )
        total = jnp.zeros_like(summary)
        for d in range(1, outer):
            joined = sequence_of((place - d + 1) * windows - 1) == seq_first
            total = total + jnp.where(joined & (place >= d), got[d - 1], 0.0)
        return total, out_own

    last_tokens = jnp.repeat(last_mask, WINDOW)[None]
    feats, summary = key_features(keys, values, map_k_turned, last_tokens)
    carried, out_parts = carry_forward(summary)
    if per_head >= layer:
        out_own = out_parts.transpose(1, 0, 2, 3).reshape(-1, width)
    else:
        start = (rank % (layer // per_head)) * per_head
        out_own = lax.dynamic_slice_in_dim(out_parts, start, per_head, 0).reshape(-1, width)
    attended, ratios, denoms, states = attention_forward(
        keep, queries, keys, values, feats, maps_q_turned, carried
    )
    low_out = dot_tn(oa_own, attended, BF16)
    pad = 16 - rank_size
    out_both = jnp.concatenate([out_own, output_adapter_second, jnp.zeros((pad, width), BF16)], 0)
    attended_both = jnp.concatenate([attended, low_out, jnp.zeros((pad, layer_rows), BF16)], 0)
    resid = inputs_full + links.scatter_products(([attended_both], [out_both], None))[0]

    normed_two, inv_two, rows_two = rms_forward(resid, gain_two)
    rows_two = after(rows_two, blocks[0])
    grad_y = output_gradient.astype(F32) * valid
    weight_t = qkv_weight.T
    seconds = jnp.zeros((adapters.shape[1], kv_end), BF16)
    seconds = seconds.at[:rank_size, :q_wide].set(second_q)
    seconds = seconds.at[rank_size : 2 * rank_size, q_wide : q_wide + HEAD].set(second_k)
    seconds = seconds.at[2 * rank_size : 3 * rank_size, q_wide + HEAD :].set(second_v)
    joined = [
        (sequence_of((place + d) * windows) == seq_last) & (place + d < outer)
        for d in range(outer - 1, 0, -1)
    ]
    padded = jnp.pad(oa_own, ((0, 0), (0, pad)))
    joined = jnp.stack(joined).astype(F32)
    weight_t, seconds, padded, joined, maps_q, map_k = lax.optimization_barrier(
        (weight_t, seconds, padded, joined, maps_q, map_k)
    )
    hiddens, grads_two, block_sums = [], [], []
    for c in range(CHUNKS):
        if c == 0:
            two_all, grad_all, *made = links.gather_feedforward(
                rows_two, grad_y.astype(BF16), blocks[c], chunk
            )
        else:
            ready = after(two_all, weight_t, seconds, padded, joined, maps_q, map_k)
            made = feedforward(ready, grad_all, blocks[c], chunk, outer)
        hidden, grad_gate, grad_up, grad_block = made
        hiddens.append(hidden)
        grads_two += [grad_gate, grad_up]
        block_sums.append(links.scatter_outer(grad_block.reshape(outer * 3 * chunk, -1)))
    (grad_rows_two,) = links.scatter_products(
        (grads_two, [blocks[i // 2] for i in range(2 * CHUNKS)], [0, chunk] * CHUNKS)
    )

    grad_gain_two = jnp.sum(grad_rows_two * normed_two, 0)
    grad_resid = grad_y + rms_backward(grad_rows_two, normed_two, inv_two, gain_two)
    grads_all, sums, all_sum, part, mlp_out = links.backward_rows(
        (first_mask, keep, joined),
        grad_resid.astype(BF16),
        first_all,
        {
            "out_w": out_both,
            "attended": attended_both,
            "adapter": padded,
            "queries": queries,
            "keys": keys,
            "values": values,
            "map_t": maps_q_turned,
            "maps": maps_q,
            "map_k_t": map_k_turned,
            "map_k": map_k,
            "states": states,
            "ratios": ratios,
            "denoms": denoms,
            "feats": feats,
            "seconds": seconds,
            "low_all": low_rank,
            "weight_t": weight_t,
            "gains": jnp.pad(jnp.stack([gain_one, grad_gain_two]), ((0, 6), (0, 0))),
        },
        held if per_head < layer else None,
        row_part,
        (hiddens, blocks, [2 * chunk] * CHUNKS),
    )
    sums = after(sums, block_sums[0])
    grads_all = after(grads_all, sums)
    sums = links.scatter_outer(sums.reshape(-1, sums.shape[-1]))
    early = block_sums[:1] if third % 128 == 0 else []
    grad_rows_one, columns, others, *theirs = links.scatter_products(
        ([grads_all], [weight_t], None), sums=(all_sum, part), swap=tuple(early)
    )
    small_done = grad_rows_one
    wide = width // outer
    grad_out_sh = sums[kv_end:].reshape(outer, row_part, wide).transpose(1, 0, 2)
    grad_out_sh = grad_out_sh.reshape(row_part, width).astype(F32)
    sums = after(sums[:kv_end].T, grad_rows_one)
    got = links.exchange(sums.reshape(layer, row_part, kv_end))
    columns, others, got = lax.optimization_barrier((columns, others, got))
    got, columns, others = got.astype(F32), columns.astype(F32), others.astype(F32)
    grad_query_sh = got[:, :, :q_wide].transpose(1, 0, 2).reshape(row_part, -1)
    grad_key_sh = got[:, :, q_wide : q_wide + HEAD].transpose(1, 0, 2).reshape(row_part, -1)
    grad_value_sh = got[:, :, q_wide + HEAD :].transpose(1, 0, 2).reshape(row_part, -1)

    block_out = (valid * (resid + mlp_out)).astype(BF16)
    in_grad = grad_resid + rms_backward(grad_rows_one, normed_one, inv_one, gain_one)

    grad_qa, grad_ka, grad_va = (
        columns[i * rank_size : (i + 1) * rank_size].T for i in range(3)
    )
    grad_ob, grad_gain_one, grad_gain_two = columns[24:32], columns[32], columns[33]
    grad_qb, grad_oa = columns[40:48], columns[48:56].T
    grad_map_q = others[:, :HEAD].reshape(layer, HEAD, group, HEAD).transpose(0, 2, 1, 3)
    grad_map_q = grad_map_q.reshape(-1, HEAD, HEAD)
    grad_map_k = others[:, HEAD : 2 * HEAD, :HEAD]
    grad_kb, grad_vb = (
        others[:, HEAD : HEAD + rank_size, 128 + i * HEAD : 128 + (i + 1) * HEAD]
        .transpose(1, 0, 2)
        .reshape(rank_size, -1)
        for i in range(2)
    )

    mine = [lax.dynamic_slice_in_dim(v, side * third, third, 1) for v in block_sums]
    for summed in block_sums[len(early) :]:
        summed = after(summed, small_done)
        theirs.append(
            links.other_side(lax.dynamic_slice_in_dim(summed, (1 - side) * third, third, 1))
        )

    def units(k):
        own, other = (
            jnp.concatenate([v[k * chunk : (k + 1) * chunk] for v in many], 0)
            for many in (mine, theirs)
        )
        return jnp.concatenate(
            [jnp.where(side == 0, own, other), jnp.where(side == 0, other, own)], 0
        )

    grad_gate_sh, grad_up_sh = units(0).T.astype(F32), units(1).T.astype(F32)
    grad_down_sh = units(2).astype(F32)
    return (
        block_out,
        in_grad,
        grad_gain_one,
        grad_query_sh,
        grad_key_sh,
        grad_value_sh,
        grad_out_sh,
        grad_qa,
        grad_qb,
        grad_ka,
        grad_kb,
        grad_va,
        grad_vb,
        grad_oa,
        grad_ob,
        grad_map_q,
        grad_map_k,
        grad_gain_two,
        grad_gate_sh,
        grad_up_sh,
        grad_down_sh,
    )


def solution(mesh):
    rows = P(("dp", "tensor"), None)
    gate = P("dp", "tensor")
    down = P("tensor", "dp")
    links = Links(mesh)
    return jax.shard_map(
        lambda *args: shards(links, *args),
        mesh=mesh,
        in_specs=(rows, rows, P(), P(), rows, rows, rows, rows)
        + (P(),) * 11
        + (gate, gate, down),
        out_specs=(rows, rows, P(), rows, rows, rows, rows)
        + (P(),) * 11
        + (gate, gate, down),
        check_vma=False,
    )
```
